32 devices in a mesh: subj: 4 (over y, x), slab: 8 (over z, core).
Axes of the slice: x: 2, y: 2, z: 4, core: 2. Of those that a mesh axis runs over, the one named last changes fastest.
Arguments:
- template: float32 [4096, 128], P('slab'), may hold values from -6 to 6
- images: float32 [4, 4096, 128], P('subj', 'slab'), may hold values from -6 to 6
- velocity: float32 [4, 3, 4096, 128], P('subj', None, 'slab'), may hold values from -6 to 6
- stiffness: float32 [4096, 128], P('slab'), may hold values from 0.1 to 1
- send_rows: int32 [4, 8, 8, 64], P('subj', 'slab'), may hold values from 0 to 511, as said below
- ref_slot: int32 [4, 4096, 8], P('subj', 'slab'), may hold values from 0 to 511, as said below
- columns: int32 [4, 4096, 8, 128], P('subj', 'slab'), may hold values from 0 to 127, as said below
- weights: bfloat16 [4, 4096, 8, 128], P('subj', 'slab'), may hold values from 0 to 0.25
Outputs:
- template_out: float32 [4096, 128], P('slab')
- velocity_out: float32 [4, 3, 4096, 128], P('subj', None, 'slab')
The draws below stay inside these ranges and needn't reach their ends.
Inputs may be any that keep to these rules, and one draw needn't show every extreme that they name: `send_rows`: local rows of the owner slab. `ref_slot`: for each subject and each owner k and destination slab j, the referenced c lie below a count of that pair between 32 and 64; for each subject one destination slab has the count 64 from every owner. columns[s, g, b, x] differs from x by at most 2.
All inputs are finite; a program needn't handle non-finite values.
Results may differ from the reference program's by a relative error of at most 0.0003.
Values sent between devices are 32-bit elements; how exact they have to be, the bound alone decides.
No kernel may reach another device: no remote copies, remote signals or barrier semaphores. Data moves between devices by JAX's collectives and lax.ppermute only.
A program may use at most 64 MiB of HBM per device.

```python
import math
import jax
import jax.numpy as jnp
from jax import lax

W = 128
YR = 256
PLANES = 2
NB = 8
SMOOTH = 2
SLABS = 8
SUBJECTS = 4
ROWS = 512
NR = 4096
CAP = 64


def pair_counts(key):
    base_key = jax.random.fold_in(key, 11)
    count_key, full_key = jax.random.split(base_key)
    counts = jax.random.randint(count_key, (SUBJECTS, SLABS, SLABS), (CAP + 1) // 2, CAP + 1)
    full_dest = jax.random.randint(full_key, (SUBJECTS,), 0, SLABS)
    destination = jnp.arange(SLABS)
    return jnp.where(destination[None, None, :] == full_dest[:, None, None], CAP, counts)


def draw_send_rows(key, part):
    return jax.random.randint(jax.random.fold_in(key, 23), (SUBJECTS, SLABS, SLABS, CAP), 0, ROWS).astype(jnp.int32)


def draw_ref_slot(key, part):
    counts = pair_counts(key)
    owner_key, slot_key = jax.random.split(jax.random.fold_in(key, 37))
    owners = jax.random.randint(owner_key, (SUBJECTS, NR, NB), 0, SLABS)
    destination = (jnp.arange(NR) // ROWS)[None, :, None]
    subject_ids = jnp.arange(SUBJECTS)[:, None, None]
    limits = counts[subject_ids, owners, destination]
    within = jax.random.randint(slot_key, (SUBJECTS, NR, NB), 0, limits)
    return (owners * CAP + within).astype(jnp.int32)


def draw_columns(key, part):
    offsets = jax.random.randint(jax.random.fold_in(key, 53), (SUBJECTS, NR, NB, W), -2, 3)
    cells = jnp.arange(W, dtype=jnp.int32)
    return jnp.clip(cells + offsets, 0, W - 1).astype(jnp.int32)


def level_of(rng, shape, pieces, low, top_value):
    loudness = 1.0
    for axis_at, parts in pieces:
        draws = jax.random.uniform(jax.random.fold_in(jax.random.fold_in(rng, 6), axis_at), (parts,), jnp.float32, low / len(pieces), top_value / len(pieces))
        loudness = loudness * jnp.repeat(jnp.exp(draws), shape[axis_at] // parts).reshape((-1,) + (1,) * (len(shape) - 1 - axis_at))
    return loudness


def normal_values(stream_key, dims, spread, most, shards=(), kind=jnp.bfloat16):
    result = spread * jax.random.normal(stream_key, dims, jnp.float32)
    if shards:
        result = result * level_of(stream_key, dims, shards, -0.22, 0.18)
    return jnp.clip(result, -most, most).astype(kind)


def setup_inputs(seed: int = 0) -> dict:
    keys = jax.random.split(jax.random.key(seed), 9)
    return {
        "template": normal_values(keys[0], (NR, W), 1.0, 6.0, ((0, 8),), jnp.float32),
        "images": normal_values(keys[1], (SUBJECTS, NR, W), 1.0, 6.0, ((0, 4), (1, 8)), jnp.float32),
        "velocity": normal_values(keys[2], (SUBJECTS, 3, NR, W), 1.0, 6.0, ((0, 4), (2, 8)), jnp.float32),
        "stiffness": jnp.clip(jnp.exp(math.log(1.0) - 2.3025851 * jax.random.uniform(keys[3], (NR, W), jnp.float32) ** level_of(keys[3], (NR, W), ((0, 8),), -0.2, 0.2)), 0.1, 1.0),
        "send_rows": draw_send_rows(jax.random.fold_in(keys[8], 71), 0),
        "ref_slot": draw_ref_slot(jax.random.fold_in(keys[8], 71), 0),
        "columns": draw_columns(jax.random.fold_in(keys[8], 71), 0),
        "weights": jnp.clip(0.25 * jax.random.uniform(keys[7], (SUBJECTS, NR, NB, W), jnp.float32) ** level_of(keys[7], (SUBJECTS, NR, NB, W), ((0, 4), (1, 8)), -0.2, 0.2), 0.0, 0.25).astype(jnp.bfloat16),
    }


force_step = 1.0
diffusion_dt = 0.16
template_rate = 2.0


def central_slopes(grid_field):
    padded = jnp.pad(grid_field, 1)
    along_x = 0.5 * (padded[1:-1, 1:-1, 2:] - padded[1:-1, 1:-1, :-2])
    along_y = 0.5 * (padded[1:-1, 2:, 1:-1] - padded[1:-1, :-2, 1:-1])
    along_z = 0.5 * (padded[2:, 1:-1, 1:-1] - padded[:-2, 1:-1, 1:-1])
    return jnp.stack([along_x, along_y, along_z])


def smooth_step(field_padded, coef_padded):
    center = field_padded[:, 1:-1]
    coef_center = coef_padded[1:-1]
    field_yx = jnp.pad(center, ((0, 0), (0, 0), (1, 1), (1, 1)))
    coef_yx = jnp.pad(coef_center, ((0, 0), (1, 1), (1, 1)))
    pairs = [
        (field_padded[:, 2:], coef_padded[2:]),
        (field_padded[:, :-2], coef_padded[:-2]),
        (field_yx[:, :, 2:, 1:-1], coef_yx[:, 2:, 1:-1]),
        (field_yx[:, :, :-2, 1:-1], coef_yx[:, :-2, 1:-1]),
        (field_yx[:, :, 1:-1, 2:], coef_yx[:, 1:-1, 2:]),
        (field_yx[:, :, 1:-1, :-2], coef_yx[:, 1:-1, :-2]),
    ]
    summed = jnp.zeros(center.shape, jnp.float32)
    for neighbour, coef_near in pairs:
        face_coef = 0.5 * (coef_center + coef_near)
        summed = summed + face_coef[None] * (neighbour - center)
    return center + diffusion_dt * summed


def reference(template, images, velocity, stiffness, send_rows, ref_slot, columns, weights):
    depth_all = SLABS * PLANES
    owner_base = (jnp.arange(SLABS) * ROWS).astype(jnp.int32)
    dest_base = ((jnp.arange(NR) // ROWS) * (SLABS * CAP)).astype(jnp.int32)
    coef_grid = jnp.pad(stiffness.reshape(depth_all, YR, W), ((1, 1), (0, 0), (0, 0)))

    def per_subject(inputs):
        image_one, velocity_one, send_one, slot_one, columns_one, weights_one = inputs
        global_rows = owner_base[:, None, None] + send_one
        buffers = jnp.transpose(template[global_rows], (1, 0, 2, 3)).reshape(SLABS * SLABS * CAP, W)
        slot_global = dest_base[:, None] + slot_one
        picked = buffers[slot_global]
        values = jnp.take_along_axis(picked, columns_one, axis=2)
        weight_f = weights_one.astype(jnp.float32)
        warped = jnp.sum(weight_f * values, axis=1)
        mismatch = warped - image_one
        contrib = weight_f * mismatch[:, None, :]
        flat_index = (slot_global * W)[:, :, None] + columns_one
        slot_grad = jnp.zeros((SLABS * SLABS * CAP * W,), jnp.float32).at[flat_index.reshape(-1)].add(contrib.reshape(-1))
        slot_grad = jnp.transpose(slot_grad.reshape(SLABS, SLABS, CAP, W), (1, 0, 2, 3)).reshape(-1, W)
        row_grad = jnp.zeros((NR, W), jnp.float32).at[global_rows.reshape(-1)].add(slot_grad)
        slopes = central_slopes(warped.reshape(depth_all, YR, W))
        field = velocity_one.reshape(3, depth_all, YR, W) - force_step * mismatch.reshape(depth_all, YR, W)[None] * slopes
        for repeat in range(SMOOTH):
            field = smooth_step(jnp.pad(field, ((0, 0), (1, 1), (0, 0), (0, 0))), coef_grid)
        return row_grad, field.reshape(3, NR, W)

    row_grads, fields = lax.map(per_subject, (images, velocity, send_rows, ref_slot, columns, weights))
    template_out = template - template_rate * jnp.sum(row_grads, axis=0) / SUBJECTS
    return template_out, fields
```

```python
import functools

import jax
import jax.numpy as jnp
from jax import lax
from jax.experimental import pallas as pl
from jax.experimental.pallas import tpu as pltpu
from jax.sharding import PartitionSpec as P

YR = 256
SMOOTH = 2
LANES = 128


force_step = 1.0
diffusion_dt = 0.16
template_rate = 2.0

VMEM_LIMIT = 48 * 1024 * 1024


def call(kernel, out_shape, *args, scratch=()):
    return pl.pallas_call(
        kernel,
        out_shape=out_shape,
        scratch_shapes=scratch,
        compiler_params=pltpu.CompilerParams(vmem_limit_bytes=VMEM_LIMIT),
    )(*args)


def halves(values):
    high = values.astype(jnp.bfloat16)
    low = (values - high.astype(jnp.float32)).astype(jnp.bfloat16)
    return jnp.concatenate([high, low], axis=1)


def joined(pair):
    width = pair.shape[1] // 2
    return pair[:, :width] + pair[:, width:]


def dot(left, right):
    return jnp.dot(left, right, preferred_element_type=jnp.float32)


def one_hot(matches):
    return jnp.where(matches, 1.0, 0.0).astype(jnp.bfloat16)


def send_kernel(send_ref, template_ref, out_ref):
    slabs, capacity = send_ref.shape
    rows = template_ref.shape[0]
    pair = halves(template_ref[...])
    padded = jnp.concatenate(
        [send_ref[...], jnp.zeros((slabs, LANES - capacity), jnp.int32)], axis=1
    )
    turned = padded.T
    number = lax.broadcasted_iota(jnp.int32, (capacity, rows), 1)
    for k in range(slabs):
        wanted = jnp.broadcast_to(turned[:capacity, k : k + 1], (capacity, rows))
        out_ref[k * capacity : (k + 1) * capacity, :] = joined(dot(one_hot(wanted == number), pair))


def pick_kernel(step, wide_ref, flat_ref, pick_ref, drop_ref):
    terms, slots = pick_ref.shape
    lane = lax.broadcasted_iota(jnp.int32, (step, LANES), 1)
    row = lax.broadcasted_iota(jnp.int32, (slots, step), 0)

    def body(i, carry):
        at = pl.multiple_of(i * step, step)
        wide = wide_ref[pl.ds(at, step), :]
        for t in range(slots // LANES):
            pick_ref[pl.ds(at, step), t * LANES : (t + 1) * LANES] = one_hot(wide == lane + t * LANES)
        flat = jnp.broadcast_to(flat_ref[:, pl.ds(at, step)], (slots, step))
        drop_ref[:, pl.ds(at, step)] = one_hot(flat == row)
        return carry

    lax.fori_loop(0, terms // step, body, 0)


def warp_kernel(
    step,
    subjects,
    received_ref,
    pick_ref,
    drop_ref,
    columns_ref,
    weights_ref,
    images_ref,
    warped_ref,
    sent_ref,
    total_ref,
):
    terms, slots = pick_ref.shape
    rows, width = images_ref.shape
    each = terms // rows
    step_rows = step // each
    pair = halves(received_ref[...])
    total_ref[...] = jnp.zeros_like(total_ref)
    cell = lax.broadcasted_iota(jnp.int32, (step, width), 1)

    def body(i, carry):
        at = pl.multiple_of(i * step, step)
        at_row = pl.multiple_of(i * step_rows, step_rows)
        picked = joined(dot(pick_ref[pl.ds(at, step), :], pair))
        columns = columns_ref[pl.ds(at, step), :]
        weights = weights_ref[pl.ds(at, step), :].astype(jnp.float32)
        values = weights * jnp.take_along_axis(picked, columns, axis=1, mode="promise_in_bounds")
        warped = jnp.sum(values.reshape(step_rows, each, width), axis=1)
        warped_ref[pl.ds(at_row, step_rows), :] = warped
        mismatch = warped - images_ref[pl.ds(at_row, step_rows), :]
        spread = jnp.broadcast_to(mismatch[:, None, :], (step_rows, each, width)).reshape(step, width)
        contrib = weights * spread
        offset = columns - cell
        placed = jnp.where(offset == 0, contrib, 0.0)
        for o in (-2, -1, 1, 2):
            placed = placed + pltpu.roll(jnp.where(offset == o, contrib, 0.0), o % width, axis=1)
        total_ref[...] += dot(drop_ref[:, pl.ds(at, step)], halves(placed))
        return carry

    lax.fori_loop(0, terms // step, body, 0)
    block = width // subjects
    group = slots // subjects
    place = lax.broadcasted_iota(jnp.int32, (group, width), 1) // block
    groups = [joined(total_ref[q * group : (q + 1) * group, :]) for q in range(subjects)]
    for p in range(subjects):
        out = jnp.zeros((group, width), jnp.float32)
        for q in range(subjects):
            turn = ((q - p) * block) % width
            moved = pltpu.roll(groups[q], turn, axis=1) if turn else groups[q]
            out = jnp.where(place == q, moved, out)
        sent_ref[p * group : (p + 1) * group, :] = out


def collect_kernel(subjects, index_ref, returned_ref, out_ref):
    slots, width = returned_ref.shape
    rows = out_ref.shape[0] * subjects
    block = width // subjects
    pair = halves(returned_ref[...])
    number = lax.broadcasted_iota(jnp.int32, (rows, slots), 0)
    place = lax.broadcasted_iota(jnp.int32, (rows, width), 1) // block
    kept = jnp.zeros((rows, width), jnp.float32)
    for q in range(subjects):
        wanted = jnp.broadcast_to(index_ref[q : q + 1, :], (rows, slots))
        kept = jnp.where(place == q, joined(dot(one_hot(wanted == number), pair)), kept)
    turn = block
    while turn < width:
        kept = kept + pltpu.roll(kept, turn, axis=1)
        turn *= 2
    part = rows // subjects
    out = jnp.zeros((part, width), jnp.float32)
    for p in range(subjects):
        out = jnp.where(place[:part] == p, kept[p * part : (p + 1) * part], out)
    out_ref[...] = out


def update_kernel(subjects, template_ref, parts_ref, out_ref):
    rows, width = template_ref.shape
    block = width // subjects
    part = rows // subjects
    place = lax.broadcasted_iota(jnp.int32, (part, width), 1) // block
    for p in range(subjects):
        total = jnp.zeros((part, width), jnp.float32)
        for s in range(subjects):
            turn = ((s - p) * block) % width
            held = parts_ref[s]
            moved = pltpu.roll(held, turn, axis=1) if turn else held
            total = jnp.where(place == s, moved, total)
        at = slice(p * part, (p + 1) * part)
        out_ref[at, :] = template_ref[at, :] - template_rate * total / subjects


def over_subjects(values):
    count = lax.axis_size("subj")
    return lax.all_gather(values, "subj")


def extended(cells, sides, width):
    for axis, dim in sides:
        count = lax.axis_size(axis)
        ends = count - 1
        head = lax.slice_in_dim(cells, 0, width, axis=dim)
        tail = lax.slice_in_dim(cells, cells.shape[dim] - width, cells.shape[dim], axis=dim)
        cells = jnp.concatenate(
            [
                lax.ppermute(tail, axis, [(i, (i + 1) % count) for i in range(ends)]),
                cells,
                lax.ppermute(head, axis, [((i + 1) % count, i) for i in range(ends)]),
            ],
            axis=dim,
        )
    return cells


def smooth_step(field_padded, coef_padded):
    center = field_padded[:, 1:-1]
    coef_center = coef_padded[1:-1]
    field_yx = jnp.pad(center, ((0, 0), (0, 0), (1, 1), (1, 1)))
    coef_yx = jnp.pad(coef_center, ((0, 0), (1, 1), (1, 1)))
    pairs = [
        (field_padded[:, 2:], coef_padded[2:]),
        (field_padded[:, :-2], coef_padded[:-2]),
        (field_yx[:, :, 2:, 1:-1], coef_yx[:, 2:, 1:-1]),
        (field_yx[:, :, :-2, 1:-1], coef_yx[:, :-2, 1:-1]),
        (field_yx[:, :, 1:-1, 2:], coef_yx[:, 1:-1, 2:]),
        (field_yx[:, :, 1:-1, :-2], coef_yx[:, 1:-1, :-2]),
    ]
    summed = jnp.zeros(center.shape, jnp.float32)
    for neighbour, coef_near in pairs:
        face_coef = 0.5 * (coef_center + coef_near)
        summed = summed + face_coef[None] * (neighbour - center)
    return center + diffusion_dt * summed


def per_device(template, images, velocity, stiffness, send_rows, ref_slot, columns, weights):
    f32 = jnp.float32
    slabs = lax.axis_size("slab")
    subjects = lax.axis_size("subj")
    capacity = send_rows.shape[3]
    rows, width = template.shape
    planes = rows // YR
    each = ref_slot.shape[2]
    terms = rows * each
    slots = slabs * capacity
    group = capacity // subjects
    step = 256

    sending = call(
        send_kernel, jax.ShapeDtypeStruct((slots, width), f32), send_rows[0, 0], template
    )
    received = lax.all_to_all(sending, "slab", split_axis=0, concat_axis=0, tiled=True)

    slot_flat = ref_slot.reshape(terms)
    slot_wide = jnp.broadcast_to(slot_flat[:, None], (terms, LANES))
    owner, inner = slot_flat // capacity, slot_flat % capacity
    slot_packed = (inner // group) * (slabs * group) + owner * group + inner % group
    pick, drop = call(
        functools.partial(pick_kernel, step),
        (
            jax.ShapeDtypeStruct((terms, slots), jnp.bfloat16),
            jax.ShapeDtypeStruct((slots, terms), jnp.bfloat16),
        ),
        slot_wide,
        slot_packed[None],
    )
    all_rows = over_subjects(send_rows[0, 0]).reshape(subjects, slabs, subjects, group)
    row_index = jnp.transpose(all_rows, (2, 0, 1, 3)).reshape(subjects, slots)

    warped, sent = call(
        functools.partial(warp_kernel, step, subjects),
        (
            jax.ShapeDtypeStruct((rows, width), f32),
            jax.ShapeDtypeStruct((slots, width), f32),
        ),
        received,
        pick,
        drop,
        columns.reshape(terms, width),
        weights.reshape(terms, width),
        images[0],
        scratch=(pltpu.VMEM((slots, 2 * width), f32),),
    )
    returned = lax.all_to_all(sent, ("subj", "slab"), split_axis=0, concat_axis=0, tiled=True)
    part = call(
        functools.partial(collect_kernel, subjects),
        jax.ShapeDtypeStruct((rows // subjects, width), f32),
        row_index,
        returned,
    )
    parts = over_subjects(part)
    template_out = call(
        functools.partial(update_kernel, subjects),
        jax.ShapeDtypeStruct((rows, width), f32),
        template,
        parts,
    )

    mismatch = warped - images[0]
    warped_grid = warped.reshape(planes, YR, width)
    warped_padded = extended(warped_grid, (("slab", 0),), 1)
    warped_yx = jnp.pad(warped_grid, ((0, 0), (1, 1), (1, 1)))
    along_x = 0.5 * (warped_yx[:, 1:-1, 2:] - warped_yx[:, 1:-1, :-2])
    along_y = 0.5 * (warped_yx[:, 2:, 1:-1] - warped_yx[:, :-2, 1:-1])
    along_z = 0.5 * (warped_padded[2:] - warped_padded[:-2])
    slopes = jnp.stack([along_x, along_y, along_z])
    field = (
        velocity[0].reshape(3, planes, YR, width)
        - force_step * mismatch.reshape(planes, YR, width)[None] * slopes
    )
    coef_grid = stiffness.reshape(planes, YR, width)
    coef_padded = extended(coef_grid, (("slab", 0),), 1)
    for repeat in range(SMOOTH):
        field_padded = extended(field, (("slab", 1),), 1)
        field = smooth_step(field_padded, coef_padded)
    velocity_out = field.reshape(3, rows, width)[None]
    return (template_out, velocity_out)


def solution(mesh):
    return jax.shard_map(
        per_device,
        mesh=mesh,
        in_specs=(
            P("slab", None),
            P("subj", "slab", None),
            P("subj", None, "slab", None),
            P("slab", None),
            P("subj", "slab", None, None),
            P("subj", "slab", None),
            P("subj", "slab", None, None),
            P("subj", "slab", None, None),
        ),
        out_specs=(P("slab", None), P("subj", None, "slab", None)),
        check_vma=False,
    )
```

```python
import functools

import jax
import jax.numpy as jnp
from jax import lax
from jax.experimental import pallas as pl
from jax.experimental.pallas import tpu as pltpu
from jax.sharding import PartitionSpec as P

YR = 256
LANES = 128
OFFSETS = (0, -2, -1, 1, 2)


force_step = 1.0
diffusion_dt = 0.16
template_rate = 2.0

VMEM_LIMIT = 32 * 1024 * 1024


def call(kernel, out_shape, *args, scratch=(), smem=()):
    spaces = [pltpu.SMEM if i in smem else pltpu.VMEM for i in range(len(args))]
    return pl.pallas_call(
        kernel,
        out_shape=out_shape,
        in_specs=[pl.BlockSpec(memory_space=space) for space in spaces],
        scratch_shapes=scratch,
        compiler_params=pltpu.CompilerParams(vmem_limit_bytes=VMEM_LIMIT),
    )(*args)


def halves(values):
    high = values.astype(jnp.bfloat16)
    low = (values - high.astype(jnp.float32)).astype(jnp.bfloat16)
    return jnp.concatenate([high, low], axis=1)


def joined(pair):
    width = pair.shape[1] // 2
    return pair[:, :width] + pair[:, width:]


def turned(values, shift):
    shift %= values.shape[1]
    return pltpu.roll(values, shift, axis=1) if shift else values


def dot(left, right):
    return jnp.dot(left, right, preferred_element_type=jnp.float32)


def one_hot(matches):
    return jnp.where(matches, 1.0, 0.0).astype(jnp.bfloat16)


def send_kernel(send_ref, template_ref, out_ref):
    slabs, capacity = send_ref.shape
    rows = template_ref.shape[0]
    pair = halves(template_ref[...])
    padded = jnp.concatenate(
        [send_ref[...], jnp.zeros((slabs, LANES - capacity), jnp.int32)], axis=1
    )
    turned = padded.T
    number = lax.broadcasted_iota(jnp.int32, (capacity, rows), 1)
    for k in range(slabs):
        wanted = jnp.broadcast_to(turned[:capacity, k : k + 1], (capacity, rows))
        out_ref[k * capacity : (k + 1) * capacity, :] = joined(dot(one_hot(wanted == number), pair))


def prepare_kernel(
    step, wide_ref, flat_ref, columns_ref, weights_ref, pick_ref, drop_ref, moved_ref, plain_ref
):
    terms, slots = pick_ref.shape
    each, rows, width = moved_ref.shape[1:]
    lane = lax.broadcasted_iota(jnp.int32, (step, LANES), 1)
    row = lax.broadcasted_iota(jnp.int32, (slots, step), 0)

    def hot(i, carry):
        at = pl.multiple_of(i * step, step)
        wide = wide_ref[pl.ds(at, step), :]
        for t in range(slots // LANES):
            pick_ref[pl.ds(at, step), t * LANES : (t + 1) * LANES] = one_hot(wide == lane + t * LANES)
        flat = jnp.broadcast_to(flat_ref[:, pl.ds(at, step)], (slots, step))
        drop_ref[:, pl.ds(at, step)] = one_hot(flat == row)
        return carry

    lax.fori_loop(0, terms // step, hot, 0)
    plain_ref[...] = weights_ref[...].astype(jnp.float32)
    some = step // each
    cell = lax.broadcasted_iota(jnp.int32, (some, width), 1)

    def move(i, carry):
        at = pl.multiple_of(i * step, step)
        at_row = pl.multiple_of(i * some, some)
        for b in range(each):
            offset = columns_ref[pl.ds(at + b, some, stride=each), :] - cell
            weights = plain_ref[pl.ds(at + b, some, stride=each), :]
            for j, o in enumerate(OFFSETS):
                kept = jnp.where(offset == o, weights, 0.0)
                moved_ref[j, b, pl.ds(at_row, some), :] = turned(kept, o).astype(jnp.bfloat16)
        return carry

    lax.fori_loop(0, terms // step, move, 0)


def warp_kernel(
    some,
    subjects,
    received_ref,
    pick_ref,
    drop_ref,
    moved_ref,
    images_ref,
    warped_ref,
    sent_ref,
    picked_ref,
    placed_ref,
):
    slots, width = received_ref.shape
    each, rows = moved_ref.shape[1:3]
    terms = each * rows
    pair = halves(received_ref[...])
    for b in range(each):
        picked_ref[b] = joined(dot(pick_ref[b * rows : (b + 1) * rows, :], pair))

    def body(i, carry):
        at = pl.multiple_of(i * some, some)
        sums = [jnp.zeros((some, width), jnp.float32) for _ in OFFSETS]
        for b in range(each):
            picked = picked_ref[b, pl.ds(at, some), :]
            for j in range(len(OFFSETS)):
                sums[j] = sums[j] + moved_ref[j, b, pl.ds(at, some), :].astype(jnp.float32) * picked
        warped = sums[0]
        for j, o in enumerate(OFFSETS[1:], 1):
            warped = warped + turned(sums[j], -o)
        warped_ref[pl.ds(at, some), :] = warped
        mismatch = warped - images_ref[pl.ds(at, some), :]
        ahead = [turned(mismatch, o) for o in OFFSETS]
        for b in range(each):
            placed = moved_ref[0, b, pl.ds(at, some), :].astype(jnp.float32) * ahead[0]
            for j in range(1, len(OFFSETS)):
                placed = placed + moved_ref[j, b, pl.ds(at, some), :].astype(jnp.float32) * ahead[j]
            placed_ref[b, pl.ds(at, some), :] = halves(placed)
        return carry

    lax.fori_loop(0, rows // some, body, 0)
    total = joined(dot(drop_ref[...], placed_ref[...].reshape(terms, 2 * width)))
    block = width // subjects
    group = slots // subjects
    place = lax.broadcasted_iota(jnp.int32, (group, width), 1) // block
    groups = [total[q * group : (q + 1) * group, :] for q in range(subjects)]
    for p in range(subjects):
        out = jnp.zeros((group, width), jnp.float32)
        for q in range(subjects):
            out = jnp.where(place == q, turned(groups[q], (q - p) * block), out)
        sent_ref[p * group : (p + 1) * group, :] = out


def collect_kernel(subjects, index_ref, me_ref, returned_ref, out_ref):
    slots, width = returned_ref.shape
    rows = out_ref.shape[0] * subjects
    block = width // subjects
    group = slots // subjects
    me = me_ref[0]
    pair = halves(
        jnp.concatenate(
            [
                returned_ref[pl.ds(pl.multiple_of((me ^ d) * group, group), group), :]
                for d in range(subjects)
            ]
        )
    )
    number = lax.broadcasted_iota(jnp.int32, (rows, slots), 0)
    place = lax.broadcasted_iota(jnp.int32, (rows, width), 1) // block
    kept = jnp.zeros((rows, width), jnp.float32)
    for q in range(subjects):
        wanted = jnp.broadcast_to(index_ref[q : q + 1, :], (rows, slots))
        kept = jnp.where(place == q, joined(dot(one_hot(wanted == number), pair)), kept)
    turn = block
    while turn < width:
        kept = kept + turned(kept, turn)
        turn *= 2
    part = rows // subjects
    out = jnp.zeros((part, width), jnp.float32)
    for p in range(subjects):
        out = jnp.where(place[:part] == p, kept[p * part : (p + 1) * part], out)
    out_ref[...] = out


def update_kernel(subjects, me_ref, template_ref, *refs):
    parts, out_ref = refs[:-1], refs[-1]
    rows, width = template_ref.shape
    block = width // subjects
    part = rows // subjects
    me = me_ref[0]
    place = lax.broadcasted_iota(jnp.int32, (part, width), 1) // block
    for p in range(subjects):
        total = jnp.zeros((part, width), jnp.float32)
        for d in range(subjects):
            source = me ^ d
            turn = lax.rem((source - p) * block + width, width)
            total = jnp.where(place == source, pltpu.roll(parts[d][...], turn, axis=1), total)
        at = slice(p * part, (p + 1) * part)
        out_ref[at, :] = template_ref[at, :] - template_rate * total / subjects


def over_subjects(values):
    count = lax.axis_size("subj")
    return [values] + [
        lax.ppermute(values, "subj", [(i, i ^ d) for i in range(count)]) for d in range(1, count)
    ]


def with_neighbours(low_side, high_side):
    count = lax.axis_size("slab")
    odd = lax.axis_index("slab") % 2 == 1
    near = [(i, i ^ 1) for i in range(count)]
    far = [(i, i + 1 if i % 2 else i - 1) for i in range(1, count - 1)]
    from_far = lax.ppermute(jnp.where(odd, high_side, low_side), "slab", far)
    from_near = lax.ppermute(jnp.where(odd, low_side, high_side), "slab", near)
    return jnp.where(odd, from_near, from_far), jnp.where(odd, from_far, from_near)


def shifted(values, step, axis):
    size = values.shape[axis]
    index = lax.broadcasted_iota(jnp.int32, values.shape, axis)
    edge = size - 1 if step > 0 else 0
    return jnp.where(index == edge, 0.0, pltpu.roll(values, (-step) % size, axis=axis))


def diffuse(below, center, above, coef_below, coef, coef_above):
    summed = 0.5 * (coef + coef_above) * (above - center)
    summed = summed + 0.5 * (coef + coef_below) * (below - center)
    for axis in (0, 1):
        for step in (1, -1):
            face = 0.5 * (coef + shifted(coef, step, axis))
            summed = summed + face * (shifted(center, step, axis) - center)
    return center + diffusion_dt * summed


def force_kernel(
    velocity_ref,
    images_ref,
    stiffness_ref,
    warped_ref,
    low_ref,
    high_ref,
    warped_low_ref,
    warped_high_ref,
    out_ref,
):
    planes = out_ref.shape[1]
    components = out_ref.shape[0]
    coefs = [low_ref[components]] + [stiffness_ref[p] for p in range(planes)] + [high_ref[components]]
    images = [low_ref[components + 1]] + [images_ref[p] for p in range(planes)] + [high_ref[components + 1]]
    near = [warped_low_ref[p] for p in range(2)]
    far = [warped_high_ref[p] for p in range(2)]
    warped = near + [warped_ref[p] for p in range(planes)] + far
    fields = [[] for _ in range(components)]
    for p in range(planes + 2):
        here = warped[p + 1]
        mismatch = here - images[p]
        slopes = [
            0.5 * (shifted(here, 1, 1) - shifted(here, -1, 1)),
            0.5 * (shifted(here, 1, 0) - shifted(here, -1, 0)),
            0.5 * (warped[p + 2] - warped[p]),
        ]
        for a in range(components):
            if p == 0:
                velocity = low_ref[a]
            elif p == planes + 1:
                velocity = high_ref[a]
            else:
                velocity = velocity_ref[a, p - 1]
            fields[a].append(velocity - force_step * mismatch * slopes[a])
    for a in range(components):
        for p in range(planes):
            out_ref[a, p] = diffuse(*fields[a][p : p + 3], *coefs[p : p + 3])


def last_kernel(field_ref, stiffness_ref, low_ref, high_ref, coef_low_ref, coef_high_ref, out_ref):
    components, planes = out_ref.shape[:2]
    coefs = [coef_low_ref[0]] + [stiffness_ref[p] for p in range(planes)] + [coef_high_ref[0]]
    for a in range(components):
        fields = [low_ref[a]] + [field_ref[a, p] for p in range(planes)] + [high_ref[a]]
        for p in range(planes):
            out_ref[a, p] = diffuse(*fields[p : p + 3], *coefs[p : p + 3])


def per_device(template, images, velocity, stiffness, send_rows, ref_slot, columns, weights):
    f32, bf16 = jnp.float32, jnp.bfloat16
    shape = jax.ShapeDtypeStruct
    slabs = lax.axis_size("slab")
    subjects = lax.axis_size("subj")
    me = lax.axis_index("subj").astype(jnp.int32).reshape(1)
    capacity = send_rows.shape[3]
    rows, width = template.shape
    planes = rows // YR
    each = ref_slot.shape[2]
    terms = rows * each
    slots = slabs * capacity
    group = capacity // subjects
    step = 256

    sending = call(send_kernel, shape((slots, width), f32), send_rows[0, 0], template)
    received = lax.all_to_all(sending, "slab", split_axis=0, concat_axis=0, tiled=True)

    slot_flat = ref_slot[0].T.reshape(terms)
    slot_wide = jnp.broadcast_to(slot_flat[:, None], (terms, LANES))
    owner, inner = slot_flat // capacity, slot_flat % capacity
    slot_packed = (inner // group) * (slabs * group) + owner * group + inner % group
    pick, drop, moved = call(
        functools.partial(prepare_kernel, step),
        (
            shape((terms, slots), bf16),
            shape((slots, terms), bf16),
            shape((len(OFFSETS), each, rows, width), bf16),
        ),
        slot_wide,
        slot_packed[None],
        columns.reshape(terms, width),
        weights.reshape(terms, width),
        scratch=(pltpu.VMEM((terms, width), f32),),
    )
    all_rows = jnp.stack(over_subjects(send_rows[0, 0])).reshape(subjects, slabs, subjects, group)
    row_index = jnp.transpose(all_rows, (2, 0, 1, 3)).reshape(subjects, slots)

    velocity_grid = velocity[0].reshape(3, planes, YR, width)
    images_grid = images[0].reshape(planes, YR, width)
    coef_grid = stiffness.reshape(planes, YR, width)
    edges = lambda p: jnp.concatenate([velocity_grid[:, p], coef_grid[p][None], images_grid[p][None]])
    low_side, high_side = edges(0), edges(planes - 1)
    low, high = with_neighbours(low_side, high_side)

    warped, sent = call(
        functools.partial(warp_kernel, 64, subjects),
        (shape((rows, width), f32), shape((slots, width), f32)),
        received,
        pick,
        drop,
        moved,
        images[0],
        scratch=(
            pltpu.VMEM((each, rows, width), f32),
            pltpu.VMEM((each, rows, 2 * width), bf16),
        ),
    )
    returned = lax.all_to_all(sent, ("subj", "slab"), split_axis=0, concat_axis=0, tiled=True)
    warped_grid = warped.reshape(planes, YR, width)
    warped_low, warped_high = with_neighbours(warped_grid[:2], warped_grid[-2:])

    part = call(
        functools.partial(collect_kernel, subjects),
        shape((rows // subjects, width), f32),
        row_index,
        me,
        returned,
        smem=(1,),
    )
    parts = over_subjects(part)

    warped_grid, _ = lax.optimization_barrier((warped_grid, part))
    field = call(
        force_kernel,
        shape((3, planes, YR, width), f32),
        velocity_grid,
        images_grid,
        coef_grid,
        warped_grid,
        low,
        high,
        warped_low,
        warped_high,
    )
    field_low, field_high = with_neighbours(field[:, 0], field[:, -1])
    template_out = call(
        functools.partial(update_kernel, subjects),
        shape((rows, width), f32),
        me,
        template,
        *parts,
        smem=(0,),
    )
    field = call(
        last_kernel,
        shape((3, planes, YR, width), f32),
        field,
        coef_grid,
        field_low,
        field_high,
        low[3:4],
        high[3:4],
    )
    velocity_out = field.reshape(3, rows, width)[None]
    return (template_out, velocity_out)


def solution(mesh):
    return jax.shard_map(
        per_device,
        mesh=mesh,
        in_specs=(
            P("slab", None),
            P("subj", "slab", None),
            P("subj", None, "slab", None),
            P("slab", None),
            P("subj", "slab", None, None),
            P("subj", "slab", None),
            P("subj", "slab", None, None),
            P("subj", "slab", None, None),
        ),
        out_specs=(P("slab", None), P("subj", None, "slab", None)),
        check_vma=False,
    )
```

```python
import functools

import jax
import jax.numpy as jnp
from jax import lax
from jax.experimental import pallas as pl
from jax.experimental.pallas import tpu as pltpu
from jax.sharding import PartitionSpec as P

YR = 256
LANES = 128
OFFSETS = (0, -2, -1, 1, 2)


force_step = 1.0
diffusion_dt = 0.16
template_rate = 2.0

VMEM_LIMIT = 40 * 1024 * 1024
COST = 1024


def call(kernel, out_shape, *args, scratch=(), smem=(), far=(), out_far=(), cost=None):
    many = isinstance(out_shape, tuple)
    shapes = [
        pltpu.HBM(s.shape, s.dtype) if i in out_far else s
        for i, s in enumerate(out_shape if many else (out_shape,))
    ]
    spaces = [pltpu.HBM if i in out_far else pltpu.VMEM for i in range(len(shapes))]
    specs = [pl.BlockSpec(memory_space=space) for space in spaces]
    return pl.pallas_call(
        kernel,
        out_shape=tuple(shapes) if many else shapes[0],
        in_specs=[
            pl.BlockSpec(
                memory_space=pltpu.SMEM if i in smem else pltpu.HBM if i in far else pltpu.VMEM
            )
            for i in range(len(args))
        ],
        out_specs=tuple(specs) if many else specs[0],
        scratch_shapes=scratch,
        cost_estimate=cost and pl.CostEstimate(flops=0, transcendentals=0, bytes_accessed=cost),
        compiler_params=pltpu.CompilerParams(vmem_limit_bytes=VMEM_LIMIT),
    )(
        *[
            pltpu.with_memory_space_constraint(arg, pltpu.HBM) if i in far else arg
            for i, arg in enumerate(args)
        ]
    )


def halves(values):
    high = values.astype(jnp.bfloat16)
    low = (values - high.astype(jnp.float32)).astype(jnp.bfloat16)
    return jnp.concatenate([high, low], axis=1)


def joined(pair):
    width = pair.shape[1] // 2
    return pair[:, :width] + pair[:, width:]


def turned(values, shift):
    shift %= values.shape[1]
    return pltpu.roll(values, shift, axis=1) if shift else values


def dot(left, right):
    return jnp.dot(left, right, preferred_element_type=jnp.float32)


def one_hot(matches):
    return jnp.where(matches, 1.0, 0.0).astype(jnp.bfloat16)


def send_kernel(send_ref, template_ref, out_ref, send, template, sem):
    slabs, capacity = send.shape
    rows = template.shape[0]
    copies = [
        pltpu.make_async_copy(send_ref, send, sem.at[0]),
        pltpu.make_async_copy(template_ref, template, sem.at[1]),
    ]
    for copy in copies:
        copy.start()
    copies[0].wait()
    padded = jnp.concatenate([send[...], jnp.zeros((slabs, LANES - capacity), jnp.int32)], axis=1)
    columns = padded.T
    number = lax.broadcasted_iota(jnp.int32, (capacity, rows), 1)
    chosen = [
        one_hot(jnp.broadcast_to(columns[:capacity, k : k + 1], (capacity, rows)) == number)
        for k in range(slabs)
    ]
    copies[1].wait()
    pair = halves(template[...])
    for k in range(slabs):
        out_ref[k * capacity : (k + 1) * capacity, :] = joined(dot(chosen[k], pair))


def prepare_kernel(
    place_ref,
    columns_ref,
    weights_ref,
    velocity_ref,
    stiffness_ref,
    images_ref,
    moved_ref,
    near_ref,
    far_ref,
    columns,
    weights,
    plain,
    moved,
    edge,
    in_sem,
    out_sem,
    edge_sem,
):
    chunks, each, count, some, width = moved.shape
    odd = place_ref[0]
    near_plane, far_plane = pl.ds((edge.shape[1] - 1) * (1 - odd), 1), pl.ds((edge.shape[1] - 1) * odd, 1)
    step = some * each
    parts = velocity_ref.shape[0]
    reads = [
        (
            pltpu.make_async_copy(
                columns_ref.at[pl.ds(i * step, step)], columns.at[pl.ds(i * step, step)], in_sem.at[i]
            ),
            pltpu.make_async_copy(
                weights_ref.at[pl.ds(i * step, step)],
                weights.at[pl.ds(i * step, step)],
                in_sem.at[chunks + i],
            ),
        )
        for i in range(chunks)
    ]
    edges = [
        pltpu.make_async_copy(velocity_ref, edge.at[pl.ds(0, parts)], edge_sem.at[0]),
        pltpu.make_async_copy(stiffness_ref, edge.at[parts], edge_sem.at[1]),
        pltpu.make_async_copy(images_ref, edge.at[parts + 1], edge_sem.at[2]),
    ]
    writes = [
        pltpu.make_async_copy(moved.at[i], moved_ref.at[i], out_sem.at[i]) for i in range(chunks)
    ] + [
        pltpu.make_async_copy(edge.at[:, near_plane], near_ref, out_sem.at[chunks]),
        pltpu.make_async_copy(edge.at[:, far_plane], far_ref, out_sem.at[chunks + 1]),
    ]
    for copy in reads[0]:
        copy.start()
    for copy in edges:
        copy.start()
    for pair in reads[1:]:
        for copy in pair:
            copy.start()
    cell = lax.broadcasted_iota(jnp.int32, (some, width), 1)
    for i in range(chunks):
        at = i * step
        for copy in reads[i]:
            copy.wait()
        plain[...] = weights[at : at + step, :].astype(jnp.float32)
        for b in range(each):
            offset = columns[pl.ds(at + b, some, stride=each), :] - cell
            here = plain[pl.ds(b, some, stride=each), :]
            for j, o in enumerate(OFFSETS):
                kept = jnp.where(offset == o, here, 0.0)
                moved[i, b, j] = turned(kept, o).astype(jnp.bfloat16)
        writes[i].start()
        if i == 0:
            for copy in edges:
                copy.wait()
            for copy in writes[chunks:]:
                copy.start()
    for copy in writes:
        copy.wait()


def warp_kernel(
    slabs,
    subjects,
    slot_ref,
    received_ref,
    moved_ref,
    images_ref,
    warped_ref,
    sent_ref,
    received,
    images,
    moved,
    picked,
    placed,
    first_sem,
    moved_sem,
):
    slots, width = received.shape
    chunks, each, count, some = moved.shape[:4]
    rows = chunks * some
    block = width // subjects
    group = slots // subjects
    capacity = slots // slabs
    held = capacity // subjects
    first = [
        pltpu.make_async_copy(received_ref, received, first_sem.at[0]),
        pltpu.make_async_copy(images_ref, images, first_sem.at[1]),
    ]
    moves = [
        pltpu.make_async_copy(moved_ref.at[i], moved.at[i], moved_sem.at[i]) for i in range(chunks)
    ]
    for copy in first + moves:
        copy.start()
    slot = slot_ref[...]
    slot_wide = jnp.concatenate([slot, jnp.zeros((LANES - each, rows), jnp.int32)], axis=0).T
    inner = slot % capacity
    packed = (inner // held) * group + (slot // capacity) * held + inner % held
    lane = lax.broadcasted_iota(jnp.int32, (rows, LANES), 1)
    number = lax.broadcasted_iota(jnp.int32, (slots, rows), 0)
    first[0].wait()
    pair = halves(received[...])
    for b in range(each):
        wide = jnp.broadcast_to(slot_wide[:, b : b + 1], (rows, LANES))
        pick = jnp.concatenate(
            [one_hot(wide == lane + t * LANES) for t in range(slots // LANES)], axis=1
        )
        picked[b] = joined(dot(pick, pair))
    first[1].wait()
    for i in range(chunks):
        moves[i].wait()
        at = slice(i * some, (i + 1) * some)
        sums = [jnp.zeros((some, width), jnp.float32) for _ in OFFSETS]
        for b in range(each):
            values = picked[b, at, :]
            for j in range(count):
                sums[j] = sums[j] + moved[i, b, j].astype(jnp.float32) * values
        warped = sums[0]
        for j, o in enumerate(OFFSETS[1:], 1):
            warped = warped + turned(sums[j], -o)
        warped_ref[at, :] = warped
        mismatch = warped - images[at, :]
        ahead = [turned(mismatch, o) for o in OFFSETS]
        for b in range(each):
            total = moved[i, b, 0].astype(jnp.float32) * ahead[0]
            for j in range(1, count):
                total = total + moved[i, b, j].astype(jnp.float32) * ahead[j]
            placed[b, at, :] = halves(total)
    total = jnp.zeros((slots, 2 * width), jnp.float32)
    for b in range(each):
        drop = one_hot(jnp.broadcast_to(packed[b : b + 1], (slots, rows)) == number)
        total = total + dot(drop, placed[b])
    total = joined(total)
    place = lax.broadcasted_iota(jnp.int32, (group, width), 1) // block
    groups = [total[q * group : (q + 1) * group, :] for q in range(subjects)]
    for p in range(subjects):
        out = jnp.zeros((group, width), jnp.float32)
        for q in range(subjects):
            out = jnp.where(place == q, turned(groups[q], (q - p) * block), out)
        sent_ref[p * group : (p + 1) * group, :] = out


def collect_kernel(subjects, me_ref, returned_ref, *refs):
    row_refs, out_ref = refs[:-1], refs[-1]
    slots, width = returned_ref.shape
    slabs, capacity = row_refs[0].shape
    rows = out_ref.shape[0] * subjects
    block = width // subjects
    group = slots // subjects
    held = capacity // subjects
    me = me_ref[0]
    pair = halves(
        jnp.concatenate(
            [
                returned_ref[pl.ds(pl.multiple_of((me ^ d) * group, group), group), :]
                for d in range(subjects)
            ]
        )
    )
    lane = lax.broadcasted_iota(jnp.int32, (slabs, LANES), 1)
    slab = lax.broadcasted_iota(jnp.int32, (slabs, LANES), 0)
    fill = jnp.zeros((slabs, LANES - capacity), jnp.int32)
    wanted = []
    for q in range(subjects):
        chunks = [jnp.zeros((1, LANES), jnp.int32) for _ in range(slots // LANES)]
        for d in range(subjects):
            spread = jnp.concatenate([row_refs[d][...], fill], axis=1)
            spread = turned(spread, d * group - q * held)
            spread = pltpu.roll(spread, 0, axis=1, stride=held, stride_axis=0)
            first = (d * group) % LANES + slab * held
            kept = jnp.where((lane >= first) & (lane < first + held), spread, 0)
            chunks[d * group // LANES] += jnp.sum(kept, axis=0, keepdims=True)
        wanted.append(jnp.concatenate(chunks, axis=1))
    number = lax.broadcasted_iota(jnp.int32, (rows, slots), 0)
    place = lax.broadcasted_iota(jnp.int32, (rows, width), 1) // block
    kept = jnp.zeros((rows, width), jnp.float32)
    for q in range(subjects):
        match = jnp.broadcast_to(wanted[q], (rows, slots)) == number
        kept = jnp.where(place == q, joined(dot(one_hot(match), pair)), kept)
    turn = block
    while turn < width:
        kept = kept + turned(kept, turn)
        turn *= 2
    part = rows // subjects
    out = jnp.zeros((part, width), jnp.float32)
    for p in range(subjects):
        out = jnp.where(place[:part] == p, kept[p * part : (p + 1) * part], out)
    out_ref[...] = out


def update_kernel(subjects, me_ref, template_ref, *refs):
    parts, out_ref = refs[:-1], refs[-1]
    rows, width = template_ref.shape
    block = width // subjects
    part = rows // subjects
    me = me_ref[0]
    place = lax.broadcasted_iota(jnp.int32, (part, width), 1) // block
    for p in range(subjects):
        total = jnp.zeros((part, width), jnp.float32)
        for d in range(subjects):
            source = me ^ d
            turn = lax.rem((source - p) * block + width, width)
            total = jnp.where(place == source, pltpu.roll(parts[d][...], turn, axis=1), total)
        at = slice(p * part, (p + 1) * part)
        out_ref[at, :] = template_ref[at, :] - template_rate * total / subjects


def over_subjects(values):
    count = lax.axis_size("subj")
    return [values] + [
        lax.ppermute(values, "subj", [(i, i ^ d) for i in range(count)]) for d in range(1, count)
    ]


def swap_near(values):
    return lax.ppermute(values, "slab", [(i, i ^ 1) for i in range(lax.axis_size("slab"))])


def swap_far(values):
    count = lax.axis_size("slab")
    return lax.ppermute(
        values, "slab", [(i, i + 1 if i % 2 else i - 1) for i in range(1, count - 1)]
    )


def shifted(values, step, axis):
    size = values.shape[axis]
    index = lax.broadcasted_iota(jnp.int32, values.shape, axis)
    edge = size - 1 if step > 0 else 0
    return jnp.where(index == edge, 0.0, pltpu.roll(values, (-step) % size, axis=axis))


def flow(center, half, faces):
    total = None
    for axis in (0, 1):
        flux = faces[axis] * (shifted(center, 1, axis) - center)
        index = lax.broadcasted_iota(jnp.int32, center.shape, axis)
        behind = jnp.where(index == 0, half * center, pltpu.roll(flux, 1, axis=axis))
        total = flux - behind if total is None else total + (flux - behind)
    return total


def by_side(odd, pairs):
    copies = [
        (
            [pltpu.make_async_copy(near, low, sems[0]), pltpu.make_async_copy(far, high, sems[1])],
            [pltpu.make_async_copy(near, high, sems[0]), pltpu.make_async_copy(far, low, sems[1])],
        )
        for near, far, low, high, sems in pairs
    ]

    @pl.when(odd)
    def _():
        for when_odd, _ in copies:
            for copy in when_odd:
                copy.start()

    @pl.when(jnp.logical_not(odd))
    def _():
        for _, when_even in copies:
            for copy in when_even:
                copy.start()

    return [copy for when_odd, _ in copies for copy in when_odd]


def diffuse(now, coefs, first, last):
    half = [0.5 * coef for coef in coefs]
    gaps = {p: half[p] + half[p + 1] for p in range(first - 1, last + 1)}
    faces = {
        p: [half[p] + shifted(half[p], 1, axis) for axis in (0, 1)] for p in range(first, last + 1)
    }
    later = []
    for field in now:
        rise = {p: gaps[p] * (field[p + 1] - field[p]) for p in gaps}
        later.append(
            [
                field[p]
                + diffusion_dt * (rise[p] - rise[p - 1] + flow(field[p], half[p], faces[p]))
                for p in range(first, last + 1)
            ]
        )
    return later


def force_kernel(
    place_ref,
    velocity_ref,
    images_ref,
    stiffness_ref,
    warped_ref,
    edge_near_ref,
    edge_far_ref,
    warped_near_ref,
    warped_far_ref,
    out_ref,
    near_ref,
    far_ref,
    fields,
    images,
    coefs,
    warped,
    sem,
):
    parts, planes = out_ref.shape[:2]
    odd = place_ref[0] == 1
    low, mid, high = pl.ds(0, 1), pl.ds(1, planes), pl.ds(planes + 1, 1)
    every = pl.ds(0, parts)
    waits = by_side(
        odd,
        [
            (
                warped_near_ref,
                warped_far_ref,
                warped.at[pl.ds(0, 2)],
                warped.at[pl.ds(planes + 2, 2)],
                (sem.at[0], sem.at[1]),
            ),
            (
                edge_near_ref.at[parts],
                edge_far_ref.at[parts],
                coefs.at[low],
                coefs.at[high],
                (sem.at[2], sem.at[3]),
            ),
            (
                edge_near_ref.at[parts + 1],
                edge_far_ref.at[parts + 1],
                images.at[low],
                images.at[high],
                (sem.at[4], sem.at[5]),
            ),
            (
                edge_near_ref.at[every],
                edge_far_ref.at[every],
                fields.at[:, low],
                fields.at[:, high],
                (sem.at[6], sem.at[7]),
            ),
        ],
    )
    own = [
        pltpu.make_async_copy(warped_ref, warped.at[pl.ds(2, planes)], sem.at[8]),
        pltpu.make_async_copy(stiffness_ref, coefs.at[mid], sem.at[9]),
        pltpu.make_async_copy(images_ref, images.at[mid], sem.at[10]),
        pltpu.make_async_copy(velocity_ref, fields.at[:, mid], sem.at[11]),
    ]
    for copy in own:
        copy.start()
    for copy in waits + own:
        copy.wait()
    now = [[] for _ in range(parts)]
    for p in range(planes + 2):
        here = warped[p + 1]
        mismatch = here - images[p]
        slopes = [
            0.5 * (shifted(here, 1, 1) - shifted(here, -1, 1)),
            0.5 * (shifted(here, 1, 0) - shifted(here, -1, 0)),
            0.5 * (warped[p + 2] - warped[p]),
        ]
        for a in range(parts):
            now[a].append(fields[a, p] - force_step * mismatch * slopes[a])
    later = diffuse(now, [coefs[p] for p in range(planes + 2)], 1, planes)
    for a in range(parts):
        for p in range(planes):
            out_ref[a, p] = later[a][p]
        near_ref[a, 0] = jnp.where(odd, later[a][0], later[a][-1])
        far_ref[a, 0] = jnp.where(odd, later[a][-1], later[a][0])


def last_kernel(
    place_ref,
    field_ref,
    stiffness_ref,
    edge_near_ref,
    edge_far_ref,
    near_ref,
    far_ref,
    out_ref,
    fields,
    coefs,
    sem,
):
    parts, planes = out_ref.shape[:2]
    low, mid, high = pl.ds(0, 1), pl.ds(1, planes), pl.ds(planes + 1, 1)
    waits = by_side(
        place_ref[0] == 1,
        [
            (near_ref, far_ref, fields.at[:, low], fields.at[:, high], (sem.at[0], sem.at[1])),
            (
                edge_near_ref.at[parts],
                edge_far_ref.at[parts],
                coefs.at[low],
                coefs.at[high],
                (sem.at[2], sem.at[3]),
            ),
        ],
    )
    own = [
        pltpu.make_async_copy(field_ref, fields.at[:, mid], sem.at[4]),
        pltpu.make_async_copy(stiffness_ref, coefs.at[mid], sem.at[5]),
    ]
    for copy in own:
        copy.start()
    for copy in waits + own:
        copy.wait()
    now = [[fields[a, p] for p in range(planes + 2)] for a in range(parts)]
    later = diffuse(now, [coefs[p] for p in range(planes + 2)], 1, planes)
    for a in range(parts):
        for p in range(planes):
            out_ref[a, p] = later[a][p]


def per_device(template, images, velocity, stiffness, send_rows, ref_slot, columns, weights):
    f32, bf16 = jnp.float32, jnp.bfloat16
    shape = jax.ShapeDtypeStruct
    slabs = lax.axis_size("slab")
    subjects = lax.axis_size("subj")
    me = lax.axis_index("subj").astype(jnp.int32).reshape(1)
    slab = lax.axis_index("slab")
    odd = slab % 2 == 1
    place = odd.astype(jnp.int32).reshape(1)
    capacity = send_rows.shape[3]
    rows, width = template.shape
    planes = rows // YR
    parts = velocity.shape[1]
    each = ref_slot.shape[2]
    terms = rows * each
    slots = slabs * capacity
    grid = (planes, YR, width)
    velocity_grid = velocity[0].reshape((parts,) + grid)
    images_grid = images[0].reshape(grid)
    coef_grid = stiffness.reshape(grid)
    dma = pltpu.SemaphoreType.DMA

    sending = call(
        send_kernel,
        shape((slots, width), f32),
        send_rows[0, 0],
        template,
        far=(0, 1),
        scratch=(pltpu.VMEM((slabs, capacity), jnp.int32), pltpu.VMEM((rows, width), f32), dma((2,))),
    )
    received = lax.all_to_all(sending, "slab", split_axis=0, concat_axis=0, tiled=True)

    chunks = 4
    moved_shape = (chunks, each, len(OFFSETS), rows // chunks, width)
    edge_shape = (parts + 2, 1, YR, width)
    moved, edge_near, edge_far = call(
        prepare_kernel,
        (shape(moved_shape, bf16), shape(edge_shape, f32), shape(edge_shape, f32)),
        place,
        columns.reshape(terms, width),
        weights.reshape(terms, width),
        velocity_grid,
        coef_grid,
        images_grid,
        smem=(0,),
        far=(1, 2, 3, 4, 5),
        out_far=(0, 1, 2),
        scratch=(
            pltpu.VMEM((terms, width), jnp.int32),
            pltpu.VMEM((terms, width), bf16),
            pltpu.VMEM((terms // chunks, width), f32),
            pltpu.VMEM(moved_shape, bf16),
            pltpu.VMEM((parts + 2,) + grid, f32),
            dma((2 * chunks,)),
            dma((chunks + 2,)),
            dma((3,)),
        ),
    )
    edge_far, edge_near = swap_far(edge_far), swap_near(edge_near)

    warped, sent = call(
        functools.partial(warp_kernel, slabs, subjects),
        (shape((rows, width), f32), shape((slots, width), f32)),
        ref_slot[0].T,
        received,
        moved,
        images[0],
        far=(1, 2, 3),
        cost=COST,
        scratch=(
            pltpu.VMEM((slots, width), f32),
            pltpu.VMEM((rows, width), f32),
            pltpu.VMEM(moved_shape, bf16),
            pltpu.VMEM((each, rows, width), f32),
            pltpu.VMEM((each, rows, 2 * width), bf16),
            dma((2,)),
            dma((chunks,)),
        ),
    )
    sent, edge_far, edge_near = lax.optimization_barrier((sent, edge_far, edge_near))
    returned = lax.all_to_all(sent, ("subj", "slab"), split_axis=0, concat_axis=0, tiled=True)

    own_rows, warped = lax.optimization_barrier((send_rows[0, 0], warped))
    warped_grid = warped.reshape(grid)
    warped_far, warped_near = swap_far(warped_grid), swap_near(warped_grid)
    all_rows = over_subjects(own_rows)

    field, field_near, field_far = call(
        force_kernel,
        (
            shape((parts,) + grid, f32),
            shape((parts, 1, YR, width), f32),
            shape((parts, 1, YR, width), f32),
        ),
        place,
        velocity_grid,
        images_grid,
        coef_grid,
        warped_grid,
        edge_near,
        edge_far,
        warped_near,
        warped_far,
        smem=(0,),
        far=tuple(range(1, 9)),
        cost=COST,
        scratch=(
            pltpu.VMEM((parts, planes + 2, YR, width), f32),
            pltpu.VMEM((planes + 2, YR, width), f32),
            pltpu.VMEM((planes + 2, YR, width), f32),
            pltpu.VMEM((planes + 4, YR, width), f32),
            dma((12,)),
        ),
    )
    field_far, field_near = swap_far(field_far), swap_near(field_near)

    part = call(
        functools.partial(collect_kernel, subjects),
        shape((rows // subjects, width), f32),
        me,
        returned,
        *all_rows,
        smem=(0,),
    )
    pieces = over_subjects(part)
    template_out = call(
        functools.partial(update_kernel, subjects),
        shape((rows, width), f32),
        me,
        template,
        *pieces,
        smem=(0,),
    )
    field = call(
        last_kernel,
        shape((parts,) + grid, f32),
        place,
        field,
        coef_grid,
        edge_near,
        edge_far,
        field_near,
        field_far,
        smem=(0,),
        far=tuple(range(1, 7)),
        scratch=(
            pltpu.VMEM((parts, planes + 2, YR, width), f32),
            pltpu.VMEM((planes + 2, YR, width), f32),
            dma((6,)),
        ),
    )
    velocity_out = field.reshape(parts, rows, width)[None]
    return (template_out, velocity_out)


def solution(mesh):
    return jax.shard_map(
        per_device,
        mesh=mesh,
        in_specs=(
            P("slab", None),
            P("subj", "slab", None),
            P("subj", None, "slab", None),
            P("slab", None),
            P("subj", "slab", None, None),
            P("subj", "slab", None),
            P("subj", "slab", None, None),
            P("subj", "slab", None, None),
        ),
        out_specs=(P("slab", None), P("subj", None, "slab", None)),
        check_vma=False,
    )
```

```python
import functools

import jax
import jax.numpy as jnp
from jax import lax
from jax.experimental import pallas as pl
from jax.experimental.pallas import tpu as pltpu
from jax.sharding import PartitionSpec as P

YR = 256
LANES = 128
OFFSETS = (0, -2, -1, 1, 2)


force_step = 1.0
diffusion_dt = 0.16
template_rate = 2.0

VMEM_LIMIT = 40 * 1024 * 1024


def call(kernel, out_shape, *args, scratch=(), smem=(), far=(), free=(), out_far=()):
    many = isinstance(out_shape, tuple)
    shapes = [
        pltpu.HBM(s.shape, s.dtype) if i in out_far else s
        for i, s in enumerate(out_shape if many else (out_shape,))
    ]
    spaces = [pltpu.HBM if i in out_far else pltpu.VMEM for i in range(len(shapes))]
    specs = [pl.BlockSpec(memory_space=space) for space in spaces]
    return pl.pallas_call(
        kernel,
        out_shape=tuple(shapes) if many else shapes[0],
        in_specs=[
            pl.BlockSpec(
                memory_space=(
                    pltpu.SMEM
                    if i in smem
                    else pltpu.HBM
                    if i in far
                    else pl.ANY
                    if i in free
                    else pltpu.VMEM
                )
            )
            for i in range(len(args))
        ],
        out_specs=tuple(specs) if many else specs[0],
        scratch_shapes=scratch,
        compiler_params=pltpu.CompilerParams(vmem_limit_bytes=VMEM_LIMIT),
    )(
        *[
            pltpu.with_memory_space_constraint(arg, pltpu.HBM) if i in far else arg
            for i, arg in enumerate(args)
        ]
    )


def halves(values):
    high = values.astype(jnp.bfloat16)
    low = (values - high.astype(jnp.float32)).astype(jnp.bfloat16)
    return jnp.concatenate([high, low], axis=1)


def joined(pair):
    width = pair.shape[1] // 2
    return pair[:, :width] + pair[:, width:]


def turned(values, shift):
    shift %= values.shape[1]
    return pltpu.roll(values, shift, axis=1) if shift else values


def dot(left, right):
    return jnp.dot(left, right, preferred_element_type=jnp.float32)


def one_hot(matches):
    return jnp.where(matches, 1.0, 0.0).astype(jnp.bfloat16)


def send_kernel(send_ref, template_ref, out_ref, send, template, sem):
    slabs, capacity = send.shape
    rows = template.shape[0]
    copies = [
        pltpu.make_async_copy(send_ref, send, sem.at[0]),
        pltpu.make_async_copy(template_ref, template, sem.at[1]),
    ]
    for copy in copies:
        copy.start()
    copies[0].wait()
    padded = jnp.concatenate([send[...], jnp.zeros((slabs, LANES - capacity), jnp.int32)], axis=1)
    columns = padded.T
    number = lax.broadcasted_iota(jnp.int32, (capacity, rows), 1)
    chosen = [
        one_hot(jnp.broadcast_to(columns[:capacity, k : k + 1], (capacity, rows)) == number)
        for k in range(slabs)
    ]
    copies[1].wait()
    pair = halves(template[...])
    for k in range(slabs):
        out_ref[k * capacity : (k + 1) * capacity, :] = joined(dot(chosen[k], pair))


def prepare_kernel(
    place_ref,
    columns_ref,
    weights_ref,
    velocity_ref,
    stiffness_ref,
    images_ref,
    moved_ref,
    near_ref,
    far_ref,
    columns,
    weights,
    plain,
    moved,
    edge,
    in_sem,
    out_sem,
    edge_sem,
):
    chunks, each, count, some, width = moved.shape
    odd = place_ref[0]
    near_plane, far_plane = pl.ds((edge.shape[1] - 1) * (1 - odd), 1), pl.ds((edge.shape[1] - 1) * odd, 1)
    step = some * each
    parts = velocity_ref.shape[0]
    reads = [
        (
            pltpu.make_async_copy(
                columns_ref.at[pl.ds(i * step, step)], columns.at[pl.ds(i * step, step)], in_sem.at[i]
            ),
            pltpu.make_async_copy(
                weights_ref.at[pl.ds(i * step, step)],
                weights.at[pl.ds(i * step, step)],
                in_sem.at[chunks + i],
            ),
        )
        for i in range(chunks)
    ]
    edges = [
        pltpu.make_async_copy(velocity_ref, edge.at[pl.ds(0, parts)], edge_sem.at[0]),
        pltpu.make_async_copy(stiffness_ref, edge.at[parts], edge_sem.at[1]),
        pltpu.make_async_copy(images_ref, edge.at[parts + 1], edge_sem.at[2]),
    ]
    writes = [
        pltpu.make_async_copy(moved.at[i], moved_ref.at[i], out_sem.at[i]) for i in range(chunks)
    ] + [
        pltpu.make_async_copy(edge.at[:, near_plane], near_ref, out_sem.at[chunks]),
        pltpu.make_async_copy(edge.at[:, far_plane], far_ref, out_sem.at[chunks + 1]),
    ]
    for copy in reads[0]:
        copy.start()
    for copy in edges:
        copy.start()
    for pair in reads[1:]:
        for copy in pair:
            copy.start()
    cell = lax.broadcasted_iota(jnp.int32, (some, width), 1)
    for i in range(chunks):
        at = i * step
        for copy in reads[i]:
            copy.wait()
        plain[...] = weights[at : at + step, :].astype(jnp.float32)
        for b in range(each):
            offset = columns[pl.ds(at + b, some, stride=each), :] - cell
            here = plain[pl.ds(b, some, stride=each), :]
            for j, o in enumerate(OFFSETS):
                kept = jnp.where(offset == o, here, 0.0)
                moved[i, b, j] = turned(kept, o).astype(jnp.bfloat16)
        writes[i].start()
        if i == 0:
            for copy in edges:
                copy.wait()
            for copy in writes[chunks:]:
                copy.start()
    for copy in writes:
        copy.wait()


def warp_kernel(
    slabs,
    subjects,
    slot_ref,
    received_ref,
    moved_ref,
    images_ref,
    warped_ref,
    sent_ref,
    images,
    moved,
    picked,
    placed,
    first_sem,
    moved_sem,
):
    slots, width = received_ref.shape
    chunks, each, count, some = moved.shape[:4]
    rows = chunks * some
    block = width // subjects
    group = slots // subjects
    capacity = slots // slabs
    held = capacity // subjects
    first = pltpu.make_async_copy(images_ref, images, first_sem)
    moves = [
        pltpu.make_async_copy(moved_ref.at[i], moved.at[i], moved_sem.at[i]) for i in range(chunks)
    ]
    for copy in moves[:1] + [first] + moves[1:]:
        copy.start()
    slot = slot_ref[...]
    slot_wide = jnp.concatenate([slot, jnp.zeros((LANES - each, rows), jnp.int32)], axis=0).T
    inner = slot % capacity
    packed = (inner // held) * group + (slot // capacity) * held + inner % held
    lane = lax.broadcasted_iota(jnp.int32, (rows, LANES), 1)
    number = lax.broadcasted_iota(jnp.int32, (slots, rows), 0)
    pair = halves(received_ref[...])
    for b in range(each):
        wide = jnp.broadcast_to(slot_wide[:, b : b + 1], (rows, LANES))
        pick = jnp.concatenate(
            [one_hot(wide == lane + t * LANES) for t in range(slots // LANES)], axis=1
        )
        picked[b] = joined(dot(pick, pair))
    first.wait()
    for i in range(chunks):
        moves[i].wait()
        at = slice(i * some, (i + 1) * some)
        sums = [jnp.zeros((some, width), jnp.float32) for _ in OFFSETS]
        for b in range(each):
            values = picked[b, at, :]
            for j in range(count):
                sums[j] = sums[j] + moved[i, b, j].astype(jnp.float32) * values
        warped = sums[0]
        for j, o in enumerate(OFFSETS[1:], 1):
            warped = warped + turned(sums[j], -o)
        warped_ref[at, :] = warped
        mismatch = warped - images[at, :]
        ahead = [turned(mismatch, o) for o in OFFSETS]
        for b in range(each):
            total = moved[i, b, 0].astype(jnp.float32) * ahead[0]
            for j in range(1, count):
                total = total + moved[i, b, j].astype(jnp.float32) * ahead[j]
            placed[b, at, :] = halves(total)
    total = jnp.zeros((slots, 2 * width), jnp.float32)
    for b in range(each):
        drop = one_hot(jnp.broadcast_to(packed[b : b + 1], (slots, rows)) == number)
        total = total + dot(drop, placed[b])
    total = joined(total)
    place = lax.broadcasted_iota(jnp.int32, (group, width), 1) // block
    groups = [total[q * group : (q + 1) * group, :] for q in range(subjects)]
    for p in range(subjects):
        out = jnp.zeros((group, width), jnp.float32)
        for q in range(subjects):
            out = jnp.where(place == q, turned(groups[q], (q - p) * block), out)
        sent_ref[p * group : (p + 1) * group, :] = out


def collect_kernel(subjects, me_ref, returned_ref, *refs):
    row_refs, out_ref = refs[:-1], refs[-1]
    slots, width = returned_ref.shape
    slabs, capacity = row_refs[0].shape
    rows = out_ref.shape[0] * subjects
    block = width // subjects
    group = slots // subjects
    held = capacity // subjects
    me = me_ref[0]
    pair = halves(
        jnp.concatenate(
            [
                returned_ref[pl.ds(pl.multiple_of((me ^ d) * group, group), group), :]
                for d in range(subjects)
            ]
        )
    )
    lane = lax.broadcasted_iota(jnp.int32, (slabs, LANES), 1)
    slab = lax.broadcasted_iota(jnp.int32, (slabs, LANES), 0)
    fill = jnp.zeros((slabs, LANES - capacity), jnp.int32)
    wanted = []
    for q in range(subjects):
        chunks = [jnp.zeros((1, LANES), jnp.int32) for _ in range(slots // LANES)]
        for d in range(subjects):
            spread = jnp.concatenate([row_refs[d][...], fill], axis=1)
            spread = turned(spread, d * group - q * held)
            spread = pltpu.roll(spread, 0, axis=1, stride=held, stride_axis=0)
            first = (d * group) % LANES + slab * held
            kept = jnp.where((lane >= first) & (lane < first + held), spread, 0)
            chunks[d * group // LANES] += jnp.sum(kept, axis=0, keepdims=True)
        wanted.append(jnp.concatenate(chunks, axis=1))
    number = lax.broadcasted_iota(jnp.int32, (rows, slots), 0)
    place = lax.broadcasted_iota(jnp.int32, (rows, width), 1) // block
    kept = jnp.zeros((rows, width), jnp.float32)
    for q in range(subjects):
        match = jnp.broadcast_to(wanted[q], (rows, slots)) == number
        kept = jnp.where(place == q, joined(dot(one_hot(match), pair)), kept)
    turn = block
    while turn < width:
        kept = kept + turned(kept, turn)
        turn *= 2
    part = rows // subjects
    out = jnp.zeros((part, width), jnp.float32)
    for p in range(subjects):
        out = jnp.where(place[:part] == p, kept[p * part : (p + 1) * part], out)
    out_ref[...] = out


def update_kernel(subjects, me_ref, template_ref, *refs):
    parts, out_ref = refs[:-1], refs[-1]
    rows, width = template_ref.shape
    block = width // subjects
    part = rows // subjects
    me = me_ref[0]
    place = lax.broadcasted_iota(jnp.int32, (part, width), 1) // block
    for p in range(subjects):
        total = jnp.zeros((part, width), jnp.float32)
        for d in range(subjects):
            source = me ^ d
            turn = lax.rem((source - p) * block + width, width)
            total = jnp.where(place == source, pltpu.roll(parts[d][...], turn, axis=1), total)
        at = slice(p * part, (p + 1) * part)
        out_ref[at, :] = template_ref[at, :] - template_rate * total / subjects


def over_subjects(values):
    count = lax.axis_size("subj")
    return [values] + [
        lax.ppermute(values, "subj", [(i, i ^ d) for i in range(count)]) for d in range(1, count)
    ]


def swap_near(values):
    return lax.ppermute(values, "slab", [(i, i ^ 1) for i in range(lax.axis_size("slab"))])


def swap_far(values):
    count = lax.axis_size("slab")
    return lax.ppermute(
        values, "slab", [(i, i + 1 if i % 2 else i - 1) for i in range(1, count - 1)]
    )


def shifted(values, step, axis):
    size = values.shape[axis]
    index = lax.broadcasted_iota(jnp.int32, values.shape, axis)
    edge = size - 1 if step > 0 else 0
    return jnp.where(index == edge, 0.0, pltpu.roll(values, (-step) % size, axis=axis))


def flow(center, half, faces):
    total = None
    for axis in (0, 1):
        flux = faces[axis] * (shifted(center, 1, axis) - center)
        index = lax.broadcasted_iota(jnp.int32, center.shape, axis)
        behind = jnp.where(index == 0, half * center, pltpu.roll(flux, 1, axis=axis))
        total = flux - behind if total is None else total + (flux - behind)
    return total


def by_side(odd, pairs):
    copies = [
        (
            [pltpu.make_async_copy(near, low, sems[0]), pltpu.make_async_copy(far, high, sems[1])],
            [pltpu.make_async_copy(near, high, sems[0]), pltpu.make_async_copy(far, low, sems[1])],
        )
        for near, far, low, high, sems in pairs
    ]

    @pl.when(odd)
    def _():
        for when_odd, _ in copies:
            for copy in when_odd:
                copy.start()

    @pl.when(jnp.logical_not(odd))
    def _():
        for _, when_even in copies:
            for copy in when_even:
                copy.start()

    return [copy for when_odd, _ in copies for copy in when_odd]


def diffuse(now, coefs, first, last):
    half = [0.5 * coef for coef in coefs]
    gaps = {p: half[p] + half[p + 1] for p in range(first - 1, last + 1)}
    faces = {
        p: [half[p] + shifted(half[p], 1, axis) for axis in (0, 1)] for p in range(first, last + 1)
    }
    later = []
    for field in now:
        rise = {p: gaps[p] * (field[p + 1] - field[p]) for p in gaps}
        later.append(
            [
                field[p]
                + diffusion_dt * (rise[p] - rise[p - 1] + flow(field[p], half[p], faces[p]))
                for p in range(first, last + 1)
            ]
        )
    return later


def force_kernel(
    place_ref,
    velocity_ref,
    images_ref,
    stiffness_ref,
    warped_ref,
    edge_near_ref,
    edge_far_ref,
    warped_near_ref,
    warped_far_ref,
    out_ref,
    near_ref,
    far_ref,
    fields,
    images,
    coefs,
    warped,
    sem,
):
    parts, planes = out_ref.shape[:2]
    odd = place_ref[0] == 1
    low, mid, high = pl.ds(0, 1), pl.ds(1, planes), pl.ds(planes + 1, 1)
    every = pl.ds(0, parts)
    waits = by_side(
        odd,
        [
            (
                warped_near_ref,
                warped_far_ref,
                warped.at[pl.ds(0, 2)],
                warped.at[pl.ds(planes + 2, 2)],
                (sem.at[0], sem.at[1]),
            ),
            (
                edge_near_ref.at[parts],
                edge_far_ref.at[parts],
                coefs.at[low],
                coefs.at[high],
                (sem.at[2], sem.at[3]),
            ),
            (
                edge_near_ref.at[parts + 1],
                edge_far_ref.at[parts + 1],
                images.at[low],
                images.at[high],
                (sem.at[4], sem.at[5]),
            ),
            (
                edge_near_ref.at[every],
                edge_far_ref.at[every],
                fields.at[:, low],
                fields.at[:, high],
                (sem.at[6], sem.at[7]),
            ),
        ],
    )
    own = [
        pltpu.make_async_copy(warped_ref, warped.at[pl.ds(2, planes)], sem.at[8]),
        pltpu.make_async_copy(stiffness_ref, coefs.at[mid], sem.at[9]),
        pltpu.make_async_copy(images_ref, images.at[mid], sem.at[10]),
        pltpu.make_async_copy(velocity_ref, fields.at[:, mid], sem.at[11]),
    ]
    for copy in own:
        copy.start()
    for copy in waits + own:
        copy.wait()
    now = [[] for _ in range(parts)]
    for p in range(planes + 2):
        here = warped[p + 1]
        mismatch = here - images[p]
        slopes = [
            0.5 * (shifted(here, 1, 1) - shifted(here, -1, 1)),
            0.5 * (shifted(here, 1, 0) - shifted(here, -1, 0)),
            0.5 * (warped[p + 2] - warped[p]),
        ]
        for a in range(parts):
            now[a].append(fields[a, p] - force_step * mismatch * slopes[a])
    later = diffuse(now, [coefs[p] for p in range(planes + 2)], 1, planes)
    for a in range(parts):
        for p in range(planes):
            out_ref[a, p] = later[a][p]
        near_ref[a, 0] = jnp.where(odd, later[a][0], later[a][-1])
        far_ref[a, 0] = jnp.where(odd, later[a][-1], later[a][0])


def last_kernel(
    place_ref,
    field_ref,
    stiffness_ref,
    edge_near_ref,
    edge_far_ref,
    near_ref,
    far_ref,
    out_ref,
    fields,
    coefs,
    sem,
):
    parts, planes = out_ref.shape[:2]
    low, mid, high = pl.ds(0, 1), pl.ds(1, planes), pl.ds(planes + 1, 1)
    waits = by_side(
        place_ref[0] == 1,
        [
            (near_ref, far_ref, fields.at[:, low], fields.at[:, high], (sem.at[0], sem.at[1])),
            (
                edge_near_ref.at[parts],
                edge_far_ref.at[parts],
                coefs.at[low],
                coefs.at[high],
                (sem.at[2], sem.at[3]),
            ),
        ],
    )
    own = [
        pltpu.make_async_copy(field_ref, fields.at[:, mid], sem.at[4]),
        pltpu.make_async_copy(stiffness_ref, coefs.at[mid], sem.at[5]),
    ]
    for copy in own:
        copy.start()
    for copy in waits + own:
        copy.wait()
    now = [[fields[a, p] for p in range(planes + 2)] for a in range(parts)]
    later = diffuse(now, [coefs[p] for p in range(planes + 2)], 1, planes)
    for a in range(parts):
        for p in range(planes):
            out_ref[a, p] = later[a][p]


def per_device(template, images, velocity, stiffness, send_rows, ref_slot, columns, weights):
    f32, bf16 = jnp.float32, jnp.bfloat16
    shape = jax.ShapeDtypeStruct
    slabs = lax.axis_size("slab")
    subjects = lax.axis_size("subj")
    me = lax.axis_index("subj").astype(jnp.int32).reshape(1)
    slab = lax.axis_index("slab")
    odd = slab % 2 == 1
    place = odd.astype(jnp.int32).reshape(1)
    capacity = send_rows.shape[3]
    rows, width = template.shape
    planes = rows // YR
    parts = velocity.shape[1]
    each = ref_slot.shape[2]
    terms = rows * each
    slots = slabs * capacity
    grid = (planes, YR, width)
    velocity_grid = velocity[0].reshape((parts,) + grid)
    images_grid = images[0].reshape(grid)
    coef_grid = stiffness.reshape(grid)
    dma = pltpu.SemaphoreType.DMA

    sending = call(
        send_kernel,
        shape((slots, width), f32),
        send_rows[0, 0],
        template,
        far=(0, 1),
        scratch=(pltpu.VMEM((slabs, capacity), jnp.int32), pltpu.VMEM((rows, width), f32), dma((2,))),
    )
    received = lax.all_to_all(sending, "slab", split_axis=0, concat_axis=0, tiled=True)

    chunks = 4
    moved_shape = (chunks, each, len(OFFSETS), rows // chunks, width)
    edge_shape = (parts + 2, 1, YR, width)
    moved, edge_near, edge_far = call(
        prepare_kernel,
        (shape(moved_shape, bf16), shape(edge_shape, f32), shape(edge_shape, f32)),
        place,
        columns.reshape(terms, width),
        weights.reshape(terms, width),
        velocity_grid,
        coef_grid,
        images_grid,
        smem=(0,),
        far=(1, 2, 3, 4, 5),
        out_far=(0, 1, 2),
        scratch=(
            pltpu.VMEM((terms, width), jnp.int32),
            pltpu.VMEM((terms, width), bf16),
            pltpu.VMEM((terms // chunks, width), f32),
            pltpu.VMEM(moved_shape, bf16),
            pltpu.VMEM((parts + 2,) + grid, f32),
            dma((2 * chunks,)),
            dma((chunks + 2,)),
            dma((3,)),
        ),
    )
    received, edge_far, edge_near = lax.optimization_barrier((received, edge_far, edge_near))
    edge_far, edge_near = swap_far(edge_far), swap_near(edge_near)

    warped, sent = call(
        functools.partial(warp_kernel, slabs, subjects),
        (shape((rows, width), f32), shape((slots, width), f32)),
        ref_slot[0].T,
        received,
        moved,
        images[0],
        far=(2, 3),
        scratch=(
            pltpu.VMEM((rows, width), f32),
            pltpu.VMEM(moved_shape, bf16),
            pltpu.VMEM((each, rows, width), f32),
            pltpu.VMEM((each, rows, 2 * width), bf16),
            dma,
            dma((chunks,)),
        ),
    )
    sent, edge_far, edge_near = lax.optimization_barrier((sent, edge_far, edge_near))
    returned = lax.all_to_all(sent, ("subj", "slab"), split_axis=0, concat_axis=0, tiled=True)

    own_rows, warped = lax.optimization_barrier((send_rows[0, 0], warped))
    warped_grid = warped.reshape(grid)
    warped_far, warped_near = swap_far(warped_grid), swap_near(warped_grid)
    all_rows = over_subjects(own_rows)

    field, field_near, field_far = call(
        force_kernel,
        (
            shape((parts,) + grid, f32),
            shape((parts, 1, YR, width), f32),
            shape((parts, 1, YR, width), f32),
        ),
        place,
        velocity_grid,
        images_grid,
        coef_grid,
        warped_grid,
        edge_near,
        edge_far,
        warped_near,
        warped_far,
        smem=(0,),
        far=(1, 2, 3),
        free=(4, 5, 6, 7, 8),
        scratch=(
            pltpu.VMEM((parts, planes + 2, YR, width), f32),
            pltpu.VMEM((planes + 2, YR, width), f32),
            pltpu.VMEM((planes + 2, YR, width), f32),
            pltpu.VMEM((planes + 4, YR, width), f32),
            dma((12,)),
        ),
    )
    field_far, field_near = swap_far(field_far), swap_near(field_near)

    part = call(
        functools.partial(collect_kernel, subjects),
        shape((rows // subjects, width), f32),
        me,
        returned,
        *all_rows,
        smem=(0,),
    )
    pieces = over_subjects(part)
    template_out = call(
        functools.partial(update_kernel, subjects),
        shape((rows, width), f32),
        me,
        template,
        *pieces,
        smem=(0,),
    )
    field = call(
        last_kernel,
        shape((parts,) + grid, f32),
        place,
        field,
        coef_grid,
        edge_near,
        edge_far,
        field_near,
        field_far,
        smem=(0,),
        far=(2,),
        free=(1, 3, 4, 5, 6),
        scratch=(
            pltpu.VMEM((parts, planes + 2, YR, width), f32),
            pltpu.VMEM((planes + 2, YR, width), f32),
            dma((6,)),
        ),
    )
    velocity_out = field.reshape(parts, rows, width)[None]
    return (template_out, velocity_out)


def solution(mesh):
    return jax.shard_map(
        per_device,
        mesh=mesh,
        in_specs=(
            P("slab", None),
            P("subj", "slab", None),
            P("subj", None, "slab", None),
            P("slab", None),
            P("subj", "slab", None, None),
            P("subj", "slab", None),
            P("subj", "slab", None, None),
            P("subj", "slab", None, None),
        ),
        out_specs=(P("slab", None), P("subj", None, "slab", None)),
        check_vma=False,
    )
```

```python
import functools

import jax
import jax.numpy as jnp
from jax import lax
from jax.experimental import pallas as pl
from jax.experimental.pallas import tpu as pltpu
from jax.sharding import PartitionSpec as P

YR = 256
LANES = 128
PAD = 8
OFFSETS = (0, -2, -1, 1, 2)


force_step = 1.0
diffusion_dt = 0.16
template_rate = 2.0

VMEM_LIMIT = 40 * 1024 * 1024


def call(kernel, out_shape, *args, scratch=(), smem=(), far=(), out_far=()):
    many = isinstance(out_shape, tuple)
    shapes = [
        pltpu.HBM(s.shape, s.dtype) if i in out_far else s
        for i, s in enumerate(out_shape if many else (out_shape,))
    ]
    spaces = [pltpu.HBM if i in out_far else pltpu.VMEM for i in range(len(shapes))]
    specs = [pl.BlockSpec(memory_space=space) for space in spaces]
    return pl.pallas_call(
        kernel,
        out_shape=tuple(shapes) if many else shapes[0],
        in_specs=[
            pl.BlockSpec(
                memory_space=pltpu.SMEM if i in smem else pltpu.HBM if i in far else pltpu.VMEM
            )
            for i in range(len(args))
        ],
        out_specs=tuple(specs) if many else specs[0],
        scratch_shapes=scratch,
        compiler_params=pltpu.CompilerParams(vmem_limit_bytes=VMEM_LIMIT),
    )(
        *[
            pltpu.with_memory_space_constraint(arg, pltpu.HBM) if i in far else arg
            for i, arg in enumerate(args)
        ]
    )


def halves(values):
    high = values.astype(jnp.bfloat16)
    low = (values - high.astype(jnp.float32)).astype(jnp.bfloat16)
    return jnp.concatenate([high, low], axis=1)


def joined(pair):
    width = pair.shape[1] // 2
    return pair[:, :width] + pair[:, width:]


def turned(values, shift):
    shift %= values.shape[1]
    return pltpu.roll(values, shift, axis=1) if shift else values


def dot(left, right):
    return jnp.dot(left, right, preferred_element_type=jnp.float32)


def one_hot(matches):
    return jnp.where(matches, 1.0, 0.0).astype(jnp.bfloat16)


def send_kernel(send_ref, template_ref, out_ref, send, template, sem):
    slabs, capacity = send.shape
    rows = template.shape[0]
    copies = [
        pltpu.make_async_copy(send_ref, send, sem.at[0]),
        pltpu.make_async_copy(template_ref, template, sem.at[1]),
    ]
    for copy in copies:
        copy.start()
    copies[0].wait()
    padded = jnp.concatenate([send[...], jnp.zeros((slabs, LANES - capacity), jnp.int32)], axis=1)
    columns = padded.T
    number = lax.broadcasted_iota(jnp.int32, (capacity, rows), 1)
    chosen = [
        one_hot(jnp.broadcast_to(columns[:capacity, k : k + 1], (capacity, rows)) == number)
        for k in range(slabs)
    ]
    copies[1].wait()
    pair = halves(template[...])
    for k in range(slabs):
        out_ref[k * capacity : (k + 1) * capacity, :] = joined(dot(chosen[k], pair))


def prepare_kernel(
    place_ref,
    columns_ref,
    weights_ref,
    velocity_ref,
    stiffness_ref,
    images_ref,
    moved_ref,
    near_ref,
    far_ref,
    columns,
    weights,
    plain,
    moved,
    edge,
    in_sem,
    out_sem,
    edge_sem,
):
    chunks, each, count, some, width = moved.shape
    odd = place_ref[0]
    near_plane, far_plane = pl.ds((edge.shape[1] - 1) * (1 - odd), 1), pl.ds((edge.shape[1] - 1) * odd, 1)
    step = some * each
    parts = velocity_ref.shape[0]
    reads = [
        (
            pltpu.make_async_copy(
                columns_ref.at[pl.ds(i * step, step)], columns.at[pl.ds(i * step, step)], in_sem.at[i]
            ),
            pltpu.make_async_copy(
                weights_ref.at[pl.ds(i * step, step)],
                weights.at[pl.ds(i * step, step)],
                in_sem.at[chunks + i],
            ),
        )
        for i in range(chunks)
    ]
    edges = [
        pltpu.make_async_copy(velocity_ref, edge.at[pl.ds(0, parts)], edge_sem.at[0]),
        pltpu.make_async_copy(stiffness_ref, edge.at[parts], edge_sem.at[1]),
        pltpu.make_async_copy(images_ref, edge.at[parts + 1], edge_sem.at[2]),
    ]
    writes = [
        pltpu.make_async_copy(moved.at[i], moved_ref.at[i], out_sem.at[i]) for i in range(chunks)
    ] + [
        pltpu.make_async_copy(edge.at[:, near_plane], near_ref, out_sem.at[chunks]),
        pltpu.make_async_copy(edge.at[:, far_plane], far_ref, out_sem.at[chunks + 1]),
    ]
    for copy in reads[0]:
        copy.start()
    for copy in edges:
        copy.start()
    for pair in reads[1:]:
        for copy in pair:
            copy.start()
    cell = lax.broadcasted_iota(jnp.int32, (some, width), 1)
    for i in range(chunks):
        at = i * step
        for copy in reads[i]:
            copy.wait()
        plain[...] = weights[at : at + step, :].astype(jnp.float32)
        for b in range(each):
            offset = columns[pl.ds(at + b, some, stride=each), :] - cell
            here = plain[pl.ds(b, some, stride=each), :]
            for j, o in enumerate(OFFSETS):
                kept = jnp.where(offset == o, here, 0.0)
                moved[i, b, j] = turned(kept, o).astype(jnp.bfloat16)
        writes[i].start()
        if i == 0:
            for copy in edges:
                copy.wait()
            for copy in writes[chunks:]:
                copy.start()
    for copy in writes:
        copy.wait()


def warp_kernel(
    slabs,
    subjects,
    slot_ref,
    received_ref,
    moved_ref,
    images_ref,
    warped_ref,
    sent_ref,
    images,
    moved,
    picked,
    placed,
    first_sem,
    moved_sem,
):
    slots, width = received_ref.shape
    chunks, each, count, some = moved.shape[:4]
    rows = chunks * some
    block = width // subjects
    group = slots // subjects
    capacity = slots // slabs
    held = capacity // subjects
    first = pltpu.make_async_copy(images_ref, images, first_sem)
    moves = [
        pltpu.make_async_copy(moved_ref.at[i], moved.at[i], moved_sem.at[i]) for i in range(chunks)
    ]
    for copy in moves[:1] + [first] + moves[1:]:
        copy.start()
    slot = slot_ref[...]
    slot_wide = jnp.concatenate([slot, jnp.zeros((LANES - each, rows), jnp.int32)], axis=0).T
    inner = slot % capacity
    packed = (inner // held) * group + (slot // capacity) * held + inner % held
    lane = lax.broadcasted_iota(jnp.int32, (rows, LANES), 1)
    number = lax.broadcasted_iota(jnp.int32, (slots, rows), 0)
    pair = halves(received_ref[...])
    for b in range(each):
        wide = jnp.broadcast_to(slot_wide[:, b : b + 1], (rows, LANES))
        pick = jnp.concatenate(
            [one_hot(wide == lane + t * LANES) for t in range(slots // LANES)], axis=1
        )
        picked[b] = joined(dot(pick, pair))
    first.wait()
    for i in range(chunks):
        moves[i].wait()
        at = slice(i * some, (i + 1) * some)
        sums = [jnp.zeros((some, width), jnp.float32) for _ in OFFSETS]
        for b in range(each):
            values = picked[b, at, :]
            for j in range(count):
                sums[j] = sums[j] + moved[i, b, j].astype(jnp.float32) * values
        warped = sums[0]
        for j, o in enumerate(OFFSETS[1:], 1):
            warped = warped + turned(sums[j], -o)
        warped_ref[at, :] = warped
        mismatch = warped - images[at, :]
        ahead = [turned(mismatch, o) for o in OFFSETS]
        for b in range(each):
            total = moved[i, b, 0].astype(jnp.float32) * ahead[0]
            for j in range(1, count):
                total = total + moved[i, b, j].astype(jnp.float32) * ahead[j]
            placed[b, at, :] = halves(total)
    total = jnp.zeros((slots, 2 * width), jnp.float32)
    for b in range(each):
        drop = one_hot(jnp.broadcast_to(packed[b : b + 1], (slots, rows)) == number)
        total = total + dot(drop, placed[b])
    total = joined(total)
    place = lax.broadcasted_iota(jnp.int32, (group, width), 1) // block
    groups = [total[q * group : (q + 1) * group, :] for q in range(subjects)]
    for p in range(subjects):
        out = jnp.zeros((group, width), jnp.float32)
        for q in range(subjects):
            out = jnp.where(place == q, turned(groups[q], (q - p) * block), out)
        sent_ref[p * group : (p + 1) * group, :] = out


def collect_kernel(subjects, me_ref, returned_ref, *refs):
    row_refs, out_ref = refs[:-1], refs[-1]
    slots, width = returned_ref.shape
    slabs, capacity = row_refs[0].shape
    rows = out_ref.shape[0] * subjects
    block = width // subjects
    group = slots // subjects
    held = capacity // subjects
    me = me_ref[0]
    pair = halves(
        jnp.concatenate(
            [
                returned_ref[pl.ds(pl.multiple_of((me ^ d) * group, group), group), :]
                for d in range(subjects)
            ]
        )
    )
    lane = lax.broadcasted_iota(jnp.int32, (slabs, LANES), 1)
    slab = lax.broadcasted_iota(jnp.int32, (slabs, LANES), 0)
    fill = jnp.zeros((slabs, LANES - capacity), jnp.int32)
    wanted = []
    for q in range(subjects):
        chunks = [jnp.zeros((1, LANES), jnp.int32) for _ in range(slots // LANES)]
        for d in range(subjects):
            spread = jnp.concatenate([row_refs[d][...], fill], axis=1)
            spread = turned(spread, d * group - q * held)
            spread = pltpu.roll(spread, 0, axis=1, stride=held, stride_axis=0)
            first = (d * group) % LANES + slab * held
            kept = jnp.where((lane >= first) & (lane < first + held), spread, 0)
            chunks[d * group // LANES] += jnp.sum(kept, axis=0, keepdims=True)
        wanted.append(jnp.concatenate(chunks, axis=1))
    number = lax.broadcasted_iota(jnp.int32, (rows, slots), 0)
    place = lax.broadcasted_iota(jnp.int32, (rows, width), 1) // block
    kept = jnp.zeros((rows, width), jnp.float32)
    for q in range(subjects):
        match = jnp.broadcast_to(wanted[q], (rows, slots)) == number
        kept = jnp.where(place == q, joined(dot(one_hot(match), pair)), kept)
    turn = block
    while turn < width:
        kept = kept + turned(kept, turn)
        turn *= 2
    part = rows // subjects
    out = jnp.zeros((part, width), jnp.float32)
    for p in range(subjects):
        out = jnp.where(place[:part] == p, kept[p * part : (p + 1) * part], out)
    out_ref[...] = out


def update_kernel(subjects, me_ref, template_ref, *refs):
    parts, out_ref = refs[:-1], refs[-1]
    rows, width = template_ref.shape
    block = width // subjects
    part = rows // subjects
    me = me_ref[0]
    place = lax.broadcasted_iota(jnp.int32, (part, width), 1) // block
    for p in range(subjects):
        total = jnp.zeros((part, width), jnp.float32)
        for d in range(subjects):
            source = me ^ d
            turn = lax.rem((source - p) * block + width, width)
            total = jnp.where(place == source, pltpu.roll(parts[d][...], turn, axis=1), total)
        at = slice(p * part, (p + 1) * part)
        out_ref[at, :] = template_ref[at, :] - template_rate * total / subjects


def over_subjects(values):
    count = lax.axis_size("subj")
    return [values] + [
        lax.ppermute(values, "subj", [(i, i ^ d) for i in range(count)]) for d in range(1, count)
    ]


def swap_near(values):
    return lax.ppermute(values, "slab", [(i, i ^ 1) for i in range(lax.axis_size("slab"))])


def swap_far(values):
    count = lax.axis_size("slab")
    return lax.ppermute(
        values, "slab", [(i, i + 1 if i % 2 else i - 1) for i in range(1, count - 1)]
    )


def clear_pads(ref):
    rows = ref.shape[-2] - 2 * PAD
    zeros = jnp.zeros(ref.shape[:-2] + (PAD, ref.shape[-1]), ref.dtype)
    ref[..., :PAD, :] = zeros
    ref[..., PAD + rows :, :] = zeros


def plane_of(ref, *at, step=0):
    rows = ref.shape[-2] - 2 * PAD
    return ref[(*at, slice(PAD + step, PAD + step + rows), slice(None))]


def sides(odd, near, far):
    return jnp.where(odd, near, far), jnp.where(odd, far, near)


def step_weights(coefs, p, below, above):
    center = plane_of(coefs, p)
    lane = lax.broadcasted_iota(jnp.int32, center.shape, 1)
    scale = 0.5 * diffusion_dt
    last = center.shape[1] - 1
    right = center + jnp.where(lane == last, 0.0, turned(center, -1))
    left = center + jnp.where(lane == 0, 0.0, turned(center, 1))
    others = [
        center + near
        for near in (plane_of(coefs, p, step=1), plane_of(coefs, p, step=-1), above, below)
    ]
    total = right + left
    for face in others:
        total = total + face
    return [
        1.0 - scale * total,
        jnp.where(lane == last, 0.0, scale * right),
        jnp.where(lane == 0, 0.0, scale * left),
    ] + [scale * face for face in others]


def all_weights(coefs, low, high):
    planes = coefs.shape[0]
    column = [low] + [plane_of(coefs, p) for p in range(planes)] + [high]
    return [step_weights(coefs, p, column[p], column[p + 2]) for p in range(planes)]


def stepped(fields, a, low, high, weights):
    planes = fields.shape[1]
    column = [low] + [plane_of(fields, a, p) for p in range(planes)] + [high]
    later = []
    for p in range(planes):
        values = [
            turned(column[p + 1], -1),
            turned(column[p + 1], 1),
            plane_of(fields, a, p, step=1),
            plane_of(fields, a, p, step=-1),
            column[p + 2],
            column[p],
        ]
        total = weights[p][0] * column[p + 1]
        for weight, value in zip(weights[p][1:], values):
            total = total + weight * value
        later.append(total)
    return later


def force_kernel(
    place_ref,
    velocity_ref,
    images_ref,
    stiffness_ref,
    warped_ref,
    edge_near_ref,
    edge_far_ref,
    warped_near_ref,
    warped_far_ref,
    field_ref,
    coefs_ref,
    near_ref,
    far_ref,
    velocity,
    images,
    warped,
    fields,
    outer,
    sem,
):
    parts, planes, rows = velocity.shape[:3]
    odd = place_ref[0] == 1
    body = slice(PAD, PAD + rows)
    copies = [
        pltpu.make_async_copy(stiffness_ref, coefs_ref.at[:, pl.ds(PAD, rows)], sem.at[0]),
        pltpu.make_async_copy(images_ref, images, sem.at[1]),
    ] + [pltpu.make_async_copy(velocity_ref.at[a], velocity.at[a], sem.at[2 + a]) for a in range(parts)]
    for copy in copies:
        copy.start()
    for ref in (field_ref, fields, coefs_ref, warped):
        clear_pads(ref)
    lowest = jnp.where(odd, warped_near_ref[0], warped_far_ref[0])
    highest = jnp.where(odd, warped_far_ref[1], warped_near_ref[1])
    warped[0, body, :] = jnp.where(odd, warped_near_ref[1], warped_far_ref[1])
    warped[planes + 1, body, :] = jnp.where(odd, warped_far_ref[0], warped_near_ref[0])
    for p in range(planes):
        warped[p + 1, body, :] = warped_ref[p]
    column = [lowest] + [plane_of(warped, p) for p in range(planes + 2)] + [highest]
    image_low, image_high = sides(odd, edge_near_ref[parts + 1, 0], edge_far_ref[parts + 1, 0])
    lane = lax.broadcasted_iota(jnp.int32, (rows, LANES), 1)
    right = jnp.where(lane == LANES - 1, 0.0, 0.5 * force_step)
    left = jnp.where(lane == 0, 0.0, 0.5 * force_step)

    def forces(p, image):
        here = column[p + 1]
        mismatch = here - image
        half = (0.5 * force_step) * mismatch
        return [
            mismatch * (right * turned(here, -1) - left * turned(here, 1)),
            half * (plane_of(warped, p, step=1) - plane_of(warped, p, step=-1)),
            half * (column[p + 2] - column[p]),
        ]

    for side, p, image in ((0, 0, image_low), (1, planes + 1, image_high)):
        force = forces(p, image)
        for a in range(parts):
            outer[side, a] = sides(odd, edge_near_ref[a, 0], edge_far_ref[a, 0])[side] - force[a]
    copies[0].wait()
    weights = all_weights(
        coefs_ref, *sides(odd, edge_near_ref[parts, 0], edge_far_ref[parts, 0])
    )
    for copy in copies[1:]:
        copy.wait()
    for p in range(planes):
        force = forces(p + 1, images[p])
        for a in range(parts):
            fields[a, p, body, :] = velocity[a, p] - force[a]
    for a in range(parts):
        later = stepped(fields, a, outer[0, a], outer[1, a], weights)
        for p in range(planes):
            field_ref[a, p, body, :] = later[p]
        near_ref[a, 0], far_ref[a, 0] = sides(odd, later[0], later[-1])


def last_kernel(
    place_ref,
    field_ref,
    coefs_ref,
    edge_near_ref,
    edge_far_ref,
    near_ref,
    far_ref,
    out_ref,
    done,
    sem,
):
    parts, planes = done.shape[:2]
    odd = place_ref[0] == 1
    weights = all_weights(
        coefs_ref, *sides(odd, edge_near_ref[parts, 0], edge_far_ref[parts, 0])
    )
    writes = [pltpu.make_async_copy(done.at[a], out_ref.at[a], sem.at[a]) for a in range(parts)]
    for a in range(parts):
        later = stepped(field_ref, a, *sides(odd, near_ref[a, 0], far_ref[a, 0]), weights)
        for p in range(planes):
            done[a, p] = later[p]
        writes[a].start()
    for copy in writes:
        copy.wait()


def per_device(template, images, velocity, stiffness, send_rows, ref_slot, columns, weights):
    f32, bf16 = jnp.float32, jnp.bfloat16
    shape = jax.ShapeDtypeStruct
    slabs = lax.axis_size("slab")
    subjects = lax.axis_size("subj")
    me = lax.axis_index("subj").astype(jnp.int32).reshape(1)
    slab = lax.axis_index("slab")
    odd = slab % 2 == 1
    place = odd.astype(jnp.int32).reshape(1)
    capacity = send_rows.shape[3]
    rows, width = template.shape
    planes = rows // YR
    parts = velocity.shape[1]
    each = ref_slot.shape[2]
    terms = rows * each
    slots = slabs * capacity
    grid = (planes, YR, width)
    velocity_grid = velocity[0].reshape((parts,) + grid)
    images_grid = images[0].reshape(grid)
    coef_grid = stiffness.reshape(grid)
    dma = pltpu.SemaphoreType.DMA

    sending = call(
        send_kernel,
        shape((slots, width), f32),
        send_rows[0, 0],
        template,
        far=(0, 1),
        scratch=(pltpu.VMEM((slabs, capacity), jnp.int32), pltpu.VMEM((rows, width), f32), dma((2,))),
    )
    sending, own_rows = lax.optimization_barrier((sending, send_rows[0, 0]))
    all_rows = over_subjects(own_rows)
    received = lax.all_to_all(sending, "slab", split_axis=0, concat_axis=0, tiled=True)

    chunks = 4
    moved_shape = (chunks, each, len(OFFSETS), rows // chunks, width)
    edge_shape = (parts + 2, 1, YR, width)
    moved, edge_near, edge_far = call(
        prepare_kernel,
        (shape(moved_shape, bf16), shape(edge_shape, f32), shape(edge_shape, f32)),
        place,
        columns.reshape(terms, width),
        weights.reshape(terms, width),
        velocity_grid,
        coef_grid,
        images_grid,
        smem=(0,),
        far=(1, 2, 3, 4, 5),
        out_far=(0, 1, 2),
        scratch=(
            pltpu.VMEM((terms, width), jnp.int32),
            pltpu.VMEM((terms, width), bf16),
            pltpu.VMEM((terms // chunks, width), f32),
            pltpu.VMEM(moved_shape, bf16),
            pltpu.VMEM((parts + 2,) + grid, f32),
            dma((2 * chunks,)),
            dma((chunks + 2,)),
            dma((3,)),
        ),
    )
    received, edge_far, edge_near, *all_rows = lax.optimization_barrier(
        (received, edge_far, edge_near, *all_rows)
    )
    edge_far, edge_near = swap_far(edge_far), swap_near(edge_near)

    warped, sent = call(
        functools.partial(warp_kernel, slabs, subjects),
        (shape((rows, width), f32), shape((slots, width), f32)),
        ref_slot[0].T,
        received,
        moved,
        images[0],
        far=(2, 3),
        scratch=(
            pltpu.VMEM((rows, width), f32),
            pltpu.VMEM(moved_shape, bf16),
            pltpu.VMEM((each, rows, width), f32),
            pltpu.VMEM((each, rows, 2 * width), bf16),
            dma,
            dma((chunks,)),
        ),
    )
    sent, edge_far, edge_near = lax.optimization_barrier((sent, edge_far, edge_near))
    returned = lax.all_to_all(sent, ("subj", "slab"), split_axis=0, concat_axis=0, tiled=True)

    warped_grid = warped.reshape(grid)
    warped_far, warped_near = swap_far(warped_grid), swap_near(warped_grid)

    high = YR + 2 * PAD
    field, coefs, field_near, field_far = call(
        force_kernel,
        (
            shape((parts, planes, high, width), f32),
            shape((planes, high, width), f32),
            shape((parts, 1, YR, width), f32),
            shape((parts, 1, YR, width), f32),
        ),
        place,
        velocity_grid,
        images_grid,
        coef_grid,
        warped_grid,
        edge_near,
        edge_far,
        warped_near,
        warped_far,
        smem=(0,),
        far=(1, 2, 3),
        scratch=(
            pltpu.VMEM((parts,) + grid, f32),
            pltpu.VMEM(grid, f32),
            pltpu.VMEM((planes + 2, high, width), f32),
            pltpu.VMEM((parts, planes, high, width), f32),
            pltpu.VMEM((2, parts, YR, width), f32),
            dma((2 + parts,)),
        ),
    )
    field_far, field_near = swap_far(field_far), swap_near(field_near)

    part = call(
        functools.partial(collect_kernel, subjects),
        shape((rows // subjects, width), f32),
        me,
        returned,
        *all_rows,
        smem=(0,),
    )
    pieces = over_subjects(part)
    template_out = call(
        functools.partial(update_kernel, subjects),
        shape((rows, width), f32),
        me,
        template,
        *pieces,
        smem=(0,),
    )
    field = call(
        last_kernel,
        shape((parts,) + grid, f32),
        place,
        field,
        coefs,
        edge_near,
        edge_far,
        field_near,
        field_far,
        smem=(0,),
        out_far=(0,),
        scratch=(pltpu.VMEM((parts,) + grid, f32), dma((parts,))),
    )
    velocity_out = field.reshape(parts, rows, width)[None]
    return (template_out, velocity_out)


def solution(mesh):
    return jax.shard_map(
        per_device,
        mesh=mesh,
        in_specs=(
            P("slab", None),
            P("subj", "slab", None),
            P("subj", None, "slab", None),
            P("slab", None),
            P("subj", "slab", None, None),
            P("subj", "slab", None),
            P("subj", "slab", None, None),
            P("subj", "slab", None, None),
        ),
        out_specs=(P("slab", None), P("subj", None, "slab", None)),
        check_vma=False,
    )
```

```python
import functools

import jax
import jax.numpy as jnp
from jax import lax
from jax.experimental import pallas as pl
from jax.experimental.pallas import tpu as pltpu
from jax.sharding import PartitionSpec as P

YR = 256
LANES = 128
PAD = 8
OFFSETS = (0, -2, -1, 1, 2)


force_step = 1.0
diffusion_dt = 0.16
template_rate = 2.0

VMEM_LIMIT = 40 * 1024 * 1024


def call(kernel, out_shape, *args, scratch=(), smem=(), far=(), out_far=()):
    many = isinstance(out_shape, tuple)
    shapes = [
        pltpu.HBM(s.shape, s.dtype) if i in out_far else s
        for i, s in enumerate(out_shape if many else (out_shape,))
    ]
    spaces = [pltpu.HBM if i in out_far else pltpu.VMEM for i in range(len(shapes))]
    specs = [pl.BlockSpec(memory_space=space) for space in spaces]
    return pl.pallas_call(
        kernel,
        out_shape=tuple(shapes) if many else shapes[0],
        in_specs=[
            pl.BlockSpec(
                memory_space=pltpu.SMEM if i in smem else pltpu.HBM if i in far else pltpu.VMEM
            )
            for i in range(len(args))
        ],
        out_specs=tuple(specs) if many else specs[0],
        scratch_shapes=scratch,
        compiler_params=pltpu.CompilerParams(vmem_limit_bytes=VMEM_LIMIT),
    )(
        *[
            pltpu.with_memory_space_constraint(arg, pltpu.HBM) if i in far else arg
            for i, arg in enumerate(args)
        ]
    )


def halves(values):
    high = values.astype(jnp.bfloat16)
    low = (values - high.astype(jnp.float32)).astype(jnp.bfloat16)
    return jnp.concatenate([high, low], axis=1)


def joined(pair):
    width = pair.shape[1] // 2
    return pair[:, :width] + pair[:, width:]


def turned(values, shift):
    shift %= values.shape[1]
    return pltpu.roll(values, shift, axis=1) if shift else values


def dot(left, right):
    return jnp.dot(left, right, preferred_element_type=jnp.float32)


def one_hot(matches):
    return jnp.where(matches, 1.0, 0.0).astype(jnp.bfloat16)


def send_kernel(send_ref, template_ref, out_ref, send, template, sem):
    slabs, capacity = send.shape
    rows = template.shape[0]
    copies = [
        pltpu.make_async_copy(send_ref, send, sem.at[0]),
        pltpu.make_async_copy(template_ref, template, sem.at[1]),
    ]
    for copy in copies:
        copy.start()
    copies[0].wait()
    padded = jnp.concatenate([send[...], jnp.zeros((slabs, LANES - capacity), jnp.int32)], axis=1)
    columns = padded.T
    number = lax.broadcasted_iota(jnp.int32, (capacity, rows), 1)
    chosen = [
        one_hot(jnp.broadcast_to(columns[:capacity, k : k + 1], (capacity, rows)) == number)
        for k in range(slabs)
    ]
    copies[1].wait()
    pair = halves(template[...])
    for k in range(slabs):
        out_ref[k * capacity : (k + 1) * capacity, :] = joined(dot(chosen[k], pair))


def prepare_kernel(
    place_ref,
    columns_ref,
    weights_ref,
    velocity_ref,
    stiffness_ref,
    images_ref,
    moved_ref,
    near_ref,
    far_ref,
    columns,
    weights,
    plain,
    moved,
    edge,
    in_sem,
    out_sem,
    edge_sem,
):
    chunks, each, count, some, width = moved.shape
    odd = place_ref[0]
    near_plane, far_plane = pl.ds((edge.shape[1] - 1) * (1 - odd), 1), pl.ds((edge.shape[1] - 1) * odd, 1)
    step = some * each
    parts = velocity_ref.shape[0]
    reads = [
        (
            pltpu.make_async_copy(
                columns_ref.at[pl.ds(i * step, step)], columns.at[pl.ds(i * step, step)], in_sem.at[i]
            ),
            pltpu.make_async_copy(
                weights_ref.at[pl.ds(i * step, step)],
                weights.at[pl.ds(i * step, step)],
                in_sem.at[chunks + i],
            ),
        )
        for i in range(chunks)
    ]
    edges = [
        pltpu.make_async_copy(velocity_ref, edge.at[pl.ds(0, parts)], edge_sem.at[0]),
        pltpu.make_async_copy(stiffness_ref, edge.at[parts], edge_sem.at[1]),
        pltpu.make_async_copy(images_ref, edge.at[parts + 1], edge_sem.at[2]),
    ]
    writes = [
        pltpu.make_async_copy(moved.at[i], moved_ref.at[i], out_sem.at[i]) for i in range(chunks)
    ] + [
        pltpu.make_async_copy(edge.at[:, near_plane], near_ref, out_sem.at[chunks]),
        pltpu.make_async_copy(edge.at[:, far_plane], far_ref, out_sem.at[chunks + 1]),
    ]
    for copy in reads[0]:
        copy.start()
    for copy in edges:
        copy.start()
    for pair in reads[1:]:
        for copy in pair:
            copy.start()
    cell = lax.broadcasted_iota(jnp.int32, (some, width), 1)
    for i in range(chunks):
        at = i * step
        for copy in reads[i]:
            copy.wait()
        plain[...] = weights[at : at + step, :].astype(jnp.float32)
        for b in range(each):
            offset = columns[pl.ds(at + b, some, stride=each), :] - cell
            here = plain[pl.ds(b, some, stride=each), :]
            for j, o in enumerate(OFFSETS):
                kept = jnp.where(offset == o, here, 0.0)
                moved[i, b, j] = turned(kept, o).astype(jnp.bfloat16)
        writes[i].start()
        if i == 0:
            for copy in edges:
                copy.wait()
            for copy in writes[chunks:]:
                copy.start()
    for copy in writes:
        copy.wait()


def warp_kernel(
    slabs,
    subjects,
    slot_ref,
    received_ref,
    moved_ref,
    images_ref,
    warped_ref,
    sent_ref,
    images,
    moved,
    picked,
    placed,
    first_sem,
    moved_sem,
):
    slots, width = received_ref.shape
    chunks, each, count, some = moved.shape[:4]
    rows = chunks * some
    block = width // subjects
    group = slots // subjects
    capacity = slots // slabs
    held = capacity // subjects
    first = pltpu.make_async_copy(images_ref, images, first_sem)
    moves = [
        pltpu.make_async_copy(moved_ref.at[i], moved.at[i], moved_sem.at[i]) for i in range(chunks)
    ]
    for copy in moves[:1] + [first] + moves[1:]:
        copy.start()
    slot = slot_ref[...]
    slot_wide = jnp.concatenate([slot, jnp.zeros((LANES - each, rows), jnp.int32)], axis=0).T
    inner = slot % capacity
    packed = (inner // held) * group + (slot // capacity) * held + inner % held
    lane = lax.broadcasted_iota(jnp.int32, (rows, LANES), 1)
    number = lax.broadcasted_iota(jnp.int32, (slots, rows), 0)
    pair = halves(received_ref[...])
    for b in range(each):
        wide = jnp.broadcast_to(slot_wide[:, b : b + 1], (rows, LANES))
        pick = jnp.concatenate(
            [one_hot(wide == lane + t * LANES) for t in range(slots // LANES)], axis=1
        )
        picked[b] = joined(dot(pick, pair))
    for copy in [first] + moves:
        copy.wait()
    for i in range(chunks):
        at = slice(i * some, (i + 1) * some)
        sums = [jnp.zeros((some, width), jnp.float32) for _ in OFFSETS]
        for b in range(each):
            values = picked[b, at, :]
            for j in range(count):
                sums[j] = sums[j] + moved[i, b, j].astype(jnp.float32) * values
        warped = sums[0]
        for j, o in enumerate(OFFSETS[1:], 1):
            warped = warped + turned(sums[j], -o)
        warped_ref[at, :] = warped
        mismatch = warped - images[at, :]
        ahead = [turned(mismatch, o) for o in OFFSETS]
        for b in range(each):
            total = moved[i, b, 0].astype(jnp.float32) * ahead[0]
            for j in range(1, count):
                total = total + moved[i, b, j].astype(jnp.float32) * ahead[j]
            placed[b, at, :] = halves(total)
    total = jnp.zeros((slots, 2 * width), jnp.float32)
    for b in range(each):
        drop = one_hot(jnp.broadcast_to(packed[b : b + 1], (slots, rows)) == number)
        total = total + dot(drop, placed[b])
    total = joined(total)
    place = lax.broadcasted_iota(jnp.int32, (group, width), 1) // block
    groups = [total[q * group : (q + 1) * group, :] for q in range(subjects)]
    for p in range(subjects):
        out = jnp.zeros((group, width), jnp.float32)
        for q in range(subjects):
            out = jnp.where(place == q, turned(groups[q], (q - p) * block), out)
        sent_ref[p * group : (p + 1) * group, :] = out


def collect_kernel(subjects, me_ref, returned_ref, *refs):
    row_refs, out_ref = refs[:-1], refs[-1]
    slots, width = returned_ref.shape
    slabs, capacity = row_refs[0].shape
    rows = out_ref.shape[0] * subjects
    block = width // subjects
    group = slots // subjects
    held = capacity // subjects
    me = me_ref[0]
    pair = halves(
        jnp.concatenate(
            [
                returned_ref[pl.ds(pl.multiple_of((me ^ d) * group, group), group), :]
                for d in range(subjects)
            ]
        )
    )
    lane = lax.broadcasted_iota(jnp.int32, (slabs, LANES), 1)
    slab = lax.broadcasted_iota(jnp.int32, (slabs, LANES), 0)
    fill = jnp.zeros((slabs, LANES - capacity), jnp.int32)
    wanted = []
    for q in range(subjects):
        chunks = [jnp.zeros((1, LANES), jnp.int32) for _ in range(slots // LANES)]
        for d in range(subjects):
            spread = jnp.concatenate([row_refs[d][...], fill], axis=1)
            spread = turned(spread, d * group - q * held)
            spread = pltpu.roll(spread, 0, axis=1, stride=held, stride_axis=0)
            first = (d * group) % LANES + slab * held
            kept = jnp.where((lane >= first) & (lane < first + held), spread, 0)
            chunks[d * group // LANES] += jnp.sum(kept, axis=0, keepdims=True)
        wanted.append(jnp.concatenate(chunks, axis=1))
    number = lax.broadcasted_iota(jnp.int32, (rows, slots), 0)
    place = lax.broadcasted_iota(jnp.int32, (rows, width), 1) // block
    kept = jnp.zeros((rows, width), jnp.float32)
    for q in range(subjects):
        match = jnp.broadcast_to(wanted[q], (rows, slots)) == number
        kept = jnp.where(place == q, joined(dot(one_hot(match), pair)), kept)
    turn = block
    while turn < width:
        kept = kept + turned(kept, turn)
        turn *= 2
    part = rows // subjects
    out = jnp.zeros((part, width), jnp.float32)
    for p in range(subjects):
        out = jnp.where(place[:part] == p, kept[p * part : (p + 1) * part], out)
    out_ref[...] = out


def update_kernel(subjects, me_ref, template_ref, *refs):
    parts, out_ref = refs[:-1], refs[-1]
    rows, width = template_ref.shape
    block = width // subjects
    part = rows // subjects
    me = me_ref[0]
    place = lax.broadcasted_iota(jnp.int32, (part, width), 1) // block
    for p in range(subjects):
        total = jnp.zeros((part, width), jnp.float32)
        for d in range(subjects):
            source = me ^ d
            turn = lax.rem((source - p) * block + width, width)
            total = jnp.where(place == source, pltpu.roll(parts[d][...], turn, axis=1), total)
        at = slice(p * part, (p + 1) * part)
        out_ref[at, :] = template_ref[at, :] - template_rate * total / subjects


def over_subjects(values):
    count = lax.axis_size("subj")
    return [values] + [
        lax.ppermute(values, "subj", [(i, i ^ d) for i in range(count)]) for d in range(1, count)
    ]


def swap_near(values):
    return lax.ppermute(values, "slab", [(i, i ^ 1) for i in range(lax.axis_size("slab"))])


def swap_far(values):
    count = lax.axis_size("slab")
    return lax.ppermute(
        values, "slab", [(i, i + 1 if i % 2 else i - 1) for i in range(1, count - 1)]
    )


def clear_pads(ref):
    rows = ref.shape[-2] - 2 * PAD
    zeros = jnp.zeros(ref.shape[:-2] + (PAD, ref.shape[-1]), ref.dtype)
    ref[..., :PAD, :] = zeros
    ref[..., PAD + rows :, :] = zeros


def plane_of(ref, *at, step=0):
    rows = ref.shape[-2] - 2 * PAD
    return ref[(*at, slice(PAD + step, PAD + step + rows), slice(None))]


def sides(odd, near, far):
    return jnp.where(odd, near, far), jnp.where(odd, far, near)


def step_weights(coefs, p):
    center = plane_of(coefs, p)
    lane = lax.broadcasted_iota(jnp.int32, center.shape, 1)
    scale = 0.5 * diffusion_dt
    last = center.shape[1] - 1
    right = center + jnp.where(lane == last, 0.0, turned(center, -1))
    left = center + jnp.where(lane == 0, 0.0, turned(center, 1))
    others = [
        center + near
        for near in (
            plane_of(coefs, p, step=1),
            plane_of(coefs, p, step=-1),
            plane_of(coefs, p + 1),
            plane_of(coefs, p - 1),
        )
    ]
    total = right + left
    for face in others:
        total = total + face
    return [
        1.0 - scale * total,
        jnp.where(lane == last, 0.0, scale * right),
        jnp.where(lane == 0, 0.0, scale * left),
    ] + [scale * face for face in others]


def all_weights(coefs):
    return [step_weights(coefs, p) for p in range(1, coefs.shape[0] - 1)]


def stepped(fields, a, low, high, weights):
    planes = fields.shape[1]
    column = [low] + [plane_of(fields, a, p) for p in range(planes)] + [high]
    later = []
    for p in range(planes):
        values = [
            turned(column[p + 1], -1),
            turned(column[p + 1], 1),
            plane_of(fields, a, p, step=1),
            plane_of(fields, a, p, step=-1),
            column[p + 2],
            column[p],
        ]
        total = weights[p][0] * column[p + 1]
        for weight, value in zip(weights[p][1:], values):
            total = total + weight * value
        later.append(total)
    return later


def by_side(odd, pairs):
    copies = [
        (
            [pltpu.make_async_copy(near, low, sems[0]), pltpu.make_async_copy(far, high, sems[1])],
            [pltpu.make_async_copy(near, high, sems[0]), pltpu.make_async_copy(far, low, sems[1])],
        )
        for near, far, low, high, sems in pairs
    ]

    @pl.when(odd)
    def _():
        for when_odd, _ in copies:
            for copy in when_odd:
                copy.start()

    @pl.when(jnp.logical_not(odd))
    def _():
        for _, when_even in copies:
            for copy in when_even:
                copy.start()

    return [copy for when_odd, _ in copies for copy in when_odd]


def force_kernel(
    place_ref,
    velocity_ref,
    images_ref,
    stiffness_ref,
    warped_ref,
    edge_near_ref,
    edge_far_ref,
    warped_near_ref,
    warped_far_ref,
    field_ref,
    coefs_ref,
    near_ref,
    far_ref,
    velocity,
    images,
    warped,
    fields,
    outer,
    sem,
):
    parts, planes, rows = velocity.shape[:3]
    odd = place_ref[0] == 1
    body = slice(PAD, PAD + rows)
    within, every = pl.ds(PAD, rows), pl.ds(0, parts)
    low, mid, high = pl.ds(0, 1), pl.ds(1, planes), pl.ds(planes + 1, 1)
    copies = [
        pltpu.make_async_copy(stiffness_ref, coefs_ref.at[mid, within], sem.at[0]),
        pltpu.make_async_copy(images_ref, images.at[mid], sem.at[1]),
        pltpu.make_async_copy(velocity_ref, velocity, sem.at[2]),
    ]
    for copy in copies:
        copy.start()
    copies += by_side(
        odd,
        [
            (
                edge_near_ref.at[parts],
                edge_far_ref.at[parts],
                coefs_ref.at[low, within],
                coefs_ref.at[high, within],
                (sem.at[3], sem.at[4]),
            ),
            (
                edge_near_ref.at[parts + 1],
                edge_far_ref.at[parts + 1],
                images.at[low],
                images.at[high],
                (sem.at[5], sem.at[6]),
            ),
            (
                edge_near_ref.at[every],
                edge_far_ref.at[every],
                outer.at[:, low],
                outer.at[:, pl.ds(1, 1)],
                (sem.at[7], sem.at[8]),
            ),
        ],
    )
    for ref in (field_ref, fields, coefs_ref, warped):
        clear_pads(ref)
    lowest = jnp.where(odd, warped_near_ref[0], warped_far_ref[0])
    highest = jnp.where(odd, warped_far_ref[1], warped_near_ref[1])
    warped[0, body, :] = jnp.where(odd, warped_near_ref[1], warped_far_ref[1])
    warped[planes + 1, body, :] = jnp.where(odd, warped_far_ref[0], warped_near_ref[0])
    for p in range(planes):
        warped[p + 1, body, :] = warped_ref[p]
    column = [lowest] + [plane_of(warped, p) for p in range(planes + 2)] + [highest]
    lane = lax.broadcasted_iota(jnp.int32, (rows, LANES), 1)
    right = jnp.where(lane == LANES - 1, 0.0, 0.5 * force_step)
    left = jnp.where(lane == 0, 0.0, 0.5 * force_step)

    def forces(p, image):
        here = column[p + 1]
        mismatch = here - image
        half = (0.5 * force_step) * mismatch
        return [
            mismatch * (right * turned(here, -1) - left * turned(here, 1)),
            half * (plane_of(warped, p, step=1) - plane_of(warped, p, step=-1)),
            half * (column[p + 2] - column[p]),
        ]

    for copy in (copies[0], copies[3], copies[4]):
        copy.wait()
    weights = all_weights(coefs_ref)
    for copy in copies[1:3] + copies[5:]:
        copy.wait()
    for p in range(planes + 2):
        force = forces(p, images[p])
        for a in range(parts):
            if p == 0:
                outer[a, 0] = outer[a, 0] - force[a]
            elif p == planes + 1:
                outer[a, 1] = outer[a, 1] - force[a]
            else:
                fields[a, p - 1, body, :] = velocity[a, p - 1] - force[a]
    for a in range(parts):
        later = stepped(fields, a, outer[a, 0], outer[a, 1], weights)
        for p in range(planes):
            field_ref[a, p, body, :] = later[p]
        near_ref[a, 0], far_ref[a, 0] = sides(odd, later[0], later[-1])


def last_kernel(
    place_ref,
    field_ref,
    coefs_ref,
    near_ref,
    far_ref,
    out_ref,
    done,
    sem,
):
    parts, planes = done.shape[:2]
    odd = place_ref[0] == 1
    weights = all_weights(coefs_ref)
    writes = [pltpu.make_async_copy(done.at[a], out_ref.at[a], sem.at[a]) for a in range(parts)]
    for a in range(parts):
        later = stepped(field_ref, a, *sides(odd, near_ref[a, 0], far_ref[a, 0]), weights)
        for p in range(planes):
            done[a, p] = later[p]
        writes[a].start()
    for copy in writes:
        copy.wait()


def per_device(template, images, velocity, stiffness, send_rows, ref_slot, columns, weights):
    f32, bf16 = jnp.float32, jnp.bfloat16
    shape = jax.ShapeDtypeStruct
    slabs = lax.axis_size("slab")
    subjects = lax.axis_size("subj")
    me = lax.axis_index("subj").astype(jnp.int32).reshape(1)
    slab = lax.axis_index("slab")
    odd = slab % 2 == 1
    place = odd.astype(jnp.int32).reshape(1)
    capacity = send_rows.shape[3]
    rows, width = template.shape
    planes = rows // YR
    parts = velocity.shape[1]
    each = ref_slot.shape[2]
    terms = rows * each
    slots = slabs * capacity
    grid = (planes, YR, width)
    velocity_grid = velocity[0].reshape((parts,) + grid)
    images_grid = images[0].reshape(grid)
    coef_grid = stiffness.reshape(grid)
    dma = pltpu.SemaphoreType.DMA

    sending = call(
        send_kernel,
        shape((slots, width), f32),
        send_rows[0, 0],
        template,
        far=(0, 1),
        scratch=(pltpu.VMEM((slabs, capacity), jnp.int32), pltpu.VMEM((rows, width), f32), dma((2,))),
    )
    sending, own_rows = lax.optimization_barrier((sending, send_rows[0, 0]))
    all_rows = over_subjects(own_rows)
    received = lax.all_to_all(sending, "slab", split_axis=0, concat_axis=0, tiled=True)

    chunks = 4
    moved_shape = (chunks, each, len(OFFSETS), rows // chunks, width)
    edge_shape = (parts + 2, 1, YR, width)
    moved, edge_near, edge_far = call(
        prepare_kernel,
        (shape(moved_shape, bf16), shape(edge_shape, f32), shape(edge_shape, f32)),
        place,
        columns.reshape(terms, width),
        weights.reshape(terms, width),
        velocity_grid,
        coef_grid,
        images_grid,
        smem=(0,),
        far=(1, 2, 3, 4, 5),
        out_far=(0, 1, 2),
        scratch=(
            pltpu.VMEM((terms, width), jnp.int32),
            pltpu.VMEM((terms, width), bf16),
            pltpu.VMEM((terms // chunks, width), f32),
            pltpu.VMEM(moved_shape, bf16),
            pltpu.VMEM((parts + 2,) + grid, f32),
            dma((2 * chunks,)),
            dma((chunks + 2,)),
            dma((3,)),
        ),
    )
    received, edge_far, edge_near, *all_rows = lax.optimization_barrier(
        (received, edge_far, edge_near, *all_rows)
    )
    edge_far, edge_near = swap_far(edge_far), swap_near(edge_near)

    warped, sent = call(
        functools.partial(warp_kernel, slabs, subjects),
        (shape((rows, width), f32), shape((slots, width), f32)),
        ref_slot[0].T,
        received,
        moved,
        images[0],
        far=(2, 3),
        scratch=(
            pltpu.VMEM((rows, width), f32),
            pltpu.VMEM(moved_shape, bf16),
            pltpu.VMEM((each, rows, width), f32),
            pltpu.VMEM((each, rows, 2 * width), bf16),
            dma,
            dma((chunks,)),
        ),
    )
    sent, edge_far, edge_near = lax.optimization_barrier((sent, edge_far, edge_near))
    returned = lax.all_to_all(sent, ("subj", "slab"), split_axis=0, concat_axis=0, tiled=True)

    warped_grid = warped.reshape(grid)
    warped_far, warped_near = swap_far(warped_grid), swap_near(warped_grid)

    high = YR + 2 * PAD
    field, coefs, field_near, field_far = call(
        force_kernel,
        (
            shape((parts, planes, high, width), f32),
            shape((planes + 2, high, width), f32),
            shape((parts, 1, YR, width), f32),
            shape((parts, 1, YR, width), f32),
        ),
        place,
        velocity_grid,
        images_grid,
        coef_grid,
        warped_grid,
        edge_near,
        edge_far,
        warped_near,
        warped_far,
        smem=(0,),
        far=(1, 2, 3, 5, 6),
        scratch=(
            pltpu.VMEM((parts,) + grid, f32),
            pltpu.VMEM((planes + 2, YR, width), f32),
            pltpu.VMEM((planes + 2, high, width), f32),
            pltpu.VMEM((parts, planes, high, width), f32),
            pltpu.VMEM((parts, 2, YR, width), f32),
            dma((9,)),
        ),
    )
    field_far, field_near = swap_far(field_far), swap_near(field_near)

    part = call(
        functools.partial(collect_kernel, subjects),
        shape((rows // subjects, width), f32),
        me,
        returned,
        *all_rows,
        smem=(0,),
    )
    pieces = over_subjects(part)
    template_out = call(
        functools.partial(update_kernel, subjects),
        shape((rows, width), f32),
        me,
        template,
        *pieces,
        smem=(0,),
    )
    field = call(
        last_kernel,
        shape((parts,) + grid, f32),
        place,
        field,
        coefs,
        field_near,
        field_far,
        smem=(0,),
        out_far=(0,),
        scratch=(pltpu.VMEM((parts,) + grid, f32), dma((parts,))),
    )
    velocity_out = field.reshape(parts, rows, width)[None]
    return (template_out, velocity_out)


def solution(mesh):
    return jax.shard_map(
        per_device,
        mesh=mesh,
        in_specs=(
            P("slab", None),
            P("subj", "slab", None),
            P("subj", None, "slab", None),
            P("slab", None),
            P("subj", "slab", None, None),
            P("subj", "slab", None),
            P("subj", "slab", None, None),
            P("subj", "slab", None, None),
        ),
        out_specs=(P("slab", None), P("subj", None, "slab", None)),
        check_vma=False,
    )
```

```python
import functools

import jax
import jax.numpy as jnp
from jax import lax
from jax.experimental import pallas as pl
from jax.experimental.pallas import tpu as pltpu
from jax.sharding import PartitionSpec as P

YR = 256
LANES = 128
PAD = 8
OFFSETS = (0, -2, -1, 1, 2)


force_step = 1.0
diffusion_dt = 0.16
template_rate = 2.0

VMEM_LIMIT = 40 * 1024 * 1024


def call(kernel, out_shape, *args, scratch=(), smem=(), far=(), out_far=()):
    many = isinstance(out_shape, tuple)
    shapes = [
        pltpu.HBM(s.shape, s.dtype) if i in out_far else s
        for i, s in enumerate(out_shape if many else (out_shape,))
    ]
    spaces = [pltpu.HBM if i in out_far else pltpu.VMEM for i in range(len(shapes))]
    specs = [pl.BlockSpec(memory_space=space) for space in spaces]
    return pl.pallas_call(
        kernel,
        out_shape=tuple(shapes) if many else shapes[0],
        in_specs=[
            pl.BlockSpec(
                memory_space=pltpu.SMEM if i in smem else pltpu.HBM if i in far else pltpu.VMEM
            )
            for i in range(len(args))
        ],
        out_specs=tuple(specs) if many else specs[0],
        scratch_shapes=scratch,
        compiler_params=pltpu.CompilerParams(vmem_limit_bytes=VMEM_LIMIT),
    )(
        *[
            pltpu.with_memory_space_constraint(arg, pltpu.HBM) if i in far else arg
            for i, arg in enumerate(args)
        ]
    )


def halves(values):
    high = values.astype(jnp.bfloat16)
    low = (values - high.astype(jnp.float32)).astype(jnp.bfloat16)
    return jnp.concatenate([high, low], axis=1)


def joined(pair):
    width = pair.shape[1] // 2
    return pair[:, :width] + pair[:, width:]


def turned(values, shift):
    shift %= values.shape[1]
    return pltpu.roll(values, shift, axis=1) if shift else values


def dot(left, right):
    return jnp.dot(left, right, preferred_element_type=jnp.float32)


def one_hot(matches):
    return jnp.where(matches, 1.0, 0.0).astype(jnp.bfloat16)


def send_kernel(send_ref, template_ref, out_ref, send, template, sem):
    slabs, capacity = send.shape
    rows = template.shape[0]
    copies = [
        pltpu.make_async_copy(send_ref, send, sem.at[0]),
        pltpu.make_async_copy(template_ref, template, sem.at[1]),
    ]
    for copy in copies:
        copy.start()
    copies[0].wait()
    padded = jnp.concatenate([send[...], jnp.zeros((slabs, LANES - capacity), jnp.int32)], axis=1)
    columns = padded.T
    number = lax.broadcasted_iota(jnp.int32, (capacity, rows), 1)
    chosen = [
        one_hot(jnp.broadcast_to(columns[:capacity, k : k + 1], (capacity, rows)) == number)
        for k in range(slabs)
    ]
    copies[1].wait()
    pair = halves(template[...])
    for k in range(slabs):
        out_ref[k * capacity : (k + 1) * capacity, :] = joined(dot(chosen[k], pair))


def prepare_kernel(
    place_ref,
    columns_ref,
    weights_ref,
    velocity_ref,
    stiffness_ref,
    images_ref,
    moved_ref,
    near_ref,
    far_ref,
    columns,
    weights,
    plain,
    moved,
    edge,
    in_sem,
    out_sem,
    edge_sem,
):
    chunks, each, count, some, width = moved.shape
    odd = place_ref[0]
    near_plane, far_plane = pl.ds((edge.shape[1] - 1) * (1 - odd), 1), pl.ds((edge.shape[1] - 1) * odd, 1)
    step = some * each
    parts = velocity_ref.shape[0]
    reads = [
        (
            pltpu.make_async_copy(
                columns_ref.at[pl.ds(i * step, step)], columns.at[pl.ds(i * step, step)], in_sem.at[i]
            ),
            pltpu.make_async_copy(
                weights_ref.at[pl.ds(i * step, step)],
                weights.at[pl.ds(i * step, step)],
                in_sem.at[chunks + i],
            ),
        )
        for i in range(chunks)
    ]
    edges = [
        pltpu.make_async_copy(velocity_ref, edge.at[pl.ds(0, parts)], edge_sem.at[0]),
        pltpu.make_async_copy(stiffness_ref, edge.at[parts], edge_sem.at[1]),
        pltpu.make_async_copy(images_ref, edge.at[parts + 1], edge_sem.at[2]),
    ]
    writes = [
        pltpu.make_async_copy(moved.at[i], moved_ref.at[i], out_sem.at[i]) for i in range(chunks)
    ] + [
        pltpu.make_async_copy(edge.at[:, near_plane], near_ref, out_sem.at[chunks]),
        pltpu.make_async_copy(edge.at[:, far_plane], far_ref, out_sem.at[chunks + 1]),
    ]
    for copy in reads[0]:
        copy.start()
    for copy in edges:
        copy.start()
    for pair in reads[1:]:
        for copy in pair:
            copy.start()
    cell = lax.broadcasted_iota(jnp.int32, (some, width), 1)
    for i in range(chunks):
        at = i * step
        for copy in reads[i]:
            copy.wait()
        plain[...] = weights[at : at + step, :].astype(jnp.float32)
        for b in range(each):
            offset = columns[pl.ds(at + b, some, stride=each), :] - cell
            here = plain[pl.ds(b, some, stride=each), :]
            for j, o in enumerate(OFFSETS):
                kept = jnp.where(offset == o, here, 0.0)
                moved[i, b, j] = turned(kept, o).astype(jnp.bfloat16)
        writes[i].start()
        if i == 0:
            for copy in edges:
                copy.wait()
            for copy in writes[chunks:]:
                copy.start()
    for copy in writes:
        copy.wait()


def warp_kernel(
    slabs,
    subjects,
    slot_ref,
    received_ref,
    moved_ref,
    images_ref,
    warped_ref,
    sent_ref,
    images,
    moved,
    picked,
    placed,
    first_sem,
    moved_sem,
):
    slots, width = received_ref.shape
    chunks, each, count, some = moved.shape[:4]
    rows = chunks * some
    block = width // subjects
    group = slots // subjects
    capacity = slots // slabs
    held = capacity // subjects
    first = pltpu.make_async_copy(images_ref, images, first_sem)
    moves = [
        pltpu.make_async_copy(moved_ref.at[i], moved.at[i], moved_sem.at[i]) for i in range(chunks)
    ]
    for copy in moves[:1] + [first] + moves[1:]:
        copy.start()
    slot = slot_ref[...]
    slot_wide = jnp.concatenate([slot, jnp.zeros((LANES - each, rows), jnp.int32)], axis=0).T
    inner = slot % capacity
    packed = (inner // held) * group + (slot // capacity) * held + inner % held
    lane = lax.broadcasted_iota(jnp.int32, (rows, LANES), 1)
    number = lax.broadcasted_iota(jnp.int32, (slots, rows), 0)
    pair = halves(received_ref[...])
    for b in range(each):
        wide = jnp.broadcast_to(slot_wide[:, b : b + 1], (rows, LANES))
        pick = jnp.concatenate(
            [one_hot(wide == lane + t * LANES) for t in range(slots // LANES)], axis=1
        )
        picked[b] = joined(dot(pick, pair))
    for copy in [first] + moves:
        copy.wait()
    for i in range(chunks):
        at = slice(i * some, (i + 1) * some)
        sums = [jnp.zeros((some, width), jnp.float32) for _ in OFFSETS]
        for b in range(each):
            values = picked[b, at, :]
            for j in range(count):
                sums[j] = sums[j] + moved[i, b, j].astype(jnp.float32) * values
        warped = sums[0]
        for j, o in enumerate(OFFSETS[1:], 1):
            warped = warped + turned(sums[j], -o)
        warped_ref[at, :] = warped
        mismatch = warped - images[at, :]
        ahead = [turned(mismatch, o) for o in OFFSETS]
        for b in range(each):
            total = moved[i, b, 0].astype(jnp.float32) * ahead[0]
            for j in range(1, count):
                total = total + moved[i, b, j].astype(jnp.float32) * ahead[j]
            placed[b, at, :] = halves(total)
    total = jnp.zeros((slots, 2 * width), jnp.float32)
    for b in range(each):
        drop = one_hot(jnp.broadcast_to(packed[b : b + 1], (slots, rows)) == number)
        total = total + dot(drop, placed[b])
    total = joined(total)
    place = lax.broadcasted_iota(jnp.int32, (group, width), 1) // block
    groups = [total[q * group : (q + 1) * group, :] for q in range(subjects)]
    for p in range(subjects):
        out = jnp.zeros((group, width), jnp.float32)
        for q in range(subjects):
            out = jnp.where(place == q, turned(groups[q], (q - p) * block), out)
        sent_ref[p * group : (p + 1) * group, :] = out


def collect_kernel(subjects, me_ref, returned_ref, *refs):
    row_refs, out_ref = refs[:-1], refs[-1]
    slots, width = returned_ref.shape
    slabs, capacity = row_refs[0].shape
    rows = out_ref.shape[0] * subjects
    block = width // subjects
    group = slots // subjects
    held = capacity // subjects
    me = me_ref[0]
    pair = halves(
        jnp.concatenate(
            [
                returned_ref[pl.ds(pl.multiple_of((me ^ d) * group, group), group), :]
                for d in range(subjects)
            ]
        )
    )
    lane = lax.broadcasted_iota(jnp.int32, (slabs, LANES), 1)
    slab = lax.broadcasted_iota(jnp.int32, (slabs, LANES), 0)
    fill = jnp.zeros((slabs, LANES - capacity), jnp.int32)
    wanted = []
    for q in range(subjects):
        chunks = [jnp.zeros((1, LANES), jnp.int32) for _ in range(slots // LANES)]
        for d in range(subjects):
            spread = jnp.concatenate([row_refs[d][...], fill], axis=1)
            spread = turned(spread, d * group - q * held)
            spread = pltpu.roll(spread, 0, axis=1, stride=held, stride_axis=0)
            first = (d * group) % LANES + slab * held
            kept = jnp.where((lane >= first) & (lane < first + held), spread, 0)
            chunks[d * group // LANES] += jnp.sum(kept, axis=0, keepdims=True)
        wanted.append(jnp.concatenate(chunks, axis=1))
    number = lax.broadcasted_iota(jnp.int32, (rows, slots), 0)
    place = lax.broadcasted_iota(jnp.int32, (rows, width), 1) // block
    kept = jnp.zeros((rows, width), jnp.float32)
    for q in range(subjects):
        match = jnp.broadcast_to(wanted[q], (rows, slots)) == number
        kept = jnp.where(place == q, joined(dot(one_hot(match), pair)), kept)
    turn = block
    while turn < width:
        kept = kept + turned(kept, turn)
        turn *= 2
    part = rows // subjects
    out = jnp.zeros((part, width), jnp.float32)
    for p in range(subjects):
        out = jnp.where(place[:part] == p, kept[p * part : (p + 1) * part], out)
    out_ref[...] = out


def update_kernel(subjects, me_ref, template_ref, *refs):
    parts, out_ref = refs[:-1], refs[-1]
    rows, width = template_ref.shape
    block = width // subjects
    part = rows // subjects
    me = me_ref[0]
    place = lax.broadcasted_iota(jnp.int32, (part, width), 1) // block
    for p in range(subjects):
        total = jnp.zeros((part, width), jnp.float32)
        for d in range(subjects):
            source = me ^ d
            turn = lax.rem((source - p) * block + width, width)
            total = jnp.where(place == source, pltpu.roll(parts[d][...], turn, axis=1), total)
        at = slice(p * part, (p + 1) * part)
        out_ref[at, :] = template_ref[at, :] - template_rate * total / subjects


def over_subjects(values):
    count = lax.axis_size("subj")
    return [values] + [
        lax.ppermute(values, "subj", [(i, i ^ d) for i in range(count)]) for d in range(1, count)
    ]


def swap_near(values):
    return lax.ppermute(values, "slab", [(i, i ^ 1) for i in range(lax.axis_size("slab"))])


def swap_far(values):
    count = lax.axis_size("slab")
    return lax.ppermute(
        values, "slab", [(i, i + 1 if i % 2 else i - 1) for i in range(1, count - 1)]
    )


def clear_pads(ref):
    rows = ref.shape[-2] - 2 * PAD
    zeros = jnp.zeros(ref.shape[:-2] + (PAD, ref.shape[-1]), ref.dtype)
    ref[..., :PAD, :] = zeros
    ref[..., PAD + rows :, :] = zeros


def plane_of(ref, *at, step=0):
    rows = ref.shape[-2] - 2 * PAD
    return ref[(*at, slice(PAD + step, PAD + step + rows), slice(None))]


def sides(odd, near, far):
    return jnp.where(odd, near, far), jnp.where(odd, far, near)


def step_weights(coefs, p):
    center = plane_of(coefs, p)
    lane = lax.broadcasted_iota(jnp.int32, center.shape, 1)
    scale = 0.5 * diffusion_dt
    last = center.shape[1] - 1
    right = center + jnp.where(lane == last, 0.0, turned(center, -1))
    left = center + jnp.where(lane == 0, 0.0, turned(center, 1))
    others = [
        center + near
        for near in (
            plane_of(coefs, p, step=1),
            plane_of(coefs, p, step=-1),
            plane_of(coefs, p + 1),
            plane_of(coefs, p - 1),
        )
    ]
    total = right + left
    for face in others:
        total = total + face
    return [
        1.0 - scale * total,
        jnp.where(lane == last, 0.0, scale * right),
        jnp.where(lane == 0, 0.0, scale * left),
    ] + [scale * face for face in others]


def all_weights(coefs):
    return [step_weights(coefs, p) for p in range(1, coefs.shape[0] - 1)]


def stepped(fields, a, low, high, weights):
    planes = fields.shape[1]
    column = [low] + [plane_of(fields, a, p) for p in range(planes)] + [high]
    later = []
    for p in range(planes):
        values = [
            turned(column[p + 1], -1),
            turned(column[p + 1], 1),
            plane_of(fields, a, p, step=1),
            plane_of(fields, a, p, step=-1),
            column[p + 2],
            column[p],
        ]
        total = weights[p][0] * column[p + 1]
        for weight, value in zip(weights[p][1:], values):
            total = total + weight * value
        later.append(total)
    return later


def by_side(odd, pairs):
    copies = [
        (
            [pltpu.make_async_copy(near, low, sems[0]), pltpu.make_async_copy(far, high, sems[1])],
            [pltpu.make_async_copy(near, high, sems[0]), pltpu.make_async_copy(far, low, sems[1])],
        )
        for near, far, low, high, sems in pairs
    ]

    @pl.when(odd)
    def _():
        for when_odd, _ in copies:
            for copy in when_odd:
                copy.start()

    @pl.when(jnp.logical_not(odd))
    def _():
        for _, when_even in copies:
            for copy in when_even:
                copy.start()

    return [copy for when_odd, _ in copies for copy in when_odd]


def force_kernel(
    place_ref,
    velocity_ref,
    images_ref,
    stiffness_ref,
    warped_ref,
    edge_near_ref,
    edge_far_ref,
    warped_near_ref,
    warped_far_ref,
    field_ref,
    coefs_ref,
    near_ref,
    far_ref,
    velocity,
    images,
    warped,
    fields,
    outer,
    sem,
):
    parts, planes, rows = velocity.shape[:3]
    odd = place_ref[0] == 1
    body = slice(PAD, PAD + rows)
    within, every = pl.ds(PAD, rows), pl.ds(0, parts)
    low, mid, high = pl.ds(0, 1), pl.ds(1, planes), pl.ds(planes + 1, 1)
    copies = [
        pltpu.make_async_copy(stiffness_ref, coefs_ref.at[mid, within], sem.at[0]),
        pltpu.make_async_copy(images_ref, images.at[mid], sem.at[1]),
        pltpu.make_async_copy(velocity_ref, velocity, sem.at[2]),
    ]
    for copy in copies:
        copy.start()
    copies += by_side(
        odd,
        [
            (
                edge_near_ref.at[parts],
                edge_far_ref.at[parts],
                coefs_ref.at[low, within],
                coefs_ref.at[high, within],
                (sem.at[3], sem.at[4]),
            ),
            (
                edge_near_ref.at[parts + 1],
                edge_far_ref.at[parts + 1],
                images.at[low],
                images.at[high],
                (sem.at[5], sem.at[6]),
            ),
            (
                edge_near_ref.at[every],
                edge_far_ref.at[every],
                outer.at[:, low],
                outer.at[:, pl.ds(1, 1)],
                (sem.at[7], sem.at[8]),
            ),
        ],
    )
    for ref in (field_ref, fields, coefs_ref, warped):
        clear_pads(ref)
    for p in range(2):
        warped[p, body, :], warped[planes + 2 + p, body, :] = sides(
            odd, warped_near_ref[p], warped_far_ref[p]
        )
    for p in range(planes):
        warped[p + 2, body, :] = warped_ref[p]
    lane = lax.broadcasted_iota(jnp.int32, (rows, LANES), 1)
    right = jnp.where(lane == LANES - 1, 0.0, 0.5 * force_step)
    left = jnp.where(lane == 0, 0.0, 0.5 * force_step)

    def forces(p, image):
        here = plane_of(warped, p + 1)
        mismatch = here - image
        half = (0.5 * force_step) * mismatch
        return [
            mismatch * (right * turned(here, -1) - left * turned(here, 1)),
            half * (plane_of(warped, p + 1, step=1) - plane_of(warped, p + 1, step=-1)),
            half * (plane_of(warped, p + 2) - plane_of(warped, p)),
        ]

    for copy in (copies[0], copies[3], copies[4]):
        copy.wait()
    weights = all_weights(coefs_ref)
    for copy in copies[1:3] + copies[5:]:
        copy.wait()
    for p in range(planes + 2):
        force = forces(p, images[p])
        for a in range(parts):
            if p == 0:
                outer[a, 0] = outer[a, 0] - force[a]
            elif p == planes + 1:
                outer[a, 1] = outer[a, 1] - force[a]
            else:
                fields[a, p - 1, body, :] = velocity[a, p - 1] - force[a]
    for a in range(parts):
        later = stepped(fields, a, outer[a, 0], outer[a, 1], weights)
        for p in range(planes):
            field_ref[a, p, body, :] = later[p]
        near_ref[a, 0], far_ref[a, 0] = sides(odd, later[0], later[-1])


def last_kernel(
    place_ref,
    field_ref,
    coefs_ref,
    near_ref,
    far_ref,
    out_ref,
    done,
    sem,
):
    parts, planes = done.shape[:2]
    odd = place_ref[0] == 1
    weights = all_weights(coefs_ref)
    writes = [pltpu.make_async_copy(done.at[a], out_ref.at[a], sem.at[a]) for a in range(parts)]
    for a in range(parts):
        later = stepped(field_ref, a, *sides(odd, near_ref[a, 0], far_ref[a, 0]), weights)
        for p in range(planes):
            done[a, p] = later[p]
        writes[a].start()
    for copy in writes:
        copy.wait()


def per_device(template, images, velocity, stiffness, send_rows, ref_slot, columns, weights):
    f32, bf16 = jnp.float32, jnp.bfloat16
    shape = jax.ShapeDtypeStruct
    slabs = lax.axis_size("slab")
    subjects = lax.axis_size("subj")
    me = lax.axis_index("subj").astype(jnp.int32).reshape(1)
    slab = lax.axis_index("slab")
    odd = slab % 2 == 1
    place = odd.astype(jnp.int32).reshape(1)
    capacity = send_rows.shape[3]
    rows, width = template.shape
    planes = rows // YR
    parts = velocity.shape[1]
    each = ref_slot.shape[2]
    terms = rows * each
    slots = slabs * capacity
    grid = (planes, YR, width)
    velocity_grid = velocity[0].reshape((parts,) + grid)
    images_grid = images[0].reshape(grid)
    coef_grid = stiffness.reshape(grid)
    dma = pltpu.SemaphoreType.DMA

    sending = call(
        send_kernel,
        shape((slots, width), f32),
        send_rows[0, 0],
        template,
        far=(0, 1),
        scratch=(pltpu.VMEM((slabs, capacity), jnp.int32), pltpu.VMEM((rows, width), f32), dma((2,))),
    )
    received = lax.all_to_all(sending, "slab", split_axis=0, concat_axis=0, tiled=True)

    chunks = 4
    moved_shape = (chunks, each, len(OFFSETS), rows // chunks, width)
    edge_shape = (parts + 2, 1, YR, width)
    moved, edge_near, edge_far = call(
        prepare_kernel,
        (shape(moved_shape, bf16), shape(edge_shape, f32), shape(edge_shape, f32)),
        place,
        columns.reshape(terms, width),
        weights.reshape(terms, width),
        velocity_grid,
        coef_grid,
        images_grid,
        smem=(0,),
        far=(1, 2, 3, 4, 5),
        out_far=(0, 1, 2),
        scratch=(
            pltpu.VMEM((terms, width), jnp.int32),
            pltpu.VMEM((terms, width), bf16),
            pltpu.VMEM((terms // chunks, width), f32),
            pltpu.VMEM(moved_shape, bf16),
            pltpu.VMEM((parts + 2,) + grid, f32),
            dma((2 * chunks,)),
            dma((chunks + 2,)),
            dma((3,)),
        ),
    )
    edge_far, edge_near = swap_far(edge_far), swap_near(edge_near)

    warped, sent = call(
        functools.partial(warp_kernel, slabs, subjects),
        (shape((rows, width), f32), shape((slots, width), f32)),
        ref_slot[0].T,
        received,
        moved,
        images[0],
        far=(2, 3),
        scratch=(
            pltpu.VMEM((rows, width), f32),
            pltpu.VMEM(moved_shape, bf16),
            pltpu.VMEM((each, rows, width), f32),
            pltpu.VMEM((each, rows, 2 * width), bf16),
            dma,
            dma((chunks,)),
        ),
    )
    returned = lax.all_to_all(sent, ("subj", "slab"), split_axis=0, concat_axis=0, tiled=True)

    own_rows, warped = lax.optimization_barrier((send_rows[0, 0], warped))
    all_rows = over_subjects(own_rows)
    warped_grid = warped.reshape(grid)
    warped_far, warped_near = swap_far(warped_grid), swap_near(warped_grid)

    high = YR + 2 * PAD
    field, coefs, field_near, field_far = call(
        force_kernel,
        (
            shape((parts, planes, high, width), f32),
            shape((planes + 2, high, width), f32),
            shape((parts, 1, YR, width), f32),
            shape((parts, 1, YR, width), f32),
        ),
        place,
        velocity_grid,
        images_grid,
        coef_grid,
        warped_grid,
        edge_near,
        edge_far,
        warped_near,
        warped_far,
        smem=(0,),
        far=(1, 2, 3, 5, 6),
        scratch=(
            pltpu.VMEM((parts,) + grid, f32),
            pltpu.VMEM((planes + 2, YR, width), f32),
            pltpu.VMEM((planes + 4, high, width), f32),
            pltpu.VMEM((parts, planes, high, width), f32),
            pltpu.VMEM((parts, 2, YR, width), f32),
            dma((9,)),
        ),
    )
    field_far, field_near, *all_rows = lax.optimization_barrier((field_far, field_near, *all_rows))
    field_far, field_near = swap_far(field_far), swap_near(field_near)

    part = call(
        functools.partial(collect_kernel, subjects),
        shape((rows // subjects, width), f32),
        me,
        returned,
        *all_rows,
        smem=(0,),
    )
    pieces = over_subjects(part)
    field = call(
        last_kernel,
        shape((parts,) + grid, f32),
        place,
        field,
        coefs,
        field_near,
        field_far,
        smem=(0,),
        out_far=(0,),
        scratch=(pltpu.VMEM((parts,) + grid, f32), dma((parts,))),
    )
    field, *pieces = lax.optimization_barrier((field, *pieces))
    template_out = call(
        functools.partial(update_kernel, subjects),
        shape((rows, width), f32),
        me,
        template,
        *pieces,
        smem=(0,),
    )
    velocity_out = field.reshape(parts, rows, width)[None]
    return (template_out, velocity_out)


def solution(mesh):
    return jax.shard_map(
        per_device,
        mesh=mesh,
        in_specs=(
            P("slab", None),
            P("subj", "slab", None),
            P("subj", None, "slab", None),
            P("slab", None),
            P("subj", "slab", None, None),
            P("subj", "slab", None),
            P("subj", "slab", None, None),
            P("subj", "slab", None, None),
        ),
        out_specs=(P("slab", None), P("subj", None, "slab", None)),
        check_vma=False,
    )
```

```python
import functools

import jax
import jax.numpy as jnp
from jax import lax
from jax.experimental import pallas as pl
from jax.experimental.pallas import tpu as pltpu
from jax.sharding import PartitionSpec as P

YR = 256
LANES = 128
PAD = 8
KEPT = 1
OFFSETS = (0, -2, -1, 1, 2)


force_step = 1.0
diffusion_dt = 0.16
template_rate = 2.0

VMEM_LIMIT = 40 * 1024 * 1024


def call(kernel, out_shape, *args, scratch=(), smem=(), far=(), out_far=()):
    many = isinstance(out_shape, tuple)
    shapes = [
        pltpu.HBM(s.shape, s.dtype) if i in out_far else s
        for i, s in enumerate(out_shape if many else (out_shape,))
    ]
    spaces = [pltpu.HBM if i in out_far else pltpu.VMEM for i in range(len(shapes))]
    specs = [pl.BlockSpec(memory_space=space) for space in spaces]
    return pl.pallas_call(
        kernel,
        out_shape=tuple(shapes) if many else shapes[0],
        in_specs=[
            pl.BlockSpec(
                memory_space=pltpu.SMEM if i in smem else pltpu.HBM if i in far else pltpu.VMEM
            )
            for i in range(len(args))
        ],
        out_specs=tuple(specs) if many else specs[0],
        scratch_shapes=scratch,
        compiler_params=pltpu.CompilerParams(vmem_limit_bytes=VMEM_LIMIT),
    )(
        *[
            pltpu.with_memory_space_constraint(arg, pltpu.HBM) if i in far else arg
            for i, arg in enumerate(args)
        ]
    )


def halves(values):
    high = values.astype(jnp.bfloat16)
    low = (values - high.astype(jnp.float32)).astype(jnp.bfloat16)
    return jnp.concatenate([high, low], axis=1)


def joined(pair):
    width = pair.shape[1] // 2
    return pair[:, :width] + pair[:, width:]


def turned(values, shift):
    shift %= values.shape[1]
    return pltpu.roll(values, shift, axis=1) if shift else values


def dot(left, right):
    return jnp.dot(left, right, preferred_element_type=jnp.float32)


def one_hot(matches):
    return jnp.where(matches, 1.0, 0.0).astype(jnp.bfloat16)


def send_kernel(send_ref, template_ref, out_ref, send, template, sem):
    slabs, capacity = send.shape
    rows = template.shape[0]
    copies = [
        pltpu.make_async_copy(send_ref, send, sem.at[0]),
        pltpu.make_async_copy(template_ref, template, sem.at[1]),
    ]
    for copy in copies:
        copy.start()
    copies[0].wait()
    padded = jnp.concatenate([send[...], jnp.zeros((slabs, LANES - capacity), jnp.int32)], axis=1)
    columns = padded.T
    number = lax.broadcasted_iota(jnp.int32, (capacity, rows), 1)
    chosen = [
        one_hot(jnp.broadcast_to(columns[:capacity, k : k + 1], (capacity, rows)) == number)
        for k in range(slabs)
    ]
    copies[1].wait()
    pair = halves(template[...])
    for k in range(slabs):
        out_ref[k * capacity : (k + 1) * capacity, :] = joined(dot(chosen[k], pair))


def prepare_kernel(
    place_ref,
    columns_ref,
    weights_ref,
    velocity_ref,
    stiffness_ref,
    images_ref,
    kept_ref,
    moved_ref,
    near_ref,
    far_ref,
    columns,
    weights,
    plain,
    moved,
    edge,
    in_sem,
    out_sem,
    edge_sem,
):
    held = kept_ref.shape[0]
    each, count, some, width = moved.shape[1:]
    chunks = held + moved.shape[0]
    odd = place_ref[0]
    near_plane, far_plane = pl.ds((edge.shape[1] - 1) * (1 - odd), 1), pl.ds((edge.shape[1] - 1) * odd, 1)
    step = some * each
    parts = velocity_ref.shape[0]
    reads = [
        (
            pltpu.make_async_copy(
                columns_ref.at[pl.ds(i * step, step)], columns.at[pl.ds(i * step, step)], in_sem.at[i]
            ),
            pltpu.make_async_copy(
                weights_ref.at[pl.ds(i * step, step)],
                weights.at[pl.ds(i * step, step)],
                in_sem.at[chunks + i],
            ),
        )
        for i in range(chunks)
    ]
    edges = [
        pltpu.make_async_copy(velocity_ref, edge.at[pl.ds(0, parts)], edge_sem.at[0]),
        pltpu.make_async_copy(stiffness_ref, edge.at[parts], edge_sem.at[1]),
        pltpu.make_async_copy(images_ref, edge.at[parts + 1], edge_sem.at[2]),
    ]
    writes = [
        pltpu.make_async_copy(moved.at[i], moved_ref.at[i], out_sem.at[i])
        for i in range(chunks - held)
    ]
    edge_writes = [
        pltpu.make_async_copy(edge.at[:, near_plane], near_ref, out_sem.at[chunks]),
        pltpu.make_async_copy(edge.at[:, far_plane], far_ref, out_sem.at[chunks + 1]),
    ]
    for copy in reads[0]:
        copy.start()
    for copy in edges:
        copy.start()
    for pair in reads[1:]:
        for copy in pair:
            copy.start()
    cell = lax.broadcasted_iota(jnp.int32, (some, width), 1)
    for i in range(chunks):
        at = i * step
        for copy in reads[i]:
            copy.wait()
        plain[...] = weights[at : at + step, :].astype(jnp.float32)
        for b in range(each):
            offset = columns[pl.ds(at + b, some, stride=each), :] - cell
            here = plain[pl.ds(b, some, stride=each), :]
            for j, o in enumerate(OFFSETS):
                kept = jnp.where(offset == o, here, 0.0)
                target, at_chunk = (moved, i) if i < chunks - held else (kept_ref, i - chunks + held)
                target[at_chunk, b, j] = turned(kept, o).astype(jnp.bfloat16)
        if i < chunks - held:
            writes[i].start()
        if i == 0:
            for copy in edges:
                copy.wait()
            for copy in edge_writes:
                copy.start()
    for copy in writes + edge_writes:
        copy.wait()


def warp_kernel(
    slabs,
    subjects,
    slot_ref,
    received_ref,
    kept_ref,
    moved_ref,
    images_ref,
    warped_ref,
    sent_ref,
    images,
    moved,
    picked,
    placed,
    first_sem,
    moved_sem,
):
    slots, width = received_ref.shape
    each, count, some = moved.shape[1:4]
    held = kept_ref.shape[0]
    loaded = moved.shape[0]
    chunks = loaded + held
    rows = chunks * some
    block = width // subjects
    group = slots // subjects
    capacity = slots // slabs
    held = capacity // subjects
    first = pltpu.make_async_copy(images_ref, images, first_sem)
    moves = [
        pltpu.make_async_copy(moved_ref.at[i], moved.at[i], moved_sem.at[i]) for i in range(loaded)
    ]
    for copy in [first] + moves:
        copy.start()
    slot = slot_ref[...]
    slot_wide = jnp.concatenate([slot, jnp.zeros((LANES - each, rows), jnp.int32)], axis=0).T
    inner = slot % capacity
    packed = (inner // held) * group + (slot // capacity) * held + inner % held
    lane = lax.broadcasted_iota(jnp.int32, (rows, LANES), 1)
    number = lax.broadcasted_iota(jnp.int32, (slots, rows), 0)
    pair = halves(received_ref[...])
    for b in range(each):
        wide = jnp.broadcast_to(slot_wide[:, b : b + 1], (rows, LANES))
        pick = jnp.concatenate(
            [one_hot(wide == lane + t * LANES) for t in range(slots // LANES)], axis=1
        )
        picked[b] = joined(dot(pick, pair))
    first.wait()
    for i in list(range(loaded, chunks)) + list(range(loaded)):
        if i == 0:
            for copy in moves:
                copy.wait()
        here, h = (moved, i) if i < loaded else (kept_ref, i - loaded)
        at = slice(i * some, (i + 1) * some)
        sums = [jnp.zeros((some, width), jnp.float32) for _ in OFFSETS]
        for b in range(each):
            values = picked[b, at, :]
            for j in range(count):
                sums[j] = sums[j] + here[h, b, j].astype(jnp.float32) * values
        warped = sums[0]
        for j, o in enumerate(OFFSETS[1:], 1):
            warped = warped + turned(sums[j], -o)
        warped_ref[at, :] = warped
        mismatch = warped - images[at, :]
        ahead = [turned(mismatch, o) for o in OFFSETS]
        for b in range(each):
            total = here[h, b, 0].astype(jnp.float32) * ahead[0]
            for j in range(1, count):
                total = total + here[h, b, j].astype(jnp.float32) * ahead[j]
            placed[b, at, :] = halves(total)
    total = jnp.zeros((slots, 2 * width), jnp.float32)
    for b in range(each):
        drop = one_hot(jnp.broadcast_to(packed[b : b + 1], (slots, rows)) == number)
        total = total + dot(drop, placed[b])
    total = joined(total)
    place = lax.broadcasted_iota(jnp.int32, (group, width), 1) // block
    groups = [total[q * group : (q + 1) * group, :] for q in range(subjects)]
    for p in range(subjects):
        out = jnp.zeros((group, width), jnp.float32)
        for q in range(subjects):
            out = jnp.where(place == q, turned(groups[q], (q - p) * block), out)
        sent_ref[p * group : (p + 1) * group, :] = out


def collect_kernel(subjects, me_ref, returned_ref, *refs):
    row_refs, out_ref = refs[:-1], refs[-1]
    slots, width = returned_ref.shape
    slabs, capacity = row_refs[0].shape
    rows = out_ref.shape[0] * subjects
    block = width // subjects
    group = slots // subjects
    held = capacity // subjects
    me = me_ref[0]
    pair = halves(
        jnp.concatenate(
            [
                returned_ref[pl.ds(pl.multiple_of((me ^ d) * group, group), group), :]
                for d in range(subjects)
            ]
        )
    )
    lane = lax.broadcasted_iota(jnp.int32, (slabs, LANES), 1)
    slab = lax.broadcasted_iota(jnp.int32, (slabs, LANES), 0)
    fill = jnp.zeros((slabs, LANES - capacity), jnp.int32)
    wanted = []
    for q in range(subjects):
        chunks = [jnp.zeros((1, LANES), jnp.int32) for _ in range(slots // LANES)]
        for d in range(subjects):
            spread = jnp.concatenate([row_refs[d][...], fill], axis=1)
            spread = turned(spread, d * group - q * held)
            spread = pltpu.roll(spread, 0, axis=1, stride=held, stride_axis=0)
            first = (d * group) % LANES + slab * held
            kept = jnp.where((lane >= first) & (lane < first + held), spread, 0)
            chunks[d * group // LANES] += jnp.sum(kept, axis=0, keepdims=True)
        wanted.append(jnp.concatenate(chunks, axis=1))
    number = lax.broadcasted_iota(jnp.int32, (rows, slots), 0)
    place = lax.broadcasted_iota(jnp.int32, (rows, width), 1) // block
    kept = jnp.zeros((rows, width), jnp.float32)
    for q in range(subjects):
        match = jnp.broadcast_to(wanted[q], (rows, slots)) == number
        kept = jnp.where(place == q, joined(dot(one_hot(match), pair)), kept)
    turn = block
    while turn < width:
        kept = kept + turned(kept, turn)
        turn *= 2
    part = rows // subjects
    out = jnp.zeros((part, width), jnp.float32)
    for p in range(subjects):
        out = jnp.where(place[:part] == p, kept[p * part : (p + 1) * part], out)
    out_ref[...] = out


def update_kernel(subjects, me_ref, template_ref, *refs):
    parts, out_ref = refs[:-1], refs[-1]
    rows, width = template_ref.shape
    block = width // subjects
    part = rows // subjects
    me = me_ref[0]
    place = lax.broadcasted_iota(jnp.int32, (part, width), 1) // block
    for p in range(subjects):
        total = jnp.zeros((part, width), jnp.float32)
        for d in range(subjects):
            source = me ^ d
            turn = lax.rem((source - p) * block + width, width)
            total = jnp.where(place == source, pltpu.roll(parts[d][...], turn, axis=1), total)
        at = slice(p * part, (p + 1) * part)
        out_ref[at, :] = template_ref[at, :] - template_rate * total / subjects


def over_subjects(values):
    count = lax.axis_size("subj")
    return [values] + [
        lax.ppermute(values, "subj", [(i, i ^ d) for i in range(count)]) for d in range(1, count)
    ]


def swap_near(values):
    return lax.ppermute(values, "slab", [(i, i ^ 1) for i in range(lax.axis_size("slab"))])


def swap_far(values):
    count = lax.axis_size("slab")
    return lax.ppermute(
        values, "slab", [(i, i + 1 if i % 2 else i - 1) for i in range(1, count - 1)]
    )


def clear_pads(ref):
    rows = ref.shape[-2] - 2 * PAD
    zeros = jnp.zeros(ref.shape[:-2] + (PAD, ref.shape[-1]), ref.dtype)
    ref[..., :PAD, :] = zeros
    ref[..., PAD + rows :, :] = zeros


def plane_of(ref, *at, step=0):
    rows = ref.shape[-2] - 2 * PAD
    return ref[(*at, slice(PAD + step, PAD + step + rows), slice(None))]


def sides(odd, near, far):
    return jnp.where(odd, near, far), jnp.where(odd, far, near)


def step_weights(coefs, p):
    center = plane_of(coefs, p)
    lane = lax.broadcasted_iota(jnp.int32, center.shape, 1)
    scale = 0.5 * diffusion_dt
    last = center.shape[1] - 1
    right = center + jnp.where(lane == last, 0.0, turned(center, -1))
    left = center + jnp.where(lane == 0, 0.0, turned(center, 1))
    others = [
        center + near
        for near in (
            plane_of(coefs, p, step=1),
            plane_of(coefs, p, step=-1),
            plane_of(coefs, p + 1),
            plane_of(coefs, p - 1),
        )
    ]
    total = right + left
    for face in others:
        total = total + face
    return [
        1.0 - scale * total,
        jnp.where(lane == last, 0.0, scale * right),
        jnp.where(lane == 0, 0.0, scale * left),
    ] + [scale * face for face in others]


def all_weights(coefs):
    return [step_weights(coefs, p) for p in range(1, coefs.shape[0] - 1)]


def stepped(fields, a, low, high, weights):
    planes = fields.shape[1]
    column = [low] + [plane_of(fields, a, p) for p in range(planes)] + [high]
    later = []
    for p in range(planes):
        values = [
            turned(column[p + 1], -1),
            turned(column[p + 1], 1),
            plane_of(fields, a, p, step=1),
            plane_of(fields, a, p, step=-1),
            column[p + 2],
            column[p],
        ]
        total = weights[p][0] * column[p + 1]
        for weight, value in zip(weights[p][1:], values):
            total = total + weight * value
        later.append(total)
    return later


def by_side(odd, pairs):
    copies = [
        (
            [pltpu.make_async_copy(near, low, sems[0]), pltpu.make_async_copy(far, high, sems[1])],
            [pltpu.make_async_copy(near, high, sems[0]), pltpu.make_async_copy(far, low, sems[1])],
        )
        for near, far, low, high, sems in pairs
    ]

    @pl.when(odd)
    def _():
        for when_odd, _ in copies:
            for copy in when_odd:
                copy.start()

    @pl.when(jnp.logical_not(odd))
    def _():
        for _, when_even in copies:
            for copy in when_even:
                copy.start()

    return [copy for when_odd, _ in copies for copy in when_odd]


def force_kernel(
    place_ref,
    velocity_ref,
    images_ref,
    stiffness_ref,
    warped_ref,
    edge_near_ref,
    edge_far_ref,
    warped_near_ref,
    warped_far_ref,
    field_ref,
    coefs_ref,
    near_ref,
    far_ref,
    velocity,
    images,
    warped,
    fields,
    outer,
    sem,
):
    parts, planes, rows = velocity.shape[:3]
    odd = place_ref[0] == 1
    body = slice(PAD, PAD + rows)
    within, every = pl.ds(PAD, rows), pl.ds(0, parts)
    low, mid, high = pl.ds(0, 1), pl.ds(1, planes), pl.ds(planes + 1, 1)
    copies = [
        pltpu.make_async_copy(stiffness_ref, coefs_ref.at[mid, within], sem.at[0]),
        pltpu.make_async_copy(images_ref, images.at[mid], sem.at[1]),
        pltpu.make_async_copy(velocity_ref, velocity, sem.at[2]),
    ]
    for copy in copies:
        copy.start()
    copies += by_side(
        odd,
        [
            (
                edge_near_ref.at[parts],
                edge_far_ref.at[parts],
                coefs_ref.at[low, within],
                coefs_ref.at[high, within],
                (sem.at[3], sem.at[4]),
            ),
            (
                edge_near_ref.at[parts + 1],
                edge_far_ref.at[parts + 1],
                images.at[low],
                images.at[high],
                (sem.at[5], sem.at[6]),
            ),
            (
                edge_near_ref.at[every],
                edge_far_ref.at[every],
                outer.at[:, low],
                outer.at[:, pl.ds(1, 1)],
                (sem.at[7], sem.at[8]),
            ),
        ],
    )
    for ref in (field_ref, fields, coefs_ref, warped):
        clear_pads(ref)
    for p in range(2):
        warped[p, body, :], warped[planes + 2 + p, body, :] = sides(
            odd, warped_near_ref[p], warped_far_ref[p]
        )
    for p in range(planes):
        warped[p + 2, body, :] = warped_ref[p]
    lane = lax.broadcasted_iota(jnp.int32, (rows, LANES), 1)
    right = jnp.where(lane == LANES - 1, 0.0, 0.5 * force_step)
    left = jnp.where(lane == 0, 0.0, 0.5 * force_step)

    def forces(p, image):
        here = plane_of(warped, p + 1)
        mismatch = here - image
        half = (0.5 * force_step) * mismatch
        return [
            mismatch * (right * turned(here, -1) - left * turned(here, 1)),
            half * (plane_of(warped, p + 1, step=1) - plane_of(warped, p + 1, step=-1)),
            half * (plane_of(warped, p + 2) - plane_of(warped, p)),
        ]

    for copy in (copies[0], copies[3], copies[4]):
        copy.wait()
    weights = all_weights(coefs_ref)
    for copy in copies[1:3] + copies[5:]:
        copy.wait()
    for p in range(planes + 2):
        force = forces(p, images[p])
        for a in range(parts):
            if p == 0:
                outer[a, 0] = outer[a, 0] - force[a]
            elif p == planes + 1:
                outer[a, 1] = outer[a, 1] - force[a]
            else:
                fields[a, p - 1, body, :] = velocity[a, p - 1] - force[a]
    for a in range(parts):
        later = stepped(fields, a, outer[a, 0], outer[a, 1], weights)
        for p in range(planes):
            field_ref[a, p, body, :] = later[p]
        near_ref[a, 0], far_ref[a, 0] = sides(odd, later[0], later[-1])


def last_kernel(
    place_ref,
    field_ref,
    coefs_ref,
    near_ref,
    far_ref,
    out_ref,
    done,
    sem,
):
    parts, planes = done.shape[:2]
    odd = place_ref[0] == 1
    weights = all_weights(coefs_ref)
    writes = [pltpu.make_async_copy(done.at[a], out_ref.at[a], sem.at[a]) for a in range(parts)]
    for a in range(parts):
        later = stepped(field_ref, a, *sides(odd, near_ref[a, 0], far_ref[a, 0]), weights)
        for p in range(planes):
            done[a, p] = later[p]
        writes[a].start()
    for copy in writes:
        copy.wait()


def per_device(template, images, velocity, stiffness, send_rows, ref_slot, columns, weights):
    f32, bf16 = jnp.float32, jnp.bfloat16
    shape = jax.ShapeDtypeStruct
    slabs = lax.axis_size("slab")
    subjects = lax.axis_size("subj")
    me = lax.axis_index("subj").astype(jnp.int32).reshape(1)
    slab = lax.axis_index("slab")
    odd = slab % 2 == 1
    place = odd.astype(jnp.int32).reshape(1)
    capacity = send_rows.shape[3]
    rows, width = template.shape
    planes = rows // YR
    parts = velocity.shape[1]
    each = ref_slot.shape[2]
    terms = rows * each
    slots = slabs * capacity
    grid = (planes, YR, width)
    velocity_grid = velocity[0].reshape((parts,) + grid)
    images_grid = images[0].reshape(grid)
    coef_grid = stiffness.reshape(grid)
    dma = pltpu.SemaphoreType.DMA

    sending = call(
        send_kernel,
        shape((slots, width), f32),
        send_rows[0, 0],
        template,
        far=(0, 1),
        scratch=(pltpu.VMEM((slabs, capacity), jnp.int32), pltpu.VMEM((rows, width), f32), dma((2,))),
    )
    received = lax.all_to_all(sending, "slab", split_axis=0, concat_axis=0, tiled=True)

    chunks = 4
    kept_chunks = KEPT
    chunk_shape = (each, len(OFFSETS), rows // chunks, width)
    kept_shape, moved_shape = (kept_chunks,) + chunk_shape, (chunks - kept_chunks,) + chunk_shape
    edge_shape = (parts + 2, 1, YR, width)
    kept, moved, edge_near, edge_far = call(
        prepare_kernel,
        (
            shape(kept_shape, bf16),
            shape(moved_shape, bf16),
            shape(edge_shape, f32),
            shape(edge_shape, f32),
        ),
        place,
        columns.reshape(terms, width),
        weights.reshape(terms, width),
        velocity_grid,
        coef_grid,
        images_grid,
        smem=(0,),
        far=(1, 2, 3, 4, 5),
        out_far=(1, 2, 3),
        scratch=(
            pltpu.VMEM((terms, width), jnp.int32),
            pltpu.VMEM((terms, width), bf16),
            pltpu.VMEM((terms // chunks, width), f32),
            pltpu.VMEM(moved_shape, bf16),
            pltpu.VMEM((parts + 2,) + grid, f32),
            dma((2 * chunks,)),
            dma((chunks + 2,)),
            dma((3,)),
        ),
    )
    edge_far, edge_near = swap_far(edge_far), swap_near(edge_near)

    warped, sent = call(
        functools.partial(warp_kernel, slabs, subjects),
        (shape((rows, width), f32), shape((slots, width), f32)),
        ref_slot[0].T,
        received,
        kept,
        moved,
        images[0],
        far=(3, 4),
        scratch=(
            pltpu.VMEM((rows, width), f32),
            pltpu.VMEM(moved_shape, bf16),
            pltpu.VMEM((each, rows, width), f32),
            pltpu.VMEM((each, rows, 2 * width), bf16),
            dma,
            dma((chunks - kept_chunks,)),
        ),
    )
    returned = lax.all_to_all(sent, ("subj", "slab"), split_axis=0, concat_axis=0, tiled=True)

    own_rows, warped = lax.optimization_barrier((send_rows[0, 0], warped))
    all_rows = over_subjects(own_rows)
    warped_grid = warped.reshape(grid)
    warped_far, warped_near = swap_far(warped_grid), swap_near(warped_grid)

    high = YR + 2 * PAD
    field, coefs, field_near, field_far = call(
        force_kernel,
        (
            shape((parts, planes, high, width), f32),
            shape((planes + 2, high, width), f32),
            shape((parts, 1, YR, width), f32),
            shape((parts, 1, YR, width), f32),
        ),
        place,
        velocity_grid,
        images_grid,
        coef_grid,
        warped_grid,
        edge_near,
        edge_far,
        warped_near,
        warped_far,
        smem=(0,),
        far=(1, 2, 3, 5, 6),
        scratch=(
            pltpu.VMEM((parts,) + grid, f32),
            pltpu.VMEM((planes + 2, YR, width), f32),
            pltpu.VMEM((planes + 4, high, width), f32),
            pltpu.VMEM((parts, planes, high, width), f32),
            pltpu.VMEM((parts, 2, YR, width), f32),
            dma((9,)),
        ),
    )
    field_far, field_near, *all_rows = lax.optimization_barrier((field_far, field_near, *all_rows))
    field_far, field_near = swap_far(field_far), swap_near(field_near)

    part = call(
        functools.partial(collect_kernel, subjects),
        shape((rows // subjects, width), f32),
        me,
        returned,
        *all_rows,
        smem=(0,),
    )
    pieces = over_subjects(part)
    field = call(
        last_kernel,
        shape((parts,) + grid, f32),
        place,
        field,
        coefs,
        field_near,
        field_far,
        smem=(0,),
        out_far=(0,),
        scratch=(pltpu.VMEM((parts,) + grid, f32), dma((parts,))),
    )
    field, *pieces = lax.optimization_barrier((field, *pieces))
    template_out = call(
        functools.partial(update_kernel, subjects),
        shape((rows, width), f32),
        me,
        template,
        *pieces,
        smem=(0,),
    )
    velocity_out = field.reshape(parts, rows, width)[None]
    return (template_out, velocity_out)


def solution(mesh):
    return jax.shard_map(
        per_device,
        mesh=mesh,
        in_specs=(
            P("slab", None),
            P("subj", "slab", None),
            P("subj", None, "slab", None),
            P("slab", None),
            P("subj", "slab", None, None),
            P("subj", "slab", None),
            P("subj", "slab", None, None),
            P("subj", "slab", None, None),
        ),
        out_specs=(P("slab", None), P("subj", None, "slab", None)),
        check_vma=False,
    )
```

```python
import functools

import jax
import jax.numpy as jnp
from jax import lax
from jax.experimental import pallas as pl
from jax.experimental.pallas import tpu as pltpu
from jax.sharding import PartitionSpec as P

YR = 256
LANES = 128
PAD = 8
KEPT = 1
OFFSETS = (0, -2, -1, 1, 2)


force_step = 1.0
diffusion_dt = 0.16
template_rate = 2.0

VMEM_LIMIT = 40 * 1024 * 1024


def call(kernel, out_shape, *args, scratch=(), smem=(), far=(), out_far=()):
    many = isinstance(out_shape, tuple)
    shapes = [
        pltpu.HBM(s.shape, s.dtype) if i in out_far else s
        for i, s in enumerate(out_shape if many else (out_shape,))
    ]
    spaces = [pltpu.HBM if i in out_far else pltpu.VMEM for i in range(len(shapes))]
    specs = [pl.BlockSpec(memory_space=space) for space in spaces]
    return pl.pallas_call(
        kernel,
        out_shape=tuple(shapes) if many else shapes[0],
        in_specs=[
            pl.BlockSpec(
                memory_space=pltpu.SMEM if i in smem else pltpu.HBM if i in far else pltpu.VMEM
            )
            for i in range(len(args))
        ],
        out_specs=tuple(specs) if many else specs[0],
        scratch_shapes=scratch,
        compiler_params=pltpu.CompilerParams(vmem_limit_bytes=VMEM_LIMIT),
    )(
        *[
            pltpu.with_memory_space_constraint(arg, pltpu.HBM) if i in far else arg
            for i, arg in enumerate(args)
        ]
    )


def halves(values):
    high = values.astype(jnp.bfloat16)
    low = (values - high.astype(jnp.float32)).astype(jnp.bfloat16)
    return jnp.concatenate([high, low], axis=1)


def joined(pair):
    width = pair.shape[1] // 2
    return pair[:, :width] + pair[:, width:]


def turned(values, shift):
    shift %= values.shape[1]
    return pltpu.roll(values, shift, axis=1) if shift else values


def dot(left, right):
    return jnp.dot(left, right, preferred_element_type=jnp.float32)


def one_hot(matches):
    return jnp.where(matches, 1.0, 0.0).astype(jnp.bfloat16)


def send_kernel(send_ref, template_ref, out_ref, send, template, sem):
    slabs, capacity = send.shape
    rows = template.shape[0]
    copies = [
        pltpu.make_async_copy(send_ref, send, sem.at[0]),
        pltpu.make_async_copy(template_ref, template, sem.at[1]),
    ]
    for copy in copies:
        copy.start()
    copies[0].wait()
    padded = jnp.concatenate([send[...], jnp.zeros((slabs, LANES - capacity), jnp.int32)], axis=1)
    columns = padded.T
    number = lax.broadcasted_iota(jnp.int32, (capacity, rows), 1)
    chosen = [
        one_hot(jnp.broadcast_to(columns[:capacity, k : k + 1], (capacity, rows)) == number)
        for k in range(slabs)
    ]
    copies[1].wait()
    pair = halves(template[...])
    for k in range(slabs):
        out_ref[k * capacity : (k + 1) * capacity, :] = joined(dot(chosen[k], pair))


def prepare_kernel(
    place_ref,
    columns_ref,
    weights_ref,
    velocity_ref,
    stiffness_ref,
    images_ref,
    kept_ref,
    moved_ref,
    near_ref,
    far_ref,
    columns,
    weights,
    plain,
    moved,
    edge,
    in_sem,
    out_sem,
    edge_sem,
):
    held = kept_ref.shape[0]
    each, count, some, width = moved.shape[1:]
    chunks = held + moved.shape[0]
    odd = place_ref[0]
    near_plane, far_plane = pl.ds((edge.shape[1] - 1) * (1 - odd), 1), pl.ds((edge.shape[1] - 1) * odd, 1)
    step = some * each
    parts = velocity_ref.shape[0]
    reads = [
        (
            pltpu.make_async_copy(
                columns_ref.at[pl.ds(i * step, step)], columns.at[pl.ds(i * step, step)], in_sem.at[i]
            ),
            pltpu.make_async_copy(
                weights_ref.at[pl.ds(i * step, step)],
                weights.at[pl.ds(i * step, step)],
                in_sem.at[chunks + i],
            ),
        )
        for i in range(chunks)
    ]
    edges = [
        pltpu.make_async_copy(velocity_ref, edge.at[pl.ds(0, parts)], edge_sem.at[0]),
        pltpu.make_async_copy(stiffness_ref, edge.at[parts], edge_sem.at[1]),
        pltpu.make_async_copy(images_ref, edge.at[parts + 1], edge_sem.at[2]),
    ]
    writes = [
        pltpu.make_async_copy(moved.at[i], moved_ref.at[i], out_sem.at[i])
        for i in range(chunks - held)
    ]
    edge_writes = [
        pltpu.make_async_copy(edge.at[:, near_plane], near_ref, out_sem.at[chunks]),
        pltpu.make_async_copy(edge.at[:, far_plane], far_ref, out_sem.at[chunks + 1]),
    ]
    for copy in reads[0]:
        copy.start()
    for copy in edges:
        copy.start()
    for pair in reads[1:]:
        for copy in pair:
            copy.start()
    cell = lax.broadcasted_iota(jnp.int32, (some, width), 1)
    for i in range(chunks):
        at = i * step
        for copy in reads[i]:
            copy.wait()
        plain[...] = weights[at : at + step, :].astype(jnp.float32)
        for b in range(each):
            offset = columns[pl.ds(at + b, some, stride=each), :] - cell
            here = plain[pl.ds(b, some, stride=each), :]
            for j, o in enumerate(OFFSETS):
                kept = jnp.where(offset == o, here, 0.0)
                target, at_chunk = (moved, i) if i < chunks - held else (kept_ref, i - chunks + held)
                target[at_chunk, b, j] = turned(kept, o).astype(jnp.bfloat16)
        if i < chunks - held:
            writes[i].start()
        if i == 0:
            for copy in edges:
                copy.wait()
            for copy in edge_writes:
                copy.start()
    for copy in writes + edge_writes:
        copy.wait()


def warp_kernel(
    slabs,
    subjects,
    slot_ref,
    received_ref,
    kept_ref,
    moved_ref,
    images_ref,
    warped_ref,
    sent_ref,
    images,
    moved,
    picked,
    placed,
    first_sem,
    moved_sem,
):
    slots, width = received_ref.shape
    each, count, some = moved.shape[1:4]
    held = kept_ref.shape[0]
    loaded = moved.shape[0]
    chunks = loaded + held
    rows = chunks * some
    block = width // subjects
    group = slots // subjects
    capacity = slots // slabs
    held = capacity // subjects
    first = pltpu.make_async_copy(images_ref, images, first_sem)
    moves = [
        pltpu.make_async_copy(moved_ref.at[i], moved.at[i], moved_sem.at[i]) for i in range(loaded)
    ]
    for copy in [first] + moves:
        copy.start()
    slot = slot_ref[...]
    slot_wide = jnp.concatenate([slot, jnp.zeros((LANES - each, rows), jnp.int32)], axis=0).T
    inner = slot % capacity
    packed = (inner // held) * group + (slot // capacity) * held + inner % held
    lane = lax.broadcasted_iota(jnp.int32, (rows, LANES), 1)
    number = lax.broadcasted_iota(jnp.int32, (slots, rows), 0)
    pair = halves(received_ref[...])
    for b in range(each):
        wide = jnp.broadcast_to(slot_wide[:, b : b + 1], (rows, LANES))
        pick = jnp.concatenate(
            [one_hot(wide == lane + t * LANES) for t in range(slots // LANES)], axis=1
        )
        picked[b] = joined(dot(pick, pair))
    for copy in [first] + moves:
        copy.wait()
    for i in range(chunks):
        here, h = (moved, i) if i < loaded else (kept_ref, i - loaded)
        at = slice(i * some, (i + 1) * some)
        sums = [jnp.zeros((some, width), jnp.float32) for _ in OFFSETS]
        for b in range(each):
            values = picked[b, at, :]
            for j in range(count):
                sums[j] = sums[j] + here[h, b, j].astype(jnp.float32) * values
        warped = sums[0]
        for j, o in enumerate(OFFSETS[1:], 1):
            warped = warped + turned(sums[j], -o)
        warped_ref[at, :] = warped
        mismatch = warped - images[at, :]
        ahead = [turned(mismatch, o) for o in OFFSETS]
        for b in range(each):
            total = here[h, b, 0].astype(jnp.float32) * ahead[0]
            for j in range(1, count):
                total = total + here[h, b, j].astype(jnp.float32) * ahead[j]
            placed[b, at, :] = halves(total)
    total = jnp.zeros((slots, 2 * width), jnp.float32)
    for b in range(each):
        drop = one_hot(jnp.broadcast_to(packed[b : b + 1], (slots, rows)) == number)
        total = total + dot(drop, placed[b])
    total = joined(total)
    place = lax.broadcasted_iota(jnp.int32, (group, width), 1) // block
    groups = [total[q * group : (q + 1) * group, :] for q in range(subjects)]
    for p in range(subjects):
        out = jnp.zeros((group, width), jnp.float32)
        for q in range(subjects):
            out = jnp.where(place == q, turned(groups[q], (q - p) * block), out)
        sent_ref[p * group : (p + 1) * group, :] = out


def collect_kernel(subjects, me_ref, returned_ref, *refs):
    row_refs, out_ref = refs[:-1], refs[-1]
    slots, width = returned_ref.shape
    slabs, capacity = row_refs[0].shape
    rows = out_ref.shape[0] * subjects
    block = width // subjects
    group = slots // subjects
    held = capacity // subjects
    me = me_ref[0]
    pair = halves(
        jnp.concatenate(
            [
                returned_ref[pl.ds(pl.multiple_of((me ^ d) * group, group), group), :]
                for d in range(subjects)
            ]
        )
    )
    lane = lax.broadcasted_iota(jnp.int32, (slabs, LANES), 1)
    slab = lax.broadcasted_iota(jnp.int32, (slabs, LANES), 0)
    fill = jnp.zeros((slabs, LANES - capacity), jnp.int32)
    wanted = []
    for q in range(subjects):
        chunks = [jnp.zeros((1, LANES), jnp.int32) for _ in range(slots // LANES)]
        for d in range(subjects):
            spread = jnp.concatenate([row_refs[d][...], fill], axis=1)
            spread = turned(spread, d * group - q * held)
            spread = pltpu.roll(spread, 0, axis=1, stride=held, stride_axis=0)
            first = (d * group) % LANES + slab * held
            kept = jnp.where((lane >= first) & (lane < first + held), spread, 0)
            chunks[d * group // LANES] += jnp.sum(kept, axis=0, keepdims=True)
        wanted.append(jnp.concatenate(chunks, axis=1))
    number = lax.broadcasted_iota(jnp.int32, (rows, slots), 0)
    place = lax.broadcasted_iota(jnp.int32, (rows, width), 1) // block
    kept = jnp.zeros((rows, width), jnp.float32)
    for q in range(subjects):
        match = jnp.broadcast_to(wanted[q], (rows, slots)) == number
        kept = jnp.where(place == q, joined(dot(one_hot(match), pair)), kept)
    turn = block
    while turn < width:
        kept = kept + turned(kept, turn)
        turn *= 2
    part = rows // subjects
    out = jnp.zeros((part, width), jnp.float32)
    for p in range(subjects):
        out = jnp.where(place[:part] == p, kept[p * part : (p + 1) * part], out)
    out_ref[...] = out


def update_kernel(subjects, me_ref, template_ref, *refs):
    parts, out_ref = refs[:-1], refs[-1]
    rows, width = template_ref.shape
    block = width // subjects
    part = rows // subjects
    me = me_ref[0]
    place = lax.broadcasted_iota(jnp.int32, (part, width), 1) // block
    for p in range(subjects):
        total = jnp.zeros((part, width), jnp.float32)
        for d in range(subjects):
            source = me ^ d
            turn = lax.rem((source - p) * block + width, width)
            total = jnp.where(place == source, pltpu.roll(parts[d][...], turn, axis=1), total)
        at = slice(p * part, (p + 1) * part)
        out_ref[at, :] = template_ref[at, :] - template_rate * total / subjects


def over_subjects(values):
    count = lax.axis_size("subj")
    return [values] + [
        lax.ppermute(values, "subj", [(i, i ^ d) for i in range(count)]) for d in range(1, count)
    ]


def swap_near(values):
    return lax.ppermute(values, "slab", [(i, i ^ 1) for i in range(lax.axis_size("slab"))])


def swap_far(values):
    count = lax.axis_size("slab")
    return lax.ppermute(
        values, "slab", [(i, i + 1 if i % 2 else i - 1) for i in range(1, count - 1)]
    )


def clear_pads(ref):
    rows = ref.shape[-2] - 2 * PAD
    zeros = jnp.zeros(ref.shape[:-2] + (PAD, ref.shape[-1]), ref.dtype)
    ref[..., :PAD, :] = zeros
    ref[..., PAD + rows :, :] = zeros


def plane_of(ref, *at, step=0):
    rows = ref.shape[-2] - 2 * PAD
    return ref[(*at, slice(PAD + step, PAD + step + rows), slice(None))]


def sides(odd, near, far):
    return jnp.where(odd, near, far), jnp.where(odd, far, near)


def step_weights(coefs, p):
    center = plane_of(coefs, p)
    lane = lax.broadcasted_iota(jnp.int32, center.shape, 1)
    scale = 0.5 * diffusion_dt
    last = center.shape[1] - 1
    right = center + jnp.where(lane == last, 0.0, turned(center, -1))
    left = center + jnp.where(lane == 0, 0.0, turned(center, 1))
    others = [
        center + near
        for near in (
            plane_of(coefs, p, step=1),
            plane_of(coefs, p, step=-1),
            plane_of(coefs, p + 1),
            plane_of(coefs, p - 1),
        )
    ]
    total = right + left
    for face in others:
        total = total + face
    return [
        1.0 - scale * total,
        jnp.where(lane == last, 0.0, scale * right),
        jnp.where(lane == 0, 0.0, scale * left),
    ] + [scale * face for face in others]


def all_weights(coefs):
    return [step_weights(coefs, p) for p in range(1, coefs.shape[0] - 1)]


def stepped(fields, a, low, high, weights):
    planes = fields.shape[1]
    column = [low] + [plane_of(fields, a, p) for p in range(planes)] + [high]
    later = []
    for p in range(planes):
        values = [
            turned(column[p + 1], -1),
            turned(column[p + 1], 1),
            plane_of(fields, a, p, step=1),
            plane_of(fields, a, p, step=-1),
            column[p + 2],
            column[p],
        ]
        total = weights[p][0] * column[p + 1]
        for weight, value in zip(weights[p][1:], values):
            total = total + weight * value
        later.append(total)
    return later


def by_side(odd, pairs):
    copies = [
        (
            [pltpu.make_async_copy(near, low, sems[0]), pltpu.make_async_copy(far, high, sems[1])],
            [pltpu.make_async_copy(near, high, sems[0]), pltpu.make_async_copy(far, low, sems[1])],
        )
        for near, far, low, high, sems in pairs
    ]

    @pl.when(odd)
    def _():
        for when_odd, _ in copies:
            for copy in when_odd:
                copy.start()

    @pl.when(jnp.logical_not(odd))
    def _():
        for _, when_even in copies:
            for copy in when_even:
                copy.start()

    return [copy for when_odd, _ in copies for copy in when_odd]


def force_kernel(
    place_ref,
    velocity_ref,
    images_ref,
    stiffness_ref,
    warped_ref,
    edge_near_ref,
    edge_far_ref,
    warped_near_ref,
    warped_far_ref,
    field_ref,
    coefs_ref,
    near_ref,
    far_ref,
    velocity,
    images,
    warped,
    fields,
    outer,
    sem,
):
    parts, planes, rows = velocity.shape[:3]
    odd = place_ref[0] == 1
    body = slice(PAD, PAD + rows)
    within, every = pl.ds(PAD, rows), pl.ds(0, parts)
    low, mid, high = pl.ds(0, 1), pl.ds(1, planes), pl.ds(planes + 1, 1)
    copies = [
        pltpu.make_async_copy(stiffness_ref, coefs_ref.at[mid, within], sem.at[0]),
        pltpu.make_async_copy(images_ref, images.at[mid], sem.at[1]),
        pltpu.make_async_copy(velocity_ref, velocity, sem.at[2]),
    ]
    for copy in copies:
        copy.start()
    copies += by_side(
        odd,
        [
            (
                edge_near_ref.at[parts],
                edge_far_ref.at[parts],
                coefs_ref.at[low, within],
                coefs_ref.at[high, within],
                (sem.at[3], sem.at[4]),
            ),
            (
                edge_near_ref.at[parts + 1],
                edge_far_ref.at[parts + 1],
                images.at[low],
                images.at[high],
                (sem.at[5], sem.at[6]),
            ),
            (
                edge_near_ref.at[every],
                edge_far_ref.at[every],
                outer.at[:, low],
                outer.at[:, pl.ds(1, 1)],
                (sem.at[7], sem.at[8]),
            ),
        ],
    )
    for ref in (field_ref, fields, coefs_ref, warped):
        clear_pads(ref)
    for p in range(2):
        warped[p, body, :], warped[planes + 2 + p, body, :] = sides(
            odd, warped_near_ref[p], warped_far_ref[p]
        )
    for p in range(planes):
        warped[p + 2, body, :] = warped_ref[p]
    lane = lax.broadcasted_iota(jnp.int32, (rows, LANES), 1)
    right = jnp.where(lane == LANES - 1, 0.0, 0.5 * force_step)
    left = jnp.where(lane == 0, 0.0, 0.5 * force_step)

    def forces(p, image):
        here = plane_of(warped, p + 1)
        mismatch = here - image
        half = (0.5 * force_step) * mismatch
        return [
            mismatch * (right * turned(here, -1) - left * turned(here, 1)),
            half * (plane_of(warped, p + 1, step=1) - plane_of(warped, p + 1, step=-1)),
            half * (plane_of(warped, p + 2) - plane_of(warped, p)),
        ]

    for copy in (copies[0], copies[3], copies[4]):
        copy.wait()
    weights = all_weights(coefs_ref)
    for copy in copies[1:3] + copies[5:]:
        copy.wait()
    for p in range(planes + 2):
        force = forces(p, images[p])
        for a in range(parts):
            if p == 0:
                outer[a, 0] = outer[a, 0] - force[a]
            elif p == planes + 1:
                outer[a, 1] = outer[a, 1] - force[a]
            else:
                fields[a, p - 1, body, :] = velocity[a, p - 1] - force[a]
    for a in range(parts):
        later = stepped(fields, a, outer[a, 0], outer[a, 1], weights)
        for p in range(planes):
            field_ref[a, p, body, :] = later[p]
        near_ref[a, 0], far_ref[a, 0] = sides(odd, later[0], later[-1])


def last_kernel(
    place_ref,
    field_ref,
    coefs_ref,
    near_ref,
    far_ref,
    out_ref,
    done,
    sem,
):
    parts, planes = done.shape[:2]
    odd = place_ref[0] == 1
    weights = all_weights(coefs_ref)
    writes = [pltpu.make_async_copy(done.at[a], out_ref.at[a], sem.at[a]) for a in range(parts)]
    for a in range(parts):
        later = stepped(field_ref, a, *sides(odd, near_ref[a, 0], far_ref[a, 0]), weights)
        for p in range(planes):
            done[a, p] = later[p]
        writes[a].start()
    for copy in writes:
        copy.wait()


def per_device(template, images, velocity, stiffness, send_rows, ref_slot, columns, weights):
    f32, bf16 = jnp.float32, jnp.bfloat16
    shape = jax.ShapeDtypeStruct
    slabs = lax.axis_size("slab")
    subjects = lax.axis_size("subj")
    me = lax.axis_index("subj").astype(jnp.int32).reshape(1)
    slab = lax.axis_index("slab")
    odd = slab % 2 == 1
    place = odd.astype(jnp.int32).reshape(1)
    capacity = send_rows.shape[3]
    rows, width = template.shape
    planes = rows // YR
    parts = velocity.shape[1]
    each = ref_slot.shape[2]
    terms = rows * each
    slots = slabs * capacity
    grid = (planes, YR, width)
    velocity_grid = velocity[0].reshape((parts,) + grid)
    images_grid = images[0].reshape(grid)
    coef_grid = stiffness.reshape(grid)
    dma = pltpu.SemaphoreType.DMA

    sending = call(
        send_kernel,
        shape((slots, width), f32),
        send_rows[0, 0],
        template,
        far=(0, 1),
        scratch=(pltpu.VMEM((slabs, capacity), jnp.int32), pltpu.VMEM((rows, width), f32), dma((2,))),
    )
    received = lax.all_to_all(sending, "slab", split_axis=0, concat_axis=0, tiled=True)

    chunks = 4
    kept_chunks = KEPT
    chunk_shape = (each, len(OFFSETS), rows // chunks, width)
    kept_shape, moved_shape = (kept_chunks,) + chunk_shape, (chunks - kept_chunks,) + chunk_shape
    edge_shape = (parts + 2, 1, YR, width)
    kept, moved, edge_near, edge_far = call(
        prepare_kernel,
        (
            shape(kept_shape, bf16),
            shape(moved_shape, bf16),
            shape(edge_shape, f32),
            shape(edge_shape, f32),
        ),
        place,
        columns.reshape(terms, width),
        weights.reshape(terms, width),
        velocity_grid,
        coef_grid,
        images_grid,
        smem=(0,),
        far=(1, 2, 3, 4, 5),
        out_far=(1, 2, 3),
        scratch=(
            pltpu.VMEM((terms, width), jnp.int32),
            pltpu.VMEM((terms, width), bf16),
            pltpu.VMEM((terms // chunks, width), f32),
            pltpu.VMEM(moved_shape, bf16),
            pltpu.VMEM((parts + 2,) + grid, f32),
            dma((2 * chunks,)),
            dma((chunks + 2,)),
            dma((3,)),
        ),
    )
    edge_far, edge_near = swap_far(edge_far), swap_near(edge_near)

    warped, sent = call(
        functools.partial(warp_kernel, slabs, subjects),
        (shape((rows, width), f32), shape((slots, width), f32)),
        ref_slot[0].T,
        received,
        kept,
        moved,
        images[0],
        far=(3, 4),
        scratch=(
            pltpu.VMEM((rows, width), f32),
            pltpu.VMEM(moved_shape, bf16),
            pltpu.VMEM((each, rows, width), f32),
            pltpu.VMEM((each, rows, 2 * width), bf16),
            dma,
            dma((chunks - kept_chunks,)),
        ),
    )
    returned = lax.all_to_all(sent, ("subj", "slab"), split_axis=0, concat_axis=0, tiled=True)

    own_rows, warped = lax.optimization_barrier((send_rows[0, 0], warped))
    all_rows = over_subjects(own_rows)
    warped_grid = warped.reshape(grid)
    warped_far, warped_near = swap_far(warped_grid), swap_near(warped_grid)

    high = YR + 2 * PAD
    field, coefs, field_near, field_far = call(
        force_kernel,
        (
            shape((parts, planes, high, width), f32),
            shape((planes + 2, high, width), f32),
            shape((parts, 1, YR, width), f32),
            shape((parts, 1, YR, width), f32),
        ),
        place,
        velocity_grid,
        images_grid,
        coef_grid,
        warped_grid,
        edge_near,
        edge_far,
        warped_near,
        warped_far,
        smem=(0,),
        far=(1, 2, 3, 5, 6),
        scratch=(
            pltpu.VMEM((parts,) + grid, f32),
            pltpu.VMEM((planes + 2, YR, width), f32),
            pltpu.VMEM((planes + 4, high, width), f32),
            pltpu.VMEM((parts, planes, high, width), f32),
            pltpu.VMEM((parts, 2, YR, width), f32),
            dma((9,)),
        ),
    )
    field_far, field_near, *all_rows = lax.optimization_barrier((field_far, field_near, *all_rows))
    field_far, field_near = swap_far(field_far), swap_near(field_near)

    part = call(
        functools.partial(collect_kernel, subjects),
        shape((rows // subjects, width), f32),
        me,
        returned,
        *all_rows,
        smem=(0,),
    )
    pieces = over_subjects(part)
    field = call(
        last_kernel,
        shape((parts,) + grid, f32),
        place,
        field,
        coefs,
        field_near,
        field_far,
        smem=(0,),
        out_far=(0,),
        scratch=(pltpu.VMEM((parts,) + grid, f32), dma((parts,))),
    )
    field, *pieces = lax.optimization_barrier((field, *pieces))
    template_out = call(
        functools.partial(update_kernel, subjects),
        shape((rows, width), f32),
        me,
        template,
        *pieces,
        smem=(0,),
    )
    velocity_out = field.reshape(parts, rows, width)[None]
    return (template_out, velocity_out)


def solution(mesh):
    return jax.shard_map(
        per_device,
        mesh=mesh,
        in_specs=(
            P("slab", None),
            P("subj", "slab", None),
            P("subj", None, "slab", None),
            P("slab", None),
            P("subj", "slab", None, None),
            P("subj", "slab", None),
            P("subj", "slab", None, None),
            P("subj", "slab", None, None),
        ),
        out_specs=(P("slab", None), P("subj", None, "slab", None)),
        check_vma=False,
    )
```

```python
import functools

import jax
import jax.numpy as jnp
from jax import lax
from jax.experimental import pallas as pl
from jax.experimental.pallas import tpu as pltpu
from jax.sharding import PartitionSpec as P

YR = 256
LANES = 128
PAD = 8
KEPT = 1
OFFSETS = (0, -2, -1, 1, 2)


force_step = 1.0
diffusion_dt = 0.16
template_rate = 2.0

VMEM_LIMIT = 40 * 1024 * 1024


def call(kernel, out_shape, *args, scratch=(), smem=(), far=(), out_far=()):
    many = isinstance(out_shape, tuple)
    shapes = [
        pltpu.HBM(s.shape, s.dtype) if i in out_far else s
        for i, s in enumerate(out_shape if many else (out_shape,))
    ]
    spaces = [pltpu.HBM if i in out_far else pltpu.VMEM for i in range(len(shapes))]
    specs = [pl.BlockSpec(memory_space=space) for space in spaces]
    return pl.pallas_call(
        kernel,
        out_shape=tuple(shapes) if many else shapes[0],
        in_specs=[
            pl.BlockSpec(
                memory_space=pltpu.SMEM if i in smem else pltpu.HBM if i in far else pltpu.VMEM
            )
            for i in range(len(args))
        ],
        out_specs=tuple(specs) if many else specs[0],
        scratch_shapes=scratch,
        compiler_params=pltpu.CompilerParams(vmem_limit_bytes=VMEM_LIMIT),
    )(
        *[
            pltpu.with_memory_space_constraint(arg, pltpu.HBM) if i in far else arg
            for i, arg in enumerate(args)
        ]
    )


def halves(values):
    high = values.astype(jnp.bfloat16)
    low = (values - high.astype(jnp.float32)).astype(jnp.bfloat16)
    return jnp.concatenate([high, low], axis=1)


def joined(pair):
    width = pair.shape[1] // 2
    return pair[:, :width] + pair[:, width:]


def turned(values, shift):
    shift %= values.shape[1]
    return pltpu.roll(values, shift, axis=1) if shift else values


def dot(left, right):
    return jnp.dot(left, right, preferred_element_type=jnp.float32)


def one_hot(matches):
    return jnp.where(matches, 1.0, 0.0).astype(jnp.bfloat16)


def send_kernel(send_ref, template_ref, out_ref, send, template, sem):
    slabs, capacity = send.shape
    rows = template.shape[0]
    copies = [
        pltpu.make_async_copy(send_ref, send, sem.at[0]),
        pltpu.make_async_copy(template_ref, template, sem.at[1]),
    ]
    for copy in copies:
        copy.start()
    copies[0].wait()
    padded = jnp.concatenate([send[...], jnp.zeros((slabs, LANES - capacity), jnp.int32)], axis=1)
    columns = padded.T
    number = lax.broadcasted_iota(jnp.int32, (capacity, rows), 1)
    chosen = [
        one_hot(jnp.broadcast_to(columns[:capacity, k : k + 1], (capacity, rows)) == number)
        for k in range(slabs)
    ]
    copies[1].wait()
    pair = halves(template[...])
    for k in range(slabs):
        out_ref[k * capacity : (k + 1) * capacity, :] = joined(dot(chosen[k], pair))


def prepare_kernel(
    place_ref,
    columns_ref,
    weights_ref,
    velocity_ref,
    stiffness_ref,
    images_ref,
    kept_ref,
    moved_ref,
    near_ref,
    far_ref,
    columns,
    weights,
    plain,
    moved,
    edge,
    in_sem,
    out_sem,
    edge_sem,
):
    held = kept_ref.shape[0]
    each, count, some, width = moved.shape[1:]
    chunks = held + moved.shape[0]
    odd = place_ref[0]
    near_plane, far_plane = pl.ds((edge.shape[1] - 1) * (1 - odd), 1), pl.ds((edge.shape[1] - 1) * odd, 1)
    step = some * each
    parts = velocity_ref.shape[0]
    reads = [
        (
            pltpu.make_async_copy(
                columns_ref.at[pl.ds(i * step, step)], columns.at[pl.ds(i * step, step)], in_sem.at[i]
            ),
            pltpu.make_async_copy(
                weights_ref.at[pl.ds(i * step, step)],
                weights.at[pl.ds(i * step, step)],
                in_sem.at[chunks + i],
            ),
        )
        for i in range(chunks)
    ]
    edges = [
        pltpu.make_async_copy(velocity_ref, edge.at[pl.ds(0, parts)], edge_sem.at[0]),
        pltpu.make_async_copy(stiffness_ref, edge.at[parts], edge_sem.at[1]),
        pltpu.make_async_copy(images_ref, edge.at[parts + 1], edge_sem.at[2]),
    ]
    writes = [
        pltpu.make_async_copy(moved.at[i], moved_ref.at[i], out_sem.at[i])
        for i in range(chunks - held)
    ]
    edge_writes = [
        pltpu.make_async_copy(edge.at[:, near_plane], near_ref, out_sem.at[chunks]),
        pltpu.make_async_copy(edge.at[:, far_plane], far_ref, out_sem.at[chunks + 1]),
    ]
    for copy in reads[0]:
        copy.start()
    for copy in edges:
        copy.start()
    for pair in reads[1:]:
        for copy in pair:
            copy.start()
    cell = lax.broadcasted_iota(jnp.int32, (some, width), 1)
    for i in range(chunks):
        at = i * step
        for copy in reads[i]:
            copy.wait()
        plain[:step, :] = weights[at : at + step, :].astype(jnp.float32)
        for b in range(each):
            offset = columns[pl.ds(at + b, some, stride=each), :] - cell
            here = plain[pl.ds(b, some, stride=each), :]
            for j, o in enumerate(OFFSETS):
                kept = jnp.where(offset == o, here, 0.0)
                target, at_chunk = (moved, i) if i < chunks - held else (kept_ref, i - chunks + held)
                target[at_chunk, b, j] = turned(kept.astype(jnp.bfloat16), o)
        if i < chunks - held:
            writes[i].start()
        if i == 0:
            for copy in edges:
                copy.wait()
            for copy in edge_writes:
                copy.start()
    for copy in writes + edge_writes:
        copy.wait()


def warp_kernel(
    slabs,
    subjects,
    slot_ref,
    received_ref,
    kept_ref,
    moved_ref,
    images_ref,
    warped_ref,
    sent_ref,
    images,
    moved,
    picked,
    placed,
    first_sem,
    moved_sem,
):
    slots, width = received_ref.shape
    each, count, some = moved.shape[1:4]
    held = kept_ref.shape[0]
    loaded = moved.shape[0]
    chunks = loaded + held
    rows = chunks * some
    block = width // subjects
    group = slots // subjects
    capacity = slots // slabs
    held = capacity // subjects
    first = pltpu.make_async_copy(images_ref, images, first_sem)
    moves = [
        pltpu.make_async_copy(moved_ref.at[i], moved.at[i], moved_sem.at[i]) for i in range(loaded)
    ]
    for copy in [first] + moves:
        copy.start()
    slot = slot_ref[...]
    slot_wide = jnp.concatenate([slot, jnp.zeros((LANES - each, rows), jnp.int32)], axis=0).T
    inner = slot % capacity
    packed = (inner // held) * group + (slot // capacity) * held + inner % held
    lane = lax.broadcasted_iota(jnp.int32, (rows, LANES), 1)
    number = lax.broadcasted_iota(jnp.int32, (slots, rows), 0)
    pair = halves(received_ref[...])
    for b in range(each):
        wide = jnp.broadcast_to(slot_wide[:, b : b + 1], (rows, LANES))
        pick = jnp.concatenate(
            [one_hot(wide == lane + t * LANES) for t in range(slots // LANES)], axis=1
        )
        picked[b] = joined(dot(pick, pair))
    for copy in [first] + moves:
        copy.wait()
    for i in range(chunks):
        here, h = (moved, i) if i < loaded else (kept_ref, i - loaded)
        at = slice(i * some, (i + 1) * some)
        sums = [jnp.zeros((some, width), jnp.float32) for _ in OFFSETS]
        for b in range(each):
            values = picked[b, at, :]
            for j in range(count):
                sums[j] = sums[j] + here[h, b, j].astype(jnp.float32) * values
        warped = sums[0]
        for j, o in enumerate(OFFSETS[1:], 1):
            warped = warped + turned(sums[j], -o)
        warped_ref[at, :] = warped
        mismatch = warped - images[at, :]
        ahead = [turned(mismatch, o) for o in OFFSETS]
        for b in range(each):
            total = here[h, b, 0].astype(jnp.float32) * ahead[0]
            for j in range(1, count):
                total = total + here[h, b, j].astype(jnp.float32) * ahead[j]
            placed[b, at, :] = halves(total)
    total = jnp.zeros((slots, 2 * width), jnp.float32)
    for b in range(each):
        drop = one_hot(jnp.broadcast_to(packed[b : b + 1], (slots, rows)) == number)
        total = total + dot(drop, placed[b])
    total = joined(total)
    place = lax.broadcasted_iota(jnp.int32, (group, width), 1) // block
    groups = [total[q * group : (q + 1) * group, :] for q in range(subjects)]
    for p in range(subjects):
        out = jnp.zeros((group, width), jnp.float32)
        for q in range(subjects):
            out = jnp.where(place == q, turned(groups[q], (q - p) * block), out)
        sent_ref[p * group : (p + 1) * group, :] = out


def collect_kernel(subjects, me_ref, returned_ref, *refs):
    row_refs, out_ref = refs[:-1], refs[-1]
    slots, width = returned_ref.shape
    slabs, capacity = row_refs[0].shape
    rows = out_ref.shape[0] * subjects
    block = width // subjects
    group = slots // subjects
    held = capacity // subjects
    me = me_ref[0]
    pair = halves(
        jnp.concatenate(
            [
                returned_ref[pl.ds(pl.multiple_of((me ^ d) * group, group), group), :]
                for d in range(subjects)
            ]
        )
    )
    lane = lax.broadcasted_iota(jnp.int32, (slabs, LANES), 1)
    slab = lax.broadcasted_iota(jnp.int32, (slabs, LANES), 0)
    fill = jnp.zeros((slabs, LANES - capacity), jnp.int32)
    wanted = []
    for q in range(subjects):
        chunks = [jnp.zeros((1, LANES), jnp.int32) for _ in range(slots // LANES)]
        for d in range(subjects):
            spread = jnp.concatenate([row_refs[d][...], fill], axis=1)
            spread = turned(spread, d * group - q * held)
            spread = pltpu.roll(spread, 0, axis=1, stride=held, stride_axis=0)
            first = (d * group) % LANES + slab * held
            kept = jnp.where((lane >= first) & (lane < first + held), spread, 0)
            chunks[d * group // LANES] += jnp.sum(kept, axis=0, keepdims=True)
        wanted.append(jnp.concatenate(chunks, axis=1))
    number = lax.broadcasted_iota(jnp.int32, (rows, slots), 0)
    place = lax.broadcasted_iota(jnp.int32, (rows, width), 1) // block
    kept = jnp.zeros((rows, width), jnp.float32)
    for q in range(subjects):
        match = jnp.broadcast_to(wanted[q], (rows, slots)) == number
        kept = jnp.where(place == q, joined(dot(one_hot(match), pair)), kept)
    turn = block
    while turn < width:
        kept = kept + turned(kept, turn)
        turn *= 2
    part = rows // subjects
    out = jnp.zeros((part, width), jnp.float32)
    for p in range(subjects):
        out = jnp.where(place[:part] == p, kept[p * part : (p + 1) * part], out)
    out_ref[...] = out


def update_kernel(subjects, me_ref, template_ref, *refs):
    parts, out_ref = refs[:-1], refs[-1]
    rows, width = template_ref.shape
    block = width // subjects
    part = rows // subjects
    me = me_ref[0]
    place = lax.broadcasted_iota(jnp.int32, (part, width), 1) // block
    for p in range(subjects):
        total = jnp.zeros((part, width), jnp.float32)
        for d in range(subjects):
            source = me ^ d
            turn = lax.rem((source - p) * block + width, width)
            total = jnp.where(place == source, pltpu.roll(parts[d][...], turn, axis=1), total)
        at = slice(p * part, (p + 1) * part)
        out_ref[at, :] = template_ref[at, :] - template_rate * total / subjects


def over_subjects(values):
    count = lax.axis_size("subj")
    return [values] + [
        lax.ppermute(values, "subj", [(i, i ^ d) for i in range(count)]) for d in range(1, count)
    ]


def swap_near(values):
    return lax.ppermute(values, "slab", [(i, i ^ 1) for i in range(lax.axis_size("slab"))])


def swap_far(values):
    count = lax.axis_size("slab")
    return lax.ppermute(
        values, "slab", [(i, i + 1 if i % 2 else i - 1) for i in range(1, count - 1)]
    )


def clear_pads(ref):
    rows = ref.shape[-2] - 2 * PAD
    zeros = jnp.zeros(ref.shape[:-2] + (PAD, ref.shape[-1]), ref.dtype)
    ref[..., :PAD, :] = zeros
    ref[..., PAD + rows :, :] = zeros


def plane_of(ref, *at, step=0):
    rows = ref.shape[-2] - 2 * PAD
    return ref[(*at, slice(PAD + step, PAD + step + rows), slice(None))]


def sides(odd, near, far):
    return jnp.where(odd, near, far), jnp.where(odd, far, near)


def step_weights(coefs, p):
    center = plane_of(coefs, p)
    lane = lax.broadcasted_iota(jnp.int32, center.shape, 1)
    scale = 0.5 * diffusion_dt
    last = center.shape[1] - 1
    right = center + jnp.where(lane == last, 0.0, turned(center, -1))
    left = center + jnp.where(lane == 0, 0.0, turned(center, 1))
    others = [
        center + near
        for near in (
            plane_of(coefs, p, step=1),
            plane_of(coefs, p, step=-1),
            plane_of(coefs, p + 1),
            plane_of(coefs, p - 1),
        )
    ]
    total = right + left
    for face in others:
        total = total + face
    return [
        1.0 - scale * total,
        jnp.where(lane == last, 0.0, scale * right),
        jnp.where(lane == 0, 0.0, scale * left),
    ] + [scale * face for face in others]


def all_weights(coefs):
    return [step_weights(coefs, p) for p in range(1, coefs.shape[0] - 1)]


def stepped(fields, a, low, high, weights):
    planes = fields.shape[1]
    column = [low] + [plane_of(fields, a, p) for p in range(planes)] + [high]
    later = []
    for p in range(planes):
        values = [
            turned(column[p + 1], -1),
            turned(column[p + 1], 1),
            plane_of(fields, a, p, step=1),
            plane_of(fields, a, p, step=-1),
            column[p + 2],
            column[p],
        ]
        total = weights[p][0] * column[p + 1]
        for weight, value in zip(weights[p][1:], values):
            total = total + weight * value
        later.append(total)
    return later


def by_side(odd, pairs):
    copies = [
        (
            [pltpu.make_async_copy(near, low, sems[0]), pltpu.make_async_copy(far, high, sems[1])],
            [pltpu.make_async_copy(near, high, sems[0]), pltpu.make_async_copy(far, low, sems[1])],
        )
        for near, far, low, high, sems in pairs
    ]

    @pl.when(odd)
    def _():
        for when_odd, _ in copies:
            for copy in when_odd:
                copy.start()

    @pl.when(jnp.logical_not(odd))
    def _():
        for _, when_even in copies:
            for copy in when_even:
                copy.start()

    return [copy for when_odd, _ in copies for copy in when_odd]


def force_kernel(
    place_ref,
    velocity_ref,
    images_ref,
    stiffness_ref,
    warped_ref,
    edge_near_ref,
    edge_far_ref,
    warped_near_ref,
    warped_far_ref,
    field_ref,
    coefs_ref,
    near_ref,
    far_ref,
    velocity,
    images,
    warped,
    fields,
    outer,
    sem,
):
    parts, planes, rows = velocity.shape[:3]
    odd = place_ref[0] == 1
    body = slice(PAD, PAD + rows)
    within, every = pl.ds(PAD, rows), pl.ds(0, parts)
    low, mid, high = pl.ds(0, 1), pl.ds(1, planes), pl.ds(planes + 1, 1)
    copies = [
        pltpu.make_async_copy(stiffness_ref, coefs_ref.at[mid, within], sem.at[0]),
        pltpu.make_async_copy(images_ref, images.at[mid], sem.at[1]),
        pltpu.make_async_copy(velocity_ref, velocity, sem.at[2]),
    ]
    for copy in copies:
        copy.start()
    copies += by_side(
        odd,
        [
            (
                edge_near_ref.at[parts],
                edge_far_ref.at[parts],
                coefs_ref.at[low, within],
                coefs_ref.at[high, within],
                (sem.at[3], sem.at[4]),
            ),
            (
                edge_near_ref.at[parts + 1],
                edge_far_ref.at[parts + 1],
                images.at[low],
                images.at[high],
                (sem.at[5], sem.at[6]),
            ),
            (
                edge_near_ref.at[every],
                edge_far_ref.at[every],
                outer.at[:, low],
                outer.at[:, pl.ds(1, 1)],
                (sem.at[7], sem.at[8]),
            ),
        ],
    )
    for ref in (field_ref, fields, coefs_ref, warped):
        clear_pads(ref)
    for p in range(2):
        warped[p, body, :], warped[planes + 2 + p, body, :] = sides(
            odd, warped_near_ref[p], warped_far_ref[p]
        )
    for p in range(planes):
        warped[p + 2, body, :] = warped_ref[p]
    lane = lax.broadcasted_iota(jnp.int32, (rows, LANES), 1)
    right = jnp.where(lane == LANES - 1, 0.0, 0.5 * force_step)
    left = jnp.where(lane == 0, 0.0, 0.5 * force_step)

    def forces(p, image):
        here = plane_of(warped, p + 1)
        mismatch = here - image
        half = (0.5 * force_step) * mismatch
        return [
            mismatch * (right * turned(here, -1) - left * turned(here, 1)),
            half * (plane_of(warped, p + 1, step=1) - plane_of(warped, p + 1, step=-1)),
            half * (plane_of(warped, p + 2) - plane_of(warped, p)),
        ]

    for copy in (copies[0], copies[3], copies[4]):
        copy.wait()
    weights = all_weights(coefs_ref)
    for copy in copies[1:3] + copies[5:]:
        copy.wait()
    for p in range(planes + 2):
        force = forces(p, images[p])
        for a in range(parts):
            if p == 0:
                outer[a, 0] = outer[a, 0] - force[a]
            elif p == planes + 1:
                outer[a, 1] = outer[a, 1] - force[a]
            else:
                fields[a, p - 1, body, :] = velocity[a, p - 1] - force[a]
    for a in range(parts):
        later = stepped(fields, a, outer[a, 0], outer[a, 1], weights)
        for p in range(planes):
            field_ref[a, p, body, :] = later[p]
        near_ref[a, 0], far_ref[a, 0] = sides(odd, later[0], later[-1])


def last_kernel(
    place_ref,
    field_ref,
    coefs_ref,
    near_ref,
    far_ref,
    out_ref,
    done,
    sem,
):
    parts, planes = done.shape[:2]
    odd = place_ref[0] == 1
    weights = all_weights(coefs_ref)
    writes = [pltpu.make_async_copy(done.at[a], out_ref.at[a], sem.at[a]) for a in range(parts)]
    for a in range(parts):
        later = stepped(field_ref, a, *sides(odd, near_ref[a, 0], far_ref[a, 0]), weights)
        for p in range(planes):
            done[a, p] = later[p]
        writes[a].start()
    for copy in writes:
        copy.wait()


def per_device(template, images, velocity, stiffness, send_rows, ref_slot, columns, weights):
    f32, bf16 = jnp.float32, jnp.bfloat16
    shape = jax.ShapeDtypeStruct
    slabs = lax.axis_size("slab")
    subjects = lax.axis_size("subj")
    me = lax.axis_index("subj").astype(jnp.int32).reshape(1)
    slab = lax.axis_index("slab")
    odd = slab % 2 == 1
    place = odd.astype(jnp.int32).reshape(1)
    capacity = send_rows.shape[3]
    rows, width = template.shape
    planes = rows // YR
    parts = velocity.shape[1]
    each = ref_slot.shape[2]
    terms = rows * each
    slots = slabs * capacity
    grid = (planes, YR, width)
    velocity_grid = velocity[0].reshape((parts,) + grid)
    images_grid = images[0].reshape(grid)
    coef_grid = stiffness.reshape(grid)
    dma = pltpu.SemaphoreType.DMA

    sending = call(
        send_kernel,
        shape((slots, width), f32),
        send_rows[0, 0],
        template,
        far=(0, 1),
        scratch=(pltpu.VMEM((slabs, capacity), jnp.int32), pltpu.VMEM((rows, width), f32), dma((2,))),
    )
    received = lax.all_to_all(sending, "slab", split_axis=0, concat_axis=0, tiled=True)

    chunks = 4
    kept_chunks = KEPT
    chunk_shape = (each, len(OFFSETS), rows // chunks, width)
    kept_shape, moved_shape = (kept_chunks,) + chunk_shape, (chunks - kept_chunks,) + chunk_shape
    edge_shape = (parts + 2, 1, YR, width)
    kept, moved, edge_near, edge_far = call(
        prepare_kernel,
        (
            shape(kept_shape, bf16),
            shape(moved_shape, bf16),
            shape(edge_shape, f32),
            shape(edge_shape, f32),
        ),
        place,
        columns.reshape(terms, width),
        weights.reshape(terms, width),
        velocity_grid,
        coef_grid,
        images_grid,
        smem=(0,),
        far=(1, 2, 3, 4, 5),
        out_far=(1, 2, 3),
        scratch=(
            pltpu.VMEM((terms + each, width), jnp.int32),
            pltpu.VMEM((terms, width), bf16),
            pltpu.VMEM((terms // chunks + each, width), f32),
            pltpu.VMEM(moved_shape, bf16),
            pltpu.VMEM((parts + 2,) + grid, f32),
            dma((2 * chunks,)),
            dma((chunks + 2,)),
            dma((3,)),
        ),
    )
    edge_far, edge_near = swap_far(edge_far), swap_near(edge_near)

    warped, sent = call(
        functools.partial(warp_kernel, slabs, subjects),
        (shape((rows, width), f32), shape((slots, width), f32)),
        ref_slot[0].T,
        received,
        kept,
        moved,
        images[0],
        far=(3, 4),
        scratch=(
            pltpu.VMEM((rows, width), f32),
            pltpu.VMEM(moved_shape, bf16),
            pltpu.VMEM((each, rows, width), f32),
            pltpu.VMEM((each, rows, 2 * width), bf16),
            dma,
            dma((chunks - kept_chunks,)),
        ),
    )
    returned = lax.all_to_all(sent, ("subj", "slab"), split_axis=0, concat_axis=0, tiled=True)

    own_rows, warped = lax.optimization_barrier((send_rows[0, 0], warped))
    all_rows = over_subjects(own_rows)
    warped_grid = warped.reshape(grid)
    warped_far, warped_near = swap_far(warped_grid), swap_near(warped_grid)

    high = YR + 2 * PAD
    field, coefs, field_near, field_far = call(
        force_kernel,
        (
            shape((parts, planes, high, width), f32),
            shape((planes + 2, high, width), f32),
            shape((parts, 1, YR, width), f32),
            shape((parts, 1, YR, width), f32),
        ),
        place,
        velocity_grid,
        images_grid,
        coef_grid,
        warped_grid,
        edge_near,
        edge_far,
        warped_near,
        warped_far,
        smem=(0,),
        far=(1, 2, 3, 5, 6),
        scratch=(
            pltpu.VMEM((parts,) + grid, f32),
            pltpu.VMEM((planes + 2, YR, width), f32),
            pltpu.VMEM((planes + 4, high, width), f32),
            pltpu.VMEM((parts, planes, high, width), f32),
            pltpu.VMEM((parts, 2, YR, width), f32),
            dma((9,)),
        ),
    )
    field_far, field_near, *all_rows = lax.optimization_barrier((field_far, field_near, *all_rows))
    field_far, field_near = swap_far(field_far), swap_near(field_near)

    part = call(
        functools.partial(collect_kernel, subjects),
        shape((rows // subjects, width), f32),
        me,
        returned,
        *all_rows,
        smem=(0,),
    )
    pieces = over_subjects(part)
    field = call(
        last_kernel,
        shape((parts,) + grid, f32),
        place,
        field,
        coefs,
        field_near,
        field_far,
        smem=(0,),
        out_far=(0,),
        scratch=(pltpu.VMEM((parts,) + grid, f32), dma((parts,))),
    )
    field, *pieces = lax.optimization_barrier((field, *pieces))
    template_out = call(
        functools.partial(update_kernel, subjects),
        shape((rows, width), f32),
        me,
        template,
        *pieces,
        smem=(0,),
    )
    velocity_out = field.reshape(parts, rows, width)[None]
    return (template_out, velocity_out)


def solution(mesh):
    return jax.shard_map(
        per_device,
        mesh=mesh,
        in_specs=(
            P("slab", None),
            P("subj", "slab", None),
            P("subj", None, "slab", None),
            P("slab", None),
            P("subj", "slab", None, None),
            P("subj", "slab", None),
            P("subj", "slab", None, None),
            P("subj", "slab", None, None),
        ),
        out_specs=(P("slab", None), P("subj", None, "slab", None)),
        check_vma=False,
    )
```

```python
import functools

import jax
import jax.numpy as jnp
from jax import lax
from jax.experimental import pallas as pl
from jax.experimental.pallas import tpu as pltpu
from jax.sharding import PartitionSpec as P

YR = 256
LANES = 128
PAD = 8
KEPT = 1
OFFSETS = (0, -2, -1, 1, 2)


force_step = 1.0
diffusion_dt = 0.16
template_rate = 2.0

VMEM_LIMIT = 40 * 1024 * 1024


def call(kernel, out_shape, *args, scratch=(), smem=(), far=(), out_far=()):
    many = isinstance(out_shape, tuple)
    shapes = [
        pltpu.HBM(s.shape, s.dtype) if i in out_far else s
        for i, s in enumerate(out_shape if many else (out_shape,))
    ]
    spaces = [pltpu.HBM if i in out_far else pltpu.VMEM for i in range(len(shapes))]
    specs = [pl.BlockSpec(memory_space=space) for space in spaces]
    return pl.pallas_call(
        kernel,
        out_shape=tuple(shapes) if many else shapes[0],
        in_specs=[
            pl.BlockSpec(
                memory_space=pltpu.SMEM if i in smem else pltpu.HBM if i in far else pltpu.VMEM
            )
            for i in range(len(args))
        ],
        out_specs=tuple(specs) if many else specs[0],
        scratch_shapes=scratch,
        compiler_params=pltpu.CompilerParams(vmem_limit_bytes=VMEM_LIMIT),
    )(
        *[
            pltpu.with_memory_space_constraint(arg, pltpu.HBM) if i in far else arg
            for i, arg in enumerate(args)
        ]
    )


def halves(values):
    high = values.astype(jnp.bfloat16)
    low = (values - high.astype(jnp.float32)).astype(jnp.bfloat16)
    return jnp.concatenate([high, low], axis=1)


def joined(pair):
    width = pair.shape[1] // 2
    return pair[:, :width] + pair[:, width:]


def turned(values, shift):
    shift %= values.shape[1]
    return pltpu.roll(values, shift, axis=1) if shift else values


def dot(left, right):
    return jnp.dot(left, right, preferred_element_type=jnp.float32)


def one_hot(matches):
    return jnp.where(matches, 1.0, 0.0).astype(jnp.bfloat16)


def send_kernel(send_ref, template_ref, out_ref, send, template, sem):
    slabs, capacity = send.shape
    rows = template.shape[0]
    copies = [
        pltpu.make_async_copy(send_ref, send, sem.at[0]),
        pltpu.make_async_copy(template_ref, template, sem.at[1]),
    ]
    for copy in copies:
        copy.start()
    copies[0].wait()
    padded = jnp.concatenate([send[...], jnp.zeros((slabs, LANES - capacity), jnp.int32)], axis=1)
    columns = padded.T
    number = lax.broadcasted_iota(jnp.int32, (capacity, rows), 1)
    chosen = [
        one_hot(jnp.broadcast_to(columns[:capacity, k : k + 1], (capacity, rows)) == number)
        for k in range(slabs)
    ]
    copies[1].wait()
    pair = halves(template[...])
    for k in range(slabs):
        out_ref[k * capacity : (k + 1) * capacity, :] = joined(dot(chosen[k], pair))


def prepare_kernel(
    place_ref,
    columns_ref,
    weights_ref,
    velocity_ref,
    stiffness_ref,
    images_ref,
    kept_ref,
    moved_ref,
    near_ref,
    far_ref,
    columns,
    weights,
    plain,
    moved,
    edge,
    in_sem,
    out_sem,
    edge_sem,
):
    held = kept_ref.shape[0]
    each, count, some, width = moved.shape[1:]
    chunks = held + moved.shape[0]
    odd = place_ref[0]
    near_plane, far_plane = pl.ds((edge.shape[1] - 1) * (1 - odd), 1), pl.ds((edge.shape[1] - 1) * odd, 1)
    step = some * each
    parts = velocity_ref.shape[0]
    reads = [
        (
            pltpu.make_async_copy(
                columns_ref.at[pl.ds(i * step, step)], columns.at[pl.ds(i * step, step)], in_sem.at[i]
            ),
            pltpu.make_async_copy(
                weights_ref.at[pl.ds(i * step, step)],
                weights.at[pl.ds(i * step, step)],
                in_sem.at[chunks + i],
            ),
        )
        for i in range(chunks)
    ]
    edges = [
        pltpu.make_async_copy(velocity_ref, edge.at[pl.ds(0, parts)], edge_sem.at[0]),
        pltpu.make_async_copy(stiffness_ref, edge.at[parts], edge_sem.at[1]),
        pltpu.make_async_copy(images_ref, edge.at[parts + 1], edge_sem.at[2]),
    ]
    writes = [
        pltpu.make_async_copy(moved.at[i], moved_ref.at[i], out_sem.at[i])
        for i in range(chunks - held)
    ]
    edge_writes = [
        pltpu.make_async_copy(edge.at[:, near_plane], near_ref, out_sem.at[chunks]),
        pltpu.make_async_copy(edge.at[:, far_plane], far_ref, out_sem.at[chunks + 1]),
    ]
    for copy in reads[0]:
        copy.start()
    for copy in edges:
        copy.start()
    for pair in reads[1:]:
        for copy in pair:
            copy.start()
    cell = lax.broadcasted_iota(jnp.int32, (some, width), 1)
    for i in range(chunks):
        at = i * step
        for copy in reads[i]:
            copy.wait()
        plain[:step, :] = weights[at : at + step, :].astype(jnp.float32)
        for b in range(each):
            offset = columns[pl.ds(at + b, some, stride=each), :] - cell
            here = plain[pl.ds(b, some, stride=each), :]
            for j, o in enumerate(OFFSETS):
                kept = jnp.where(offset == o, here, 0.0)
                target, at_chunk = (moved, i) if i < chunks - held else (kept_ref, i - chunks + held)
                target[at_chunk, b, j] = turned(kept.astype(jnp.bfloat16), o)
        if i < chunks - held:
            writes[i].start()
        if i == 0:
            for copy in edges:
                copy.wait()
            for copy in edge_writes:
                copy.start()
    for copy in writes + edge_writes:
        copy.wait()


def warp_kernel(
    slabs,
    subjects,
    slot_ref,
    received_ref,
    kept_ref,
    moved_ref,
    images_ref,
    warped_ref,
    sent_ref,
    images,
    moved,
    picked,
    placed,
    sent,
    first_sem,
    moved_sem,
    sent_sem,
):
    slots, width = received_ref.shape
    each, count, some = moved.shape[1:4]
    held = kept_ref.shape[0]
    loaded = moved.shape[0]
    chunks = loaded + held
    rows = chunks * some
    block = width // subjects
    group = slots // subjects
    capacity = slots // slabs
    held = capacity // subjects
    first = pltpu.make_async_copy(images_ref, images, first_sem)
    moves = [
        pltpu.make_async_copy(moved_ref.at[i], moved.at[i], moved_sem.at[i]) for i in range(loaded)
    ]
    for copy in [first] + moves:
        copy.start()
    slot = slot_ref[...]
    slot_wide = jnp.concatenate([slot, jnp.zeros((LANES - each, rows), jnp.int32)], axis=0).T
    inner = slot % capacity
    packed = (inner // held) * group + (slot // capacity) * held + inner % held
    lane = lax.broadcasted_iota(jnp.int32, (rows, LANES), 1)
    number = lax.broadcasted_iota(jnp.int32, (slots, rows), 0)
    pair = halves(received_ref[...])
    for b in range(each):
        wide = jnp.broadcast_to(slot_wide[:, b : b + 1], (rows, LANES))
        pick = jnp.concatenate(
            [one_hot(wide == lane + t * LANES) for t in range(slots // LANES)], axis=1
        )
        picked[b] = joined(dot(pick, pair))
    for copy in [first] + moves:
        copy.wait()
    for i in range(chunks):
        here, h = (moved, i) if i < loaded else (kept_ref, i - loaded)
        at = slice(i * some, (i + 1) * some)
        sums = [jnp.zeros((some, width), jnp.float32) for _ in OFFSETS]
        for b in range(each):
            values = picked[b, at, :]
            for j in range(count):
                sums[j] = sums[j] + here[h, b, j].astype(jnp.float32) * values
        warped = sums[0]
        for j, o in enumerate(OFFSETS[1:], 1):
            warped = warped + turned(sums[j], -o)
        warped_ref[at, :] = warped
        mismatch = warped - images[at, :]
        ahead = [turned(mismatch, o) for o in OFFSETS]
        for b in range(each):
            total = here[h, b, 0].astype(jnp.float32) * ahead[0]
            for j in range(1, count):
                total = total + here[h, b, j].astype(jnp.float32) * ahead[j]
            placed[b, at, :] = halves(total)
    total = jnp.zeros((slots, 2 * width), jnp.float32)
    for b in range(each):
        drop = one_hot(jnp.broadcast_to(packed[b : b + 1], (slots, rows)) == number)
        total = total + dot(drop, placed[b])
    total = joined(total)
    place = lax.broadcasted_iota(jnp.int32, (group, width), 1) // block
    writes = []
    groups = [total[q * group : (q + 1) * group, :] for q in range(subjects)]
    for p in range(subjects):
        out = jnp.zeros((group, width), jnp.float32)
        for q in range(subjects):
            out = jnp.where(place == q, turned(groups[q], (q - p) * block), out)
        sent[p * group : (p + 1) * group, :] = out
        rows_at = pl.ds(p * group, group)
        writes.append(pltpu.make_async_copy(sent.at[rows_at], sent_ref.at[rows_at], sent_sem.at[p]))
        writes[-1].start()
    for copy in writes:
        copy.wait()


def collect_kernel(subjects, me_ref, returned_ref, *refs):
    row_refs, out_ref = refs[:-1], refs[-1]
    slots, width = returned_ref.shape
    slabs, capacity = row_refs[0].shape
    rows = out_ref.shape[0] * subjects
    block = width // subjects
    group = slots // subjects
    held = capacity // subjects
    me = me_ref[0]
    pair = halves(
        jnp.concatenate(
            [
                returned_ref[pl.ds(pl.multiple_of((me ^ d) * group, group), group), :]
                for d in range(subjects)
            ]
        )
    )
    lane = lax.broadcasted_iota(jnp.int32, (slabs, LANES), 1)
    slab = lax.broadcasted_iota(jnp.int32, (slabs, LANES), 0)
    fill = jnp.zeros((slabs, LANES - capacity), jnp.int32)
    wanted = []
    for q in range(subjects):
        chunks = [jnp.zeros((1, LANES), jnp.int32) for _ in range(slots // LANES)]
        for d in range(subjects):
            spread = jnp.concatenate([row_refs[d][...], fill], axis=1)
            spread = turned(spread, d * group - q * held)
            spread = pltpu.roll(spread, 0, axis=1, stride=held, stride_axis=0)
            first = (d * group) % LANES + slab * held
            kept = jnp.where((lane >= first) & (lane < first + held), spread, 0)
            chunks[d * group // LANES] += jnp.sum(kept, axis=0, keepdims=True)
        wanted.append(jnp.concatenate(chunks, axis=1))
    number = lax.broadcasted_iota(jnp.int32, (rows, slots), 0)
    place = lax.broadcasted_iota(jnp.int32, (rows, width), 1) // block
    kept = jnp.zeros((rows, width), jnp.float32)
    for q in range(subjects):
        match = jnp.broadcast_to(wanted[q], (rows, slots)) == number
        kept = jnp.where(place == q, joined(dot(one_hot(match), pair)), kept)
    turn = block
    while turn < width:
        kept = kept + turned(kept, turn)
        turn *= 2
    part = rows // subjects
    out = jnp.zeros((part, width), jnp.float32)
    for p in range(subjects):
        out = jnp.where(place[:part] == p, kept[p * part : (p + 1) * part], out)
    out_ref[...] = out


def update_kernel(subjects, me_ref, template_ref, *refs):
    parts, (out_ref, done, sem) = refs[:-3], refs[-3:]
    rows, width = template_ref.shape
    block = width // subjects
    part = rows // subjects
    me = me_ref[0]
    place = lax.broadcasted_iota(jnp.int32, (part, width), 1) // block
    writes = []
    for p in range(subjects):
        total = jnp.zeros((part, width), jnp.float32)
        for d in range(subjects):
            source = me ^ d
            turn = lax.rem((source - p) * block + width, width)
            total = jnp.where(place == source, pltpu.roll(parts[d][...], turn, axis=1), total)
        at = slice(p * part, (p + 1) * part)
        done[at, :] = template_ref[at, :] - template_rate * total / subjects
        rows_at = pl.ds(p * part, part)
        writes.append(pltpu.make_async_copy(done.at[rows_at], out_ref.at[rows_at], sem.at[p]))
        writes[-1].start()
    for copy in writes:
        copy.wait()


def over_subjects(values):
    count = lax.axis_size("subj")
    return [values] + [
        lax.ppermute(values, "subj", [(i, i ^ d) for i in range(count)]) for d in range(1, count)
    ]


def swap_near(values):
    return lax.ppermute(values, "slab", [(i, i ^ 1) for i in range(lax.axis_size("slab"))])


def swap_far(values):
    count = lax.axis_size("slab")
    return lax.ppermute(
        values, "slab", [(i, i + 1 if i % 2 else i - 1) for i in range(1, count - 1)]
    )


def clear_pads(ref):
    rows = ref.shape[-2] - 2 * PAD
    zeros = jnp.zeros(ref.shape[:-2] + (PAD, ref.shape[-1]), ref.dtype)
    ref[..., :PAD, :] = zeros
    ref[..., PAD + rows :, :] = zeros


def plane_of(ref, *at, step=0):
    rows = ref.shape[-2] - 2 * PAD
    return ref[(*at, slice(PAD + step, PAD + step + rows), slice(None))]


def sides(odd, near, far):
    return jnp.where(odd, near, far), jnp.where(odd, far, near)


def step_weights(coefs, p):
    center = plane_of(coefs, p)
    lane = lax.broadcasted_iota(jnp.int32, center.shape, 1)
    scale = 0.5 * diffusion_dt
    last = center.shape[1] - 1
    right = center + jnp.where(lane == last, 0.0, turned(center, -1))
    left = center + jnp.where(lane == 0, 0.0, turned(center, 1))
    others = [
        center + near
        for near in (
            plane_of(coefs, p, step=1),
            plane_of(coefs, p, step=-1),
            plane_of(coefs, p + 1),
            plane_of(coefs, p - 1),
        )
    ]
    total = right + left
    for face in others:
        total = total + face
    return [
        1.0 - scale * total,
        jnp.where(lane == last, 0.0, scale * right),
        jnp.where(lane == 0, 0.0, scale * left),
    ] + [scale * face for face in others]


def all_weights(coefs):
    return [step_weights(coefs, p) for p in range(1, coefs.shape[0] - 1)]


def stepped(fields, a, low, high, weights):
    planes = fields.shape[1]
    column = [low] + [plane_of(fields, a, p) for p in range(planes)] + [high]
    later = []
    for p in range(planes):
        values = [
            turned(column[p + 1], -1),
            turned(column[p + 1], 1),
            plane_of(fields, a, p, step=1),
            plane_of(fields, a, p, step=-1),
            column[p + 2],
            column[p],
        ]
        total = weights[p][0] * column[p + 1]
        for weight, value in zip(weights[p][1:], values):
            total = total + weight * value
        later.append(total)
    return later


def by_side(odd, pairs):
    copies = [
        (
            [pltpu.make_async_copy(near, low, sems[0]), pltpu.make_async_copy(far, high, sems[1])],
            [pltpu.make_async_copy(near, high, sems[0]), pltpu.make_async_copy(far, low, sems[1])],
        )
        for near, far, low, high, sems in pairs
    ]

    @pl.when(odd)
    def _():
        for when_odd, _ in copies:
            for copy in when_odd:
                copy.start()

    @pl.when(jnp.logical_not(odd))
    def _():
        for _, when_even in copies:
            for copy in when_even:
                copy.start()

    return [copy for when_odd, _ in copies for copy in when_odd]


def force_kernel(
    place_ref,
    velocity_ref,
    images_ref,
    stiffness_ref,
    warped_ref,
    edge_near_ref,
    edge_far_ref,
    warped_near_ref,
    warped_far_ref,
    field_ref,
    coefs_ref,
    near_ref,
    far_ref,
    velocity,
    images,
    warped,
    fields,
    outer,
    sem,
):
    parts, planes, rows = velocity.shape[:3]
    odd = place_ref[0] == 1
    body = slice(PAD, PAD + rows)
    within, every = pl.ds(PAD, rows), pl.ds(0, parts)
    low, mid, high = pl.ds(0, 1), pl.ds(1, planes), pl.ds(planes + 1, 1)
    copies = [
        pltpu.make_async_copy(stiffness_ref, coefs_ref.at[mid, within], sem.at[0]),
        pltpu.make_async_copy(images_ref, images.at[mid], sem.at[1]),
        pltpu.make_async_copy(velocity_ref, velocity, sem.at[2]),
    ]
    for copy in copies:
        copy.start()
    copies += by_side(
        odd,
        [
            (
                edge_near_ref.at[parts],
                edge_far_ref.at[parts],
                coefs_ref.at[low, within],
                coefs_ref.at[high, within],
                (sem.at[3], sem.at[4]),
            ),
            (
                edge_near_ref.at[parts + 1],
                edge_far_ref.at[parts + 1],
                images.at[low],
                images.at[high],
                (sem.at[5], sem.at[6]),
            ),
            (
                edge_near_ref.at[every],
                edge_far_ref.at[every],
                outer.at[:, low],
                outer.at[:, pl.ds(1, 1)],
                (sem.at[7], sem.at[8]),
            ),
        ],
    )
    for ref in (field_ref, fields, coefs_ref, warped):
        clear_pads(ref)
    for p in range(2):
        warped[p, body, :], warped[planes + 2 + p, body, :] = sides(
            odd, warped_near_ref[p], warped_far_ref[p]
        )
    for p in range(planes):
        warped[p + 2, body, :] = warped_ref[p]
    lane = lax.broadcasted_iota(jnp.int32, (rows, LANES), 1)
    right = jnp.where(lane == LANES - 1, 0.0, 0.5 * force_step)
    left = jnp.where(lane == 0, 0.0, 0.5 * force_step)

    def forces(p, image):
        here = plane_of(warped, p + 1)
        mismatch = here - image
        half = (0.5 * force_step) * mismatch
        return [
            mismatch * (right * turned(here, -1) - left * turned(here, 1)),
            half * (plane_of(warped, p + 1, step=1) - plane_of(warped, p + 1, step=-1)),
            half * (plane_of(warped, p + 2) - plane_of(warped, p)),
        ]

    for copy in (copies[0], copies[3], copies[4]):
        copy.wait()
    weights = all_weights(coefs_ref)
    for copy in copies[1:3] + copies[5:]:
        copy.wait()
    for p in range(planes + 2):
        force = forces(p, images[p])
        for a in range(parts):
            if p == 0:
                outer[a, 0] = outer[a, 0] - force[a]
            elif p == planes + 1:
                outer[a, 1] = outer[a, 1] - force[a]
            else:
                fields[a, p - 1, body, :] = velocity[a, p - 1] - force[a]
    for a in range(parts):
        later = stepped(fields, a, outer[a, 0], outer[a, 1], weights)
        for p in range(planes):
            field_ref[a, p, body, :] = later[p]
        near_ref[a, 0], far_ref[a, 0] = sides(odd, later[0], later[-1])


def last_kernel(
    place_ref,
    field_ref,
    coefs_ref,
    near_ref,
    far_ref,
    out_ref,
    done,
    sem,
):
    parts, planes = done.shape[:2]
    odd = place_ref[0] == 1
    weights = all_weights(coefs_ref)
    writes = [pltpu.make_async_copy(done.at[a], out_ref.at[a], sem.at[a]) for a in range(parts)]
    for a in range(parts):
        later = stepped(field_ref, a, *sides(odd, near_ref[a, 0], far_ref[a, 0]), weights)
        for p in range(planes):
            done[a, p] = later[p]
        writes[a].start()
    for copy in writes:
        copy.wait()


def per_device(template, images, velocity, stiffness, send_rows, ref_slot, columns, weights):
    f32, bf16 = jnp.float32, jnp.bfloat16
    shape = jax.ShapeDtypeStruct
    slabs = lax.axis_size("slab")
    subjects = lax.axis_size("subj")
    me = lax.axis_index("subj").astype(jnp.int32).reshape(1)
    slab = lax.axis_index("slab")
    odd = slab % 2 == 1
    place = odd.astype(jnp.int32).reshape(1)
    capacity = send_rows.shape[3]
    rows, width = template.shape
    planes = rows // YR
    parts = velocity.shape[1]
    each = ref_slot.shape[2]
    terms = rows * each
    slots = slabs * capacity
    grid = (planes, YR, width)
    velocity_grid = velocity[0].reshape((parts,) + grid)
    images_grid = images[0].reshape(grid)
    coef_grid = stiffness.reshape(grid)
    dma = pltpu.SemaphoreType.DMA

    sending = call(
        send_kernel,
        shape((slots, width), f32),
        send_rows[0, 0],
        template,
        far=(0, 1),
        scratch=(pltpu.VMEM((slabs, capacity), jnp.int32), pltpu.VMEM((rows, width), f32), dma((2,))),
    )
    received = lax.all_to_all(sending, "slab", split_axis=0, concat_axis=0, tiled=True)

    chunks = 4
    kept_chunks = KEPT
    chunk_shape = (each, len(OFFSETS), rows // chunks, width)
    kept_shape, moved_shape = (kept_chunks,) + chunk_shape, (chunks - kept_chunks,) + chunk_shape
    edge_shape = (parts + 2, 1, YR, width)
    kept, moved, edge_near, edge_far = call(
        prepare_kernel,
        (
            shape(kept_shape, bf16),
            shape(moved_shape, bf16),
            shape(edge_shape, f32),
            shape(edge_shape, f32),
        ),
        place,
        columns.reshape(terms, width),
        weights.reshape(terms, width),
        velocity_grid,
        coef_grid,
        images_grid,
        smem=(0,),
        far=(1, 2, 3, 4, 5),
        out_far=(1, 2, 3),
        scratch=(
            pltpu.VMEM((terms + each, width), jnp.int32),
            pltpu.VMEM((terms, width), bf16),
            pltpu.VMEM((terms // chunks + each, width), f32),
            pltpu.VMEM(moved_shape, bf16),
            pltpu.VMEM((parts + 2,) + grid, f32),
            dma((2 * chunks,)),
            dma((chunks + 2,)),
            dma((3,)),
        ),
    )
    edge_far, edge_near = swap_far(edge_far), swap_near(edge_near)

    warped, sent = call(
        functools.partial(warp_kernel, slabs, subjects),
        (shape((rows, width), f32), shape((slots, width), f32)),
        ref_slot[0].T,
        received,
        kept,
        moved,
        images[0],
        far=(3, 4),
        out_far=(1,),
        scratch=(
            pltpu.VMEM((rows, width), f32),
            pltpu.VMEM(moved_shape, bf16),
            pltpu.VMEM((each, rows, width), f32),
            pltpu.VMEM((each, rows, 2 * width), bf16),
            pltpu.VMEM((slots, width), f32),
            dma,
            dma((chunks - kept_chunks,)),
            dma((subjects,)),
        ),
    )
    returned = lax.all_to_all(sent, ("subj", "slab"), split_axis=0, concat_axis=0, tiled=True)

    own_rows, warped = lax.optimization_barrier((send_rows[0, 0], warped))
    all_rows = over_subjects(own_rows)
    warped_grid = warped.reshape(grid)
    warped_far, warped_near = swap_far(warped_grid), swap_near(warped_grid)

    high = YR + 2 * PAD
    field, coefs, field_near, field_far = call(
        force_kernel,
        (
            shape((parts, planes, high, width), f32),
            shape((planes + 2, high, width), f32),
            shape((parts, 1, YR, width), f32),
            shape((parts, 1, YR, width), f32),
        ),
        place,
        velocity_grid,
        images_grid,
        coef_grid,
        warped_grid,
        edge_near,
        edge_far,
        warped_near,
        warped_far,
        smem=(0,),
        far=(1, 2, 3, 5, 6),
        scratch=(
            pltpu.VMEM((parts,) + grid, f32),
            pltpu.VMEM((planes + 2, YR, width), f32),
            pltpu.VMEM((planes + 4, high, width), f32),
            pltpu.VMEM((parts, planes, high, width), f32),
            pltpu.VMEM((parts, 2, YR, width), f32),
            dma((9,)),
        ),
    )
    field_far, field_near, *all_rows = lax.optimization_barrier((field_far, field_near, *all_rows))
    field_far, field_near = swap_far(field_far), swap_near(field_near)

    part = call(
        functools.partial(collect_kernel, subjects),
        shape((rows // subjects, width), f32),
        me,
        returned,
        *all_rows,
        smem=(0,),
    )
    pieces = over_subjects(part)
    field = call(
        last_kernel,
        shape((parts,) + grid, f32),
        place,
        field,
        coefs,
        field_near,
        field_far,
        smem=(0,),
        out_far=(0,),
        scratch=(pltpu.VMEM((parts,) + grid, f32), dma((parts,))),
    )
    field, *pieces = lax.optimization_barrier((field, *pieces))
    template_out = call(
        functools.partial(update_kernel, subjects),
        shape((rows, width), f32),
        me,
        template,
        *pieces,
        smem=(0,),
        out_far=(0,),
        scratch=(pltpu.VMEM((rows, width), f32), dma((subjects,))),
    )
    velocity_out = field.reshape(parts, rows, width)[None]
    return (template_out, velocity_out)


def solution(mesh):
    return jax.shard_map(
        per_device,
        mesh=mesh,
        in_specs=(
            P("slab", None),
            P("subj", "slab", None),
            P("subj", None, "slab", None),
            P("slab", None),
            P("subj", "slab", None, None),
            P("subj", "slab", None),
            P("subj", "slab", None, None),
            P("subj", "slab", None, None),
        ),
        out_specs=(P("slab", None), P("subj", None, "slab", None)),
        check_vma=False,
    )
```

```python
import functools

import jax
import jax.numpy as jnp
from jax import lax
from jax.experimental import pallas as pl
from jax.experimental.pallas import tpu as pltpu
from jax.sharding import PartitionSpec as P

YR = 256
LANES = 128
PAD = 8
KEPT = 1
OFFSETS = (0, -2, -1, 1, 2)


force_step = 1.0
diffusion_dt = 0.16
template_rate = 2.0

VMEM_LIMIT = 40 * 1024 * 1024


def call(kernel, out_shape, *args, scratch=(), smem=(), far=(), out_far=()):
    many = isinstance(out_shape, tuple)
    shapes = [
        pltpu.HBM(s.shape, s.dtype) if i in out_far else s
        for i, s in enumerate(out_shape if many else (out_shape,))
    ]
    spaces = [pltpu.HBM if i in out_far else pltpu.VMEM for i in range(len(shapes))]
    specs = [pl.BlockSpec(memory_space=space) for space in spaces]
    return pl.pallas_call(
        kernel,
        out_shape=tuple(shapes) if many else shapes[0],
        in_specs=[
            pl.BlockSpec(
                memory_space=pltpu.SMEM if i in smem else pltpu.HBM if i in far else pltpu.VMEM
            )
            for i in range(len(args))
        ],
        out_specs=tuple(specs) if many else specs[0],
        scratch_shapes=scratch,
        compiler_params=pltpu.CompilerParams(vmem_limit_bytes=VMEM_LIMIT),
    )(
        *[
            pltpu.with_memory_space_constraint(arg, pltpu.HBM) if i in far else arg
            for i, arg in enumerate(args)
        ]
    )


def halves(values):
    high = values.astype(jnp.bfloat16)
    low = (values - high.astype(jnp.float32)).astype(jnp.bfloat16)
    return jnp.concatenate([high, low], axis=1)


def joined(pair):
    width = pair.shape[1] // 2
    return pair[:, :width] + pair[:, width:]


def turned(values, shift):
    shift %= values.shape[1]
    return pltpu.roll(values, shift, axis=1) if shift else values


def dot(left, right):
    return jnp.dot(left, right, preferred_element_type=jnp.float32)


def one_hot(matches):
    return jnp.where(matches, 1.0, 0.0).astype(jnp.bfloat16)


def send_kernel(send_ref, template_ref, out_ref, send, template, sem):
    slabs, capacity = send.shape
    rows = template.shape[0]
    copies = [
        pltpu.make_async_copy(send_ref, send, sem.at[0]),
        pltpu.make_async_copy(template_ref, template, sem.at[1]),
    ]
    for copy in copies:
        copy.start()
    copies[0].wait()
    padded = jnp.concatenate([send[...], jnp.zeros((slabs, LANES - capacity), jnp.int32)], axis=1)
    columns = padded.T
    number = lax.broadcasted_iota(jnp.int32, (capacity, rows), 1)
    chosen = [
        one_hot(jnp.broadcast_to(columns[:capacity, k : k + 1], (capacity, rows)) == number)
        for k in range(slabs)
    ]
    copies[1].wait()
    pair = halves(template[...])
    for k in range(slabs):
        out_ref[k * capacity : (k + 1) * capacity, :] = joined(dot(chosen[k], pair))


def prepare_kernel(
    place_ref,
    columns_ref,
    weights_ref,
    velocity_ref,
    stiffness_ref,
    images_ref,
    kept_ref,
    moved_ref,
    near_ref,
    far_ref,
    columns,
    weights,
    plain,
    moved,
    edge,
    in_sem,
    out_sem,
    edge_sem,
):
    held = kept_ref.shape[0]
    each, count, some, width = moved.shape[1:]
    chunks = held + moved.shape[0]
    odd = place_ref[0]
    near_plane, far_plane = pl.ds((edge.shape[1] - 1) * (1 - odd), 1), pl.ds((edge.shape[1] - 1) * odd, 1)
    step = some * each
    parts = velocity_ref.shape[0]
    reads = [
        (
            pltpu.make_async_copy(
                columns_ref.at[pl.ds(i * step, step)], columns.at[pl.ds(i * step, step)], in_sem.at[i]
            ),
            pltpu.make_async_copy(
                weights_ref.at[pl.ds(i * step, step)],
                weights.at[pl.ds(i * step, step)],
                in_sem.at[chunks + i],
            ),
        )
        for i in range(chunks)
    ]
    edges = [
        pltpu.make_async_copy(velocity_ref, edge.at[pl.ds(0, parts)], edge_sem.at[0]),
        pltpu.make_async_copy(stiffness_ref, edge.at[parts], edge_sem.at[1]),
        pltpu.make_async_copy(images_ref, edge.at[parts + 1], edge_sem.at[2]),
    ]
    writes = [
        pltpu.make_async_copy(moved.at[i], moved_ref.at[i], out_sem.at[i])
        for i in range(chunks - held)
    ]
    edge_writes = [
        pltpu.make_async_copy(edge.at[:, near_plane], near_ref, out_sem.at[chunks]),
        pltpu.make_async_copy(edge.at[:, far_plane], far_ref, out_sem.at[chunks + 1]),
    ]
    for copy in reads[0]:
        copy.start()
    for copy in edges:
        copy.start()
    for pair in reads[1:]:
        for copy in pair:
            copy.start()
    cell = lax.broadcasted_iota(jnp.int32, (some, width), 1)
    for i in range(chunks):
        at = i * step
        for copy in reads[i]:
            copy.wait()
        plain[:step, :] = weights[at : at + step, :].astype(jnp.float32)
        for b in range(each):
            offset = columns[pl.ds(at + b, some, stride=each), :] - cell
            here = plain[pl.ds(b, some, stride=each), :]
            for j, o in enumerate(OFFSETS):
                kept = jnp.where(offset == o, here, 0.0)
                target, at_chunk = (moved, i) if i < chunks - held else (kept_ref, i - chunks + held)
                target[at_chunk, b, j] = turned(kept.astype(jnp.bfloat16), o)
        if i < chunks - held:
            writes[i].start()
        if i == 0:
            for copy in edges:
                copy.wait()
            for copy in edge_writes:
                copy.start()
    for copy in writes + edge_writes:
        copy.wait()


def warp_kernel(
    slabs,
    subjects,
    slot_ref,
    received_ref,
    kept_ref,
    moved_ref,
    images_ref,
    warped_ref,
    sent_ref,
    images,
    moved,
    picked,
    placed,
    sent,
    first_sem,
    moved_sem,
    sent_sem,
):
    slots, width = received_ref.shape
    each, count, some = moved.shape[1:4]
    held = kept_ref.shape[0]
    loaded = moved.shape[0]
    chunks = loaded + held
    rows = chunks * some
    block = width // subjects
    group = slots // subjects
    capacity = slots // slabs
    held = capacity // subjects
    first = pltpu.make_async_copy(images_ref, images, first_sem)
    moves = [
        pltpu.make_async_copy(moved_ref.at[i], moved.at[i], moved_sem.at[i]) for i in range(loaded)
    ]
    for copy in [first] + moves:
        copy.start()
    slot = slot_ref[...]
    slot_wide = jnp.concatenate([slot, jnp.zeros((LANES - each, rows), jnp.int32)], axis=0).T
    inner = slot % capacity
    packed = (inner // held) * group + (slot // capacity) * held + inner % held
    lane = lax.broadcasted_iota(jnp.int32, (rows, LANES), 1)
    number = lax.broadcasted_iota(jnp.int32, (slots, rows), 0)
    pair = halves(received_ref[...])
    for b in range(each):
        wide = jnp.broadcast_to(slot_wide[:, b : b + 1], (rows, LANES))
        pick = jnp.concatenate(
            [one_hot(wide == lane + t * LANES) for t in range(slots // LANES)], axis=1
        )
        picked[b] = joined(dot(pick, pair))
    for copy in [first] + moves:
        copy.wait()
    for i in range(chunks):
        here, h = (moved, i) if i < loaded else (kept_ref, i - loaded)
        at = slice(i * some, (i + 1) * some)
        sums = [jnp.zeros((some, width), jnp.float32) for _ in OFFSETS]
        for b in range(each):
            values = picked[b, at, :]
            for j in range(count):
                sums[j] = sums[j] + here[h, b, j].astype(jnp.float32) * values
        warped = sums[0]
        for j, o in enumerate(OFFSETS[1:], 1):
            warped = warped + turned(sums[j], -o)
        warped_ref[at, :] = warped
        mismatch = warped - images[at, :]
        ahead = [turned(mismatch, o) for o in OFFSETS]
        for b in range(each):
            total = here[h, b, 0].astype(jnp.float32) * ahead[0]
            for j in range(1, count):
                total = total + here[h, b, j].astype(jnp.float32) * ahead[j]
            placed[b, at, :] = halves(total)
    total = jnp.zeros((slots, 2 * width), jnp.float32)
    for b in range(each):
        drop = one_hot(jnp.broadcast_to(packed[b : b + 1], (slots, rows)) == number)
        total = total + dot(drop, placed[b])
    total = joined(total)
    place = lax.broadcasted_iota(jnp.int32, (group, width), 1) // block
    writes = []
    groups = [total[q * group : (q + 1) * group, :] for q in range(subjects)]
    for p in range(subjects):
        out = jnp.zeros((group, width), jnp.float32)
        for q in range(subjects):
            out = jnp.where(place == q, turned(groups[q], (q - p) * block), out)
        sent[p * group : (p + 1) * group, :] = out
        rows_at = pl.ds(p * group, group)
        writes.append(pltpu.make_async_copy(sent.at[rows_at], sent_ref.at[rows_at], sent_sem.at[p]))
        writes[-1].start()
    for copy in writes:
        copy.wait()


def collect_kernel(subjects, me_ref, returned_ref, *refs):
    row_refs, out_ref = refs[:-1], refs[-1]
    slots, width = returned_ref.shape
    slabs, capacity = row_refs[0].shape
    rows = out_ref.shape[0] * subjects
    block = width // subjects
    group = slots // subjects
    held = capacity // subjects
    me = me_ref[0]
    pair = halves(
        jnp.concatenate(
            [
                returned_ref[pl.ds(pl.multiple_of((me ^ d) * group, group), group), :]
                for d in range(subjects)
            ]
        )
    )
    lane = lax.broadcasted_iota(jnp.int32, (slabs, LANES), 1)
    slab = lax.broadcasted_iota(jnp.int32, (slabs, LANES), 0)
    fill = jnp.zeros((slabs, LANES - capacity), jnp.int32)
    wanted = []
    for q in range(subjects):
        chunks = [jnp.zeros((1, LANES), jnp.int32) for _ in range(slots // LANES)]
        for d in range(subjects):
            spread = jnp.concatenate([row_refs[d][...], fill], axis=1)
            spread = turned(spread, d * group - q * held)
            spread = pltpu.roll(spread, 0, axis=1, stride=held, stride_axis=0)
            first = (d * group) % LANES + slab * held
            kept = jnp.where((lane >= first) & (lane < first + held), spread, 0)
            chunks[d * group // LANES] += jnp.sum(kept, axis=0, keepdims=True)
        wanted.append(jnp.concatenate(chunks, axis=1))
    number = lax.broadcasted_iota(jnp.int32, (rows, slots), 0)
    place = lax.broadcasted_iota(jnp.int32, (rows, width), 1) // block
    kept = jnp.zeros((rows, width), jnp.float32)
    for q in range(subjects):
        match = jnp.broadcast_to(wanted[q], (rows, slots)) == number
        kept = jnp.where(place == q, joined(dot(one_hot(match), pair)), kept)
    turn = block
    while turn < width:
        kept = kept + turned(kept, turn)
        turn *= 2
    part = rows // subjects
    out = jnp.zeros((part, width), jnp.float32)
    for p in range(subjects):
        out = jnp.where(place[:part] == p, kept[p * part : (p + 1) * part], out)
    out_ref[...] = out


def update_kernel(subjects, me_ref, template_ref, *refs):
    parts, (out_ref, done, sem) = refs[:-3], refs[-3:]
    rows, width = template_ref.shape
    block = width // subjects
    part = rows // subjects
    me = me_ref[0]
    place = lax.broadcasted_iota(jnp.int32, (part, width), 1) // block
    writes = []
    for p in range(subjects):
        total = jnp.zeros((part, width), jnp.float32)
        for d in range(subjects):
            source = me ^ d
            turn = lax.rem((source - p) * block + width, width)
            total = jnp.where(place == source, pltpu.roll(parts[d][...], turn, axis=1), total)
        at = slice(p * part, (p + 1) * part)
        done[at, :] = template_ref[at, :] - template_rate * total / subjects
        rows_at = pl.ds(p * part, part)
        writes.append(pltpu.make_async_copy(done.at[rows_at], out_ref.at[rows_at], sem.at[p]))
        writes[-1].start()
    for copy in writes:
        copy.wait()


def over_subjects(values):
    count = lax.axis_size("subj")
    return [values] + [
        lax.ppermute(values, "subj", [(i, i ^ d) for i in range(count)]) for d in range(1, count)
    ]


def swap_near(values):
    return lax.ppermute(values, "slab", [(i, i ^ 1) for i in range(lax.axis_size("slab"))])


def swap_far(values):
    count = lax.axis_size("slab")
    return lax.ppermute(
        values, "slab", [(i, i + 1 if i % 2 else i - 1) for i in range(1, count - 1)]
    )


def clear_pads(ref):
    rows = ref.shape[-2] - 2 * PAD
    zeros = jnp.zeros(ref.shape[:-2] + (PAD, ref.shape[-1]), ref.dtype)
    ref[..., :PAD, :] = zeros
    ref[..., PAD + rows :, :] = zeros


def plane_of(ref, *at, step=0):
    rows = ref.shape[-2] - 2 * PAD
    return ref[(*at, slice(PAD + step, PAD + step + rows), slice(None))]


def sides(odd, near, far):
    return jnp.where(odd, near, far), jnp.where(odd, far, near)


def step_weights(coefs, p):
    center = plane_of(coefs, p)
    lane = lax.broadcasted_iota(jnp.int32, center.shape, 1)
    scale = 0.5 * diffusion_dt
    last = center.shape[1] - 1
    right = center + jnp.where(lane == last, 0.0, turned(center, -1))
    left = center + jnp.where(lane == 0, 0.0, turned(center, 1))
    others = [
        center + near
        for near in (
            plane_of(coefs, p, step=1),
            plane_of(coefs, p, step=-1),
            plane_of(coefs, p + 1),
            plane_of(coefs, p - 1),
        )
    ]
    total = right + left
    for face in others:
        total = total + face
    return [
        1.0 - scale * total,
        jnp.where(lane == last, 0.0, scale * right),
        jnp.where(lane == 0, 0.0, scale * left),
    ] + [scale * face for face in others]


def all_weights(coefs):
    return [step_weights(coefs, p) for p in range(1, coefs.shape[0] - 1)]


def stepped(fields, a, low, high, weights):
    planes = fields.shape[1]
    column = [low] + [plane_of(fields, a, p) for p in range(planes)] + [high]
    later = []
    for p in range(planes):
        values = [
            turned(column[p + 1], -1),
            turned(column[p + 1], 1),
            plane_of(fields, a, p, step=1),
            plane_of(fields, a, p, step=-1),
            column[p + 2],
            column[p],
        ]
        total = weights[p][0] * column[p + 1]
        for weight, value in zip(weights[p][1:], values):
            total = total + weight * value
        later.append(total)
    return later


def by_side(odd, pairs):
    copies = [
        (
            [pltpu.make_async_copy(near, low, sems[0]), pltpu.make_async_copy(far, high, sems[1])],
            [pltpu.make_async_copy(near, high, sems[0]), pltpu.make_async_copy(far, low, sems[1])],
        )
        for near, far, low, high, sems in pairs
    ]

    @pl.when(odd)
    def _():
        for when_odd, _ in copies:
            for copy in when_odd:
                copy.start()

    @pl.when(jnp.logical_not(odd))
    def _():
        for _, when_even in copies:
            for copy in when_even:
                copy.start()

    return [copy for when_odd, _ in copies for copy in when_odd]


def force_kernel(
    place_ref,
    velocity_ref,
    images_ref,
    stiffness_ref,
    warped_ref,
    edge_near_ref,
    edge_far_ref,
    warped_near_ref,
    warped_far_ref,
    field_ref,
    coefs_ref,
    near_ref,
    far_ref,
    velocity,
    images,
    warped,
    fields,
    outer,
    sem,
):
    parts, planes, rows = velocity.shape[:3]
    odd = place_ref[0] == 1
    body = slice(PAD, PAD + rows)
    within, every = pl.ds(PAD, rows), pl.ds(0, parts)
    low, mid, high = pl.ds(0, 1), pl.ds(1, planes), pl.ds(planes + 1, 1)
    copies = [
        pltpu.make_async_copy(stiffness_ref, coefs_ref.at[mid, within], sem.at[0]),
        pltpu.make_async_copy(images_ref, images.at[mid], sem.at[1]),
        pltpu.make_async_copy(velocity_ref, velocity, sem.at[2]),
    ]
    for copy in copies:
        copy.start()
    copies += by_side(
        odd,
        [
            (
                edge_near_ref.at[parts],
                edge_far_ref.at[parts],
                coefs_ref.at[low, within],
                coefs_ref.at[high, within],
                (sem.at[3], sem.at[4]),
            ),
            (
                edge_near_ref.at[parts + 1],
                edge_far_ref.at[parts + 1],
                images.at[low],
                images.at[high],
                (sem.at[5], sem.at[6]),
            ),
            (
                edge_near_ref.at[every],
                edge_far_ref.at[every],
                outer.at[:, low],
                outer.at[:, pl.ds(1, 1)],
                (sem.at[7], sem.at[8]),
            ),
        ],
    )
    for ref in (field_ref, fields, coefs_ref, warped):
        clear_pads(ref)
    for p in range(2):
        warped[p, body, :], warped[planes + 2 + p, body, :] = sides(
            odd, warped_near_ref[p], warped_far_ref[p]
        )
    for p in range(planes):
        warped[p + 2, body, :] = warped_ref[p]
    lane = lax.broadcasted_iota(jnp.int32, (rows, LANES), 1)
    right = jnp.where(lane == LANES - 1, 0.0, 0.5 * force_step)
    left = jnp.where(lane == 0, 0.0, 0.5 * force_step)

    def forces(p, image):
        here = plane_of(warped, p + 1)
        mismatch = here - image
        half = (0.5 * force_step) * mismatch
        return [
            mismatch * (right * turned(here, -1) - left * turned(here, 1)),
            half * (plane_of(warped, p + 1, step=1) - plane_of(warped, p + 1, step=-1)),
            half * (plane_of(warped, p + 2) - plane_of(warped, p)),
        ]

    for copy in (copies[0], copies[3], copies[4]):
        copy.wait()
    weights = all_weights(coefs_ref)
    for copy in (copies[1], copies[5], copies[6]):
        copy.wait()
    every_force = [forces(p, images[p]) for p in range(planes + 2)]
    for copy in (copies[2], copies[7], copies[8]):
        copy.wait()
    for p, force in enumerate(every_force):
        for a in range(parts):
            if p == 0:
                outer[a, 0] = outer[a, 0] - force[a]
            elif p == planes + 1:
                outer[a, 1] = outer[a, 1] - force[a]
            else:
                fields[a, p - 1, body, :] = velocity[a, p - 1] - force[a]
    for a in range(parts):
        later = stepped(fields, a, outer[a, 0], outer[a, 1], weights)
        for p in range(planes):
            field_ref[a, p, body, :] = later[p]
        near_ref[a, 0], far_ref[a, 0] = sides(odd, later[0], later[-1])


def last_kernel(
    place_ref,
    field_ref,
    coefs_ref,
    near_ref,
    far_ref,
    out_ref,
    done,
    sem,
):
    parts, planes = done.shape[:2]
    odd = place_ref[0] == 1
    weights = all_weights(coefs_ref)
    writes = [pltpu.make_async_copy(done.at[a], out_ref.at[a], sem.at[a]) for a in range(parts)]
    for a in range(parts):
        later = stepped(field_ref, a, *sides(odd, near_ref[a, 0], far_ref[a, 0]), weights)
        for p in range(planes):
            done[a, p] = later[p]
        writes[a].start()
    for copy in writes:
        copy.wait()


def per_device(template, images, velocity, stiffness, send_rows, ref_slot, columns, weights):
    f32, bf16 = jnp.float32, jnp.bfloat16
    shape = jax.ShapeDtypeStruct
    slabs = lax.axis_size("slab")
    subjects = lax.axis_size("subj")
    me = lax.axis_index("subj").astype(jnp.int32).reshape(1)
    slab = lax.axis_index("slab")
    odd = slab % 2 == 1
    place = odd.astype(jnp.int32).reshape(1)
    capacity = send_rows.shape[3]
    rows, width = template.shape
    planes = rows // YR
    parts = velocity.shape[1]
    each = ref_slot.shape[2]
    terms = rows * each
    slots = slabs * capacity
    grid = (planes, YR, width)
    velocity_grid = velocity[0].reshape((parts,) + grid)
    images_grid = images[0].reshape(grid)
    coef_grid = stiffness.reshape(grid)
    dma = pltpu.SemaphoreType.DMA

    sending = call(
        send_kernel,
        shape((slots, width), f32),
        send_rows[0, 0],
        template,
        far=(0, 1),
        scratch=(pltpu.VMEM((slabs, capacity), jnp.int32), pltpu.VMEM((rows, width), f32), dma((2,))),
    )
    received = lax.all_to_all(sending, "slab", split_axis=0, concat_axis=0, tiled=True)

    chunks = 4
    kept_chunks = KEPT
    chunk_shape = (each, len(OFFSETS), rows // chunks, width)
    kept_shape, moved_shape = (kept_chunks,) + chunk_shape, (chunks - kept_chunks,) + chunk_shape
    edge_shape = (parts + 2, 1, YR, width)
    kept, moved, edge_near, edge_far = call(
        prepare_kernel,
        (
            shape(kept_shape, bf16),
            shape(moved_shape, bf16),
            shape(edge_shape, f32),
            shape(edge_shape, f32),
        ),
        place,
        columns.reshape(terms, width),
        weights.reshape(terms, width),
        velocity_grid,
        coef_grid,
        images_grid,
        smem=(0,),
        far=(1, 2, 3, 4, 5),
        out_far=(1, 2, 3),
        scratch=(
            pltpu.VMEM((terms + each, width), jnp.int32),
            pltpu.VMEM((terms, width), bf16),
            pltpu.VMEM((terms // chunks + each, width), f32),
            pltpu.VMEM(moved_shape, bf16),
            pltpu.VMEM((parts + 2,) + grid, f32),
            dma((2 * chunks,)),
            dma((chunks + 2,)),
            dma((3,)),
        ),
    )
    edge_far, edge_near = swap_far(edge_far), swap_near(edge_near)

    warped, sent = call(
        functools.partial(warp_kernel, slabs, subjects),
        (shape((rows, width), f32), shape((slots, width), f32)),
        ref_slot[0].T,
        received,
        kept,
        moved,
        images[0],
        far=(3, 4),
        out_far=(1,),
        scratch=(
            pltpu.VMEM((rows, width), f32),
            pltpu.VMEM(moved_shape, bf16),
            pltpu.VMEM((each, rows, width), f32),
            pltpu.VMEM((each, rows, 2 * width), bf16),
            pltpu.VMEM((slots, width), f32),
            dma,
            dma((chunks - kept_chunks,)),
            dma((subjects,)),
        ),
    )
    returned = lax.all_to_all(sent, ("subj", "slab"), split_axis=0, concat_axis=0, tiled=True)

    own_rows, warped = lax.optimization_barrier((send_rows[0, 0], warped))
    all_rows = over_subjects(own_rows)
    warped_grid = warped.reshape(grid)
    warped_far, warped_near = swap_far(warped_grid), swap_near(warped_grid)

    high = YR + 2 * PAD
    field, coefs, field_near, field_far = call(
        force_kernel,
        (
            shape((parts, planes, high, width), f32),
            shape((planes + 2, high, width), f32),
            shape((parts, 1, YR, width), f32),
            shape((parts, 1, YR, width), f32),
        ),
        place,
        velocity_grid,
        images_grid,
        coef_grid,
        warped_grid,
        edge_near,
        edge_far,
        warped_near,
        warped_far,
        smem=(0,),
        far=(1, 2, 3, 5, 6),
        scratch=(
            pltpu.VMEM((parts,) + grid, f32),
            pltpu.VMEM((planes + 2, YR, width), f32),
            pltpu.VMEM((planes + 4, high, width), f32),
            pltpu.VMEM((parts, planes, high, width), f32),
            pltpu.VMEM((parts, 2, YR, width), f32),
            dma((9,)),
        ),
    )
    field_far, field_near, *all_rows = lax.optimization_barrier((field_far, field_near, *all_rows))
    field_far, field_near = swap_far(field_far), swap_near(field_near)

    part = call(
        functools.partial(collect_kernel, subjects),
        shape((rows // subjects, width), f32),
        me,
        returned,
        *all_rows,
        smem=(0,),
    )
    pieces = over_subjects(part)
    field = call(
        last_kernel,
        shape((parts,) + grid, f32),
        place,
        field,
        coefs,
        field_near,
        field_far,
        smem=(0,),
        out_far=(0,),
        scratch=(pltpu.VMEM((parts,) + grid, f32), dma((parts,))),
    )
    field, *pieces = lax.optimization_barrier((field, *pieces))
    template_out = call(
        functools.partial(update_kernel, subjects),
        shape((rows, width), f32),
        me,
        template,
        *pieces,
        smem=(0,),
        out_far=(0,),
        scratch=(pltpu.VMEM((rows, width), f32), dma((subjects,))),
    )
    velocity_out = field.reshape(parts, rows, width)[None]
    return (template_out, velocity_out)


def solution(mesh):
    return jax.shard_map(
        per_device,
        mesh=mesh,
        in_specs=(
            P("slab", None),
            P("subj", "slab", None),
            P("subj", None, "slab", None),
            P("slab", None),
            P("subj", "slab", None, None),
            P("subj", "slab", None),
            P("subj", "slab", None, None),
            P("subj", "slab", None, None),
        ),
        out_specs=(P("slab", None), P("subj", None, "slab", None)),
        check_vma=False,
    )
```
